128 devices in a mesh: section: 2 (over y_hi), wide: 16 (over x, y_lo, core), tp: 4 (over z).
Axes of the slice: x: 4, y: 4 (y_hi: 2, y_lo: 2; y = y_hi * 2 + y_lo), z: 4, core: 2. Of those that a mesh axis runs over, the one named last changes fastest.
Arguments:
- block_input: bfloat16 [2, 2048, 2048], P(None, ('wide', 'tp')), may hold values from -6 to 6
- out_grad: bfloat16 [2, 2048, 2048], P(None, ('wide', 'tp')), may hold values from -6 to 6
- seg_ids: int32 [2, 2048], replicated, may hold values from 0 to 9, as said below
- attn_gain: bfloat16 [2, 2048], P('section', 'wide'), may hold values from 0.5 to 1.5
- w_query: bfloat16 [2, 2048, 2048], P('section', 'wide', 'tp'), may hold values from -0.125 to 0.125
- w_key: bfloat16 [2, 2048, 256], P('section', 'wide', 'tp'), may hold values from -0.125 to 0.125
- w_value: bfloat16 [2, 2048, 256], P('section', 'wide', 'tp'), may hold values from -0.125 to 0.125
- w_out: bfloat16 [2, 2048, 2048], P('section', 'tp', 'wide'), may hold values from -2 to 2
- ffn_gain: bfloat16 [2, 2048], P('section', 'wide'), may hold values from 0.5 to 1.5
- w_gate: bfloat16 [2, 2048, 5632], P('section', 'wide', 'tp'), may hold values from -0.125 to 0.125
- w_up: bfloat16 [2, 2048, 5632], P('section', 'wide', 'tp'), may hold values from -0.125 to 0.125
- w_down: bfloat16 [2, 5632, 2048], P('section', 'tp', 'wide'), may hold values from -0.078125 to 0.078125
Outputs:
- block_output: bfloat16 [2, 2, 2048, 2048], P('section', None, ('wide', 'tp'))
- input_grad: float32 [2, 2, 2048, 2048], P('section', None, ('wide', 'tp'))
- grad_attn_gain: float32 [2, 2048], P('section', ('wide', 'tp'))
- grad_query: float32 [2, 2048, 2048], P('section', 'wide', 'tp')
- grad_key: float32 [2, 2048, 256], P('section', 'wide', 'tp')
- grad_value: float32 [2, 2048, 256], P('section', 'wide', 'tp')
- grad_out: float32 [2, 2048, 2048], P('section', 'tp', 'wide')
- grad_ffn_gain: float32 [2, 2048], P('section', ('wide', 'tp'))
- grad_gate: float32 [2, 2048, 5632], P('section', 'wide', 'tp')
- grad_up: float32 [2, 2048, 5632], P('section', 'wide', 'tp')
- grad_down: float32 [2, 5632, 2048], P('section', 'tp', 'wide')
The draws below stay inside these ranges and needn't reach their ends.
Inputs may be any that keep to these rules, and one draw needn't show every extreme that they name: `seg_ids`: in every micro-batch the document numbers start at 0, never fall along the sequence and rise by one at each new document; every document holds 102 to 2048 positions; in one micro-batch the whole sequence is a single document, and in another one there are ten documents.
All inputs are finite; a program needn't handle non-finite values.
Results may differ from the reference program's by a relative error of at most 0.035.
Values may be sent and summed in bfloat16 or wider, within the bound.
No kernel may reach another device: no remote copies, remote signals or barrier semaphores. Data moves between devices by JAX's collectives and lax.ppermute only.
A program may use at most 256 MiB of HBM per device.

```python
import math
import jax
import jax.numpy as jnp
from jax import lax

D = 2048
HEADS = 32
KV = 4
HD = 64
FF = 5632
SEQ = 2048
MICRO = 2
SECTIONS = 2


def draw_seg_ids(key, part):
    key = jax.random.fold_in(key, 11)
    length_key, whole_key = jax.random.split(key)
    tenth_key = jax.random.fold_in(key, 5)
    bin_key = jax.random.fold_in(key, 7)
    shortest = max(SEQ // 10, 1)
    short_doc = max(SEQ // 20, 1)
    places = jnp.arange(SEQ, dtype=jnp.int32)
    lengths = jax.random.randint(length_key, (MICRO, 10), shortest, 10 * shortest + 1)
    ends = jnp.cumsum(lengths, axis=1)
    ends = jnp.where(ends <= SEQ - shortest, ends, SEQ + 1)
    seg_rows = jnp.sum((places[None, :, None] >= ends[:, None, :]).astype(jnp.int32), axis=2)
    spare_count = SEQ - 10 * short_doc
    bins = jax.random.randint(bin_key, (spare_count,), 0, 10)
    extra = jnp.sum((bins[:, None] == jnp.arange(10, dtype=jnp.int32)[None, :]).astype(jnp.int32), axis=0)
    ten_ends = jnp.cumsum(short_doc + extra)[:9]
    ten_row = jnp.sum((places[:, None] >= ten_ends[None, :]).astype(jnp.int32), axis=1)
    whole_row = jax.random.randint(whole_key, (), 0, MICRO)
    tenth_row = (whole_row + 1 + jax.random.randint(tenth_key, (), 0, MICRO - 1)) % MICRO
    micro_index = jnp.arange(MICRO, dtype=jnp.int32)
    single = (micro_index == whole_row)[:, None]
    many = (micro_index == tenth_row)[:, None]
    seg_rows = jnp.where(many, ten_row[None, :], seg_rows)
    return jnp.where(single, 0, seg_rows).astype(jnp.int32)


def block_scale(own_key, shape, pieces, low, largest):
    loudness, own = 1.0, jax.random.fold_in(own_key, 6)
    for axis_at, blocks in pieces:
        steps = jnp.exp(jax.random.uniform(jax.random.fold_in(own, axis_at), (blocks,), jnp.float32, low / len(pieces), largest / len(pieces)))
        loudness = loudness * jnp.repeat(steps, shape[axis_at] // blocks).reshape([-1 if axis == axis_at else 1 for axis in range(len(shape))])
    return loudness


def scatter_about(key, dims, spread, bound, pieces=(), kind=jnp.bfloat16):
    factor_of = block_scale(key, dims, pieces, -0.22, 0.18) if pieces else 1.0
    drawn = jax.random.normal(key, dims, jnp.float32) * spread * factor_of
    return jnp.minimum(jnp.maximum(drawn, -bound), bound).astype(kind)


def setup_inputs(seed: int = 0) -> dict:
    key_list = jax.random.split(jax.random.key(seed), 13)
    return {
        "block_input": scatter_about(key_list[0], (MICRO, SEQ, D), 1.0, 6.0, ((1, 64),)),
        "out_grad": scatter_about(key_list[1], (MICRO, SEQ, D), 1.0, 6.0, ((1, 64),)),
        "seg_ids": draw_seg_ids(jax.random.fold_in(key_list[12], 71), 0),
        "attn_gain": jnp.clip(1.0 + 0.1 * jax.random.normal(key_list[3], (SECTIONS, D), jnp.float32), 0.5, 1.5).astype(jnp.bfloat16),
        "w_query": scatter_about(key_list[4], (SECTIONS, D, HEADS * HD), D ** -0.5, 0.125, ((0, 2), (1, 16), (2, 4))),
        "w_key": scatter_about(key_list[5], (SECTIONS, D, KV * HD), D ** -0.5, 0.125, ((0, 2), (1, 16), (2, 4))),
        "w_value": scatter_about(key_list[6], (SECTIONS, D, KV * HD), D ** -0.5, 0.125, ((0, 2), (1, 16), (2, 4))),
        "w_out": scatter_about(key_list[7], (SECTIONS, HEADS * HD, D), (max(HEADS * HD // 256, 1)) ** -0.5, 2.0, ((0, 2), (1, 4), (2, 16))),
        "ffn_gain": jnp.clip(1.0 + 0.1 * jax.random.normal(key_list[8], (SECTIONS, D), jnp.float32), 0.5, 1.5).astype(jnp.bfloat16),
        "w_gate": scatter_about(key_list[9], (SECTIONS, D, FF), D ** -0.5, 0.125, ((0, 2), (1, 16), (2, 4))),
        "w_up": scatter_about(key_list[10], (SECTIONS, D, FF), D ** -0.5, 0.125, ((0, 2), (1, 16), (2, 4))),
        "w_down": scatter_about(key_list[11], (SECTIONS, FF, D), FF ** -0.5, 0.078125, ((0, 2), (1, 4), (2, 16))),
    }


@jax.custom_vjp
def low(v):
    return lax.optimization_barrier(v.astype(jnp.bfloat16)).astype(jnp.float32)

@jax.custom_vjp
def low_back(v):
    return v

def low_keep(v):
    return (low(v), None)

def low_pass(kept, grad):
    return (grad,)

def back_keep(v):
    return (v, None)

def back_low(kept, grad):
    return (low(grad),)
low.defvjp(low_keep, low_pass)
low_back.defvjp(back_keep, back_low)
epsilon = 1e-05
masked_score = -1e+30
highest = lax.Precision.HIGHEST

def rotate(values):
    half_width = values.shape[-1] // 2
    return jnp.concatenate([-values[..., half_width:], values[..., :half_width]], axis=-1)

def rotary(values, cosine, sine_table):
    return values * cosine + rotate(values) * sine_table

def normalize(residual, gain_vector):
    return residual * lax.rsqrt(lax.optimization_barrier(jnp.mean(residual * residual, axis=-1, keepdims=True)) + epsilon) * gain_vector

def swish_gate(gate_values, up_values):
    return gate_values / (1.0 + jnp.exp(-gate_values)) * up_values

def full_dot(former, latter):
    return jnp.dot(former, latter, precision=highest)

def attend_block(query_block, query_index, query_segment, key_rows, value_rows, seg_row):
    key_index = jnp.arange(SEQ, dtype=jnp.int32)
    scores = jnp.einsum('qgjd,kgd->gjqk', query_block, key_rows, precision=highest) * (1.0 / math.sqrt(HD))
    scores = low_back(scores)
    allowed = (query_index[:, None] >= key_index[None, :]) & (query_segment[:, None] == seg_row[None, :])
    scores = jnp.where(allowed, scores, masked_score)
    row_max = lax.optimization_barrier(jnp.max(scores, axis=-1, keepdims=True))
    raised = jnp.exp(scores - row_max)
    softmax_probs = low(raised / lax.optimization_barrier(jnp.sum(raised, axis=-1, keepdims=True)))
    return jnp.einsum('gjqk,kgd->qgjd', softmax_probs, value_rows, precision=highest)

def layer(residual, weights, seg_row, cosine, sine_table):
    gain_attn, query_weight, key_weight, value_weight, out_weight, gain_ffn, gate_weight, up_weight, down_weight = weights
    group_size = HEADS // KV
    normed = low(normalize(residual, gain_attn))
    query_pre = low_back(full_dot(normed, query_weight)).reshape(SEQ, HEADS, HD)
    key_pre = low_back(full_dot(normed, key_weight)).reshape(SEQ, KV, HD)
    value_pre = full_dot(normed, value_weight).reshape(SEQ, KV, HD)
    query_rot = low(rotary(query_pre, cosine, sine_table))
    key_rot = low(rotary(key_pre, cosine, sine_table))
    value_rows = low(low_back(value_pre))
    block_rows = min(512, SEQ)
    block_count = SEQ // block_rows
    query_blocks = query_rot.reshape(block_count, block_rows, KV, group_size, HD)
    index_blocks = jnp.arange(SEQ, dtype=jnp.int32).reshape(block_count, block_rows)
    segment_blocks = seg_row.reshape(block_count, block_rows)
    checked = jax.checkpoint(attend_block)
    context = lax.map(lambda block_item: checked(block_item[0], block_item[1], block_item[2], key_rot, value_rows, seg_row), (query_blocks, index_blocks, segment_blocks))
    context = low(low_back(context.reshape(SEQ, HEADS * HD)))
    middle = residual + low_back(full_dot(context, out_weight))
    normed_ffn = low(normalize(middle, gain_ffn))
    gate_values = low_back(full_dot(normed_ffn, gate_weight))
    up_values = low_back(full_dot(normed_ffn, up_weight))
    hidden = low(swish_gate(gate_values, up_values))
    return middle + low_back(full_dot(hidden, down_weight))

def reference(block_input, out_grad, seg_ids, attn_gain, w_query, w_key, w_value, w_out, ffn_gain, w_gate, w_up, w_down):
    params = tuple((weight.astype(jnp.float32) for weight in (attn_gain, w_query, w_key, w_value, w_out, ffn_gain, w_gate, w_up, w_down)))
    positions = jnp.arange(SEQ, dtype=jnp.float32)
    frequency = 10000.0 ** (-jnp.arange(0, HD, 2, dtype=jnp.float32) / HD)
    angles = positions[:, None] * frequency[None, :]
    angles = jnp.concatenate([angles, angles], axis=1)[:, None, :]
    cosine = jnp.cos(angles)
    sine_table = jnp.sin(angles)

    def both_layers(residual, zero_add, stacked, seg_row):
        first_weights = tuple((weight[0] for weight in stacked))
        second_weights = tuple((weight[1] for weight in stacked))
        early_out = layer(residual, first_weights, seg_row, cosine, sine_table)
        later_in = low_back(low(early_out)) + zero_add
        return (early_out, layer(later_in, second_weights, seg_row, cosine, sine_table))

    def micro_step(grad_sums, batch_item):
        residual, cotangent, seg_row = batch_item
        zero_add = jnp.zeros_like(residual)
        outputs, pull_back = jax.vjp(lambda stream_arg, zero_arg, param_arg: both_layers(stream_arg, zero_arg, param_arg, seg_row), residual, zero_add, params)
        grad_residual, grad_zero, grad_params = pull_back((jnp.zeros_like(outputs[0]), cotangent))
        grad_sums = tuple((running + addend for running, addend in zip(grad_sums, grad_params)))
        return (grad_sums, (outputs[0].astype(jnp.bfloat16), outputs[1].astype(jnp.bfloat16), grad_residual, grad_zero))
    start_sums = tuple((jnp.zeros_like(weight) for weight in params))
    batch_items = (block_input.astype(jnp.float32), out_grad.astype(jnp.float32), seg_ids)
    grad_sums, (early_outs, later_outs, grad_early, grad_later) = lax.scan(micro_step, start_sums, batch_items)
    block_output = jnp.stack([early_outs, later_outs])
    input_grad = jnp.stack([grad_early, grad_later])
    return (block_output, input_grad, grad_sums[0], grad_sums[1], grad_sums[2], grad_sums[3], grad_sums[4], grad_sums[5], grad_sums[6], grad_sums[7], grad_sums[8])
```

```python
import functools

import jax
import jax.numpy as jnp
from jax import lax
from jax.experimental import pallas as pl
from jax.experimental.pallas import tpu as pltpu
from jax.sharding import Mesh, PartitionSpec as P

HD = 64
EPS = 1e-05
MASKED = -1e30
KEYS_STEP = 512
AXES = ("section", "x", "ylo", "core", "tp")
BF16 = jnp.bfloat16
F32 = jnp.float32


def nn(a, b):
    return jnp.dot(a, b, preferred_element_type=F32)


def nt(a, b):
    return lax.dot_general(a, b, (((1,), (1,)), ((), ())), preferred_element_type=F32)


def tn(a, b):
    return lax.dot_general(a, b, (((0,), (0,)), ((), ())), preferred_element_type=F32)


def from_z(rows, by):
    return lax.ppermute(rows, "tp", [((i + by) % 4, i) for i in range(4)])


def swap_core(v):
    return lax.ppermute(v, "core", [(0, 1), (1, 0)])


def swap_ylo(v):
    return lax.ppermute(v, "ylo", [(0, 1), (1, 0)])


def swap_section(v):
    return lax.ppermute(v, "section", [(0, 1), (1, 0)])


def swap_across(v):
    return lax.ppermute(v, ("section", "ylo"), [(0, 3), (3, 0), (1, 2), (2, 1)])


def pick(first, a, b):
    return jnp.where(first, a, b)


def in_order(first, own, other, dim=0):
    return jnp.where(
        first,
        jnp.concatenate([own, other], axis=dim),
        jnp.concatenate([other, own], axis=dim),
    )


def gather_rows(rows):
    near = jnp.concatenate([rows] + [from_z(rows, k) for k in (1, 2, 3)], axis=0)
    return jnp.concatenate([near, swap_core(near)], axis=0)


def reduce_rows(partial):
    half = partial.shape[0] // 2
    step = half // 4
    mine = partial[:half] + swap_core(partial[half:].astype(BF16)).astype(F32)
    low = mine.astype(BF16)
    total = mine[:step]
    for k in (1, 2, 3):
        total = total + from_z(low[k * step : (k + 1) * step], -k).astype(F32)
    return total


def gather_kv(pair):
    copies = jnp.broadcast_to(pair[None], (8, *pair.shape))
    whole = lax.all_to_all(copies, ("x", "ylo"), 0, 0, tiled=True)
    return whole.reshape(-1, pair.shape[1])


def reduce_kv(partial):
    blocks = partial.reshape(8, -1, partial.shape[1])
    arrived = lax.all_to_all(blocks, ("x", "ylo"), 0, 0, tiled=True)
    return jnp.sum(arrived.astype(F32), axis=0)


def attend_kernel(q_ref, kv_ref, bias_ref, o_ref, lse_ref, s_ref):
    rows, width = q_ref.shape
    heads = width // HD
    keys = kv_ref.shape[0]
    steps = keys // KEYS_STEP
    tops = [jnp.full((1, rows), MASKED, F32) for _ in range(heads)]
    for t in range(steps):
        at = pl.ds(t * KEYS_STEP, KEYS_STEP)
        k = kv_ref[at, :HD]
        bias = bias_ref[at, :]
        for h in range(heads):
            s = nt(k, q_ref[:, h * HD : (h + 1) * HD]) + bias
            s_ref[h, at, :] = s
            tops[h] = jnp.maximum(tops[h], jnp.max(s, axis=0, keepdims=True))
    sums = [jnp.zeros((1, rows), F32) for _ in range(heads)]
    outs = [jnp.zeros((HD, rows), F32) for _ in range(heads)]
    for t in range(steps):
        at = pl.ds(t * KEYS_STEP, KEYS_STEP)
        v_t = kv_ref[at, :].T[HD:, :]
        for h in range(heads):
            e = jnp.exp(s_ref[h, at, :] - tops[h])
            sums[h] = sums[h] + jnp.sum(e, axis=0, keepdims=True)
            outs[h] = outs[h] + nn(v_t, e.astype(BF16))
    flat = jnp.concatenate([outs[h] / sums[h] for h in range(heads)], axis=0)
    o_ref[...] = flat.T.astype(BF16)
    lse_ref[...] = jnp.concatenate(
        [tops[h] + jnp.log(sums[h]) for h in range(heads)], axis=0
    )


def attend(q, kv, bias):
    rows, width = q.shape
    heads, keys = width // HD, kv.shape[0]
    work = heads * rows * keys
    return pl.pallas_call(
        attend_kernel,
        out_shape=(
            jax.ShapeDtypeStruct((rows, width), BF16),
            jax.ShapeDtypeStruct((heads, rows), F32),
        ),
        in_specs=[pl.BlockSpec(memory_space=pltpu.VMEM)] * 3,
        out_specs=(pl.BlockSpec(memory_space=pltpu.VMEM),) * 2,
        scratch_shapes=[pltpu.VMEM((heads, keys, rows), F32)],
        compiler_params=pltpu.CompilerParams(vmem_limit_bytes=40 * 1024 * 1024),
        cost_estimate=pl.CostEstimate(
            flops=4 * work * HD, bytes_accessed=4 * keys * rows, transcendentals=work
        ),
        name="attend",
    )(q, kv, bias)


def attend_back_kernel(q_ref, kv_ref, bias_ref, o_ref, do_ref, lse_ref, dq_ref, dkv_ref):
    rows, width = q_ref.shape
    heads = width // HD
    keys = kv_ref.shape[0]
    steps = keys // KEYS_STEP
    both = (do_ref[...].astype(F32) * o_ref[...].astype(F32)).T
    deltas = [
        jnp.sum(both[h * HD : (h + 1) * HD, :], axis=0, keepdims=True) for h in range(heads)
    ]
    dq_t = [jnp.zeros((HD, rows), F32) for _ in range(heads)]
    for t in range(steps):
        at = pl.ds(t * KEYS_STEP, KEYS_STEP)
        k = kv_ref[at, :HD]
        v = kv_ref[at, HD:]
        k_t = kv_ref[at, :].T[:HD, :]
        bias = bias_ref[at, :]
        dk = jnp.zeros((KEYS_STEP, HD), F32)
        dv = jnp.zeros((KEYS_STEP, HD), F32)
        for h in range(heads):
            q_h = q_ref[:, h * HD : (h + 1) * HD]
            do_h = do_ref[:, h * HD : (h + 1) * HD]
            p = jnp.exp(nt(k, q_h) + bias - lse_ref[h : h + 1, :])
            dp = nt(v, do_h)
            ds = (p * (dp - deltas[h])).astype(BF16)
            dv = dv + nn(p.astype(BF16), do_h)
            dk = dk + nn(ds, q_h)
            dq_t[h] = dq_t[h] + nn(k_t, ds)
        dkv_ref[at, :] = jnp.concatenate([dk, dv], axis=1).astype(BF16)
    dq_ref[...] = jnp.concatenate(dq_t, axis=0).T * (HD**-0.5)


def attend_back(q, kv, bias, o, do, lse):
    rows, width = q.shape
    heads, keys = width // HD, kv.shape[0]
    work = heads * rows * keys
    return pl.pallas_call(
        attend_back_kernel,
        out_shape=(
            jax.ShapeDtypeStruct((rows, width), F32),
            jax.ShapeDtypeStruct((keys, 2 * HD), BF16),
        ),
        in_specs=[pl.BlockSpec(memory_space=pltpu.VMEM)] * 6,
        out_specs=(pl.BlockSpec(memory_space=pltpu.VMEM),) * 2,
        compiler_params=pltpu.CompilerParams(vmem_limit_bytes=40 * 1024 * 1024),
        cost_estimate=pl.CostEstimate(
            flops=10 * work * HD, bytes_accessed=4 * keys * rows, transcendentals=work
        ),
        name="attend_back",
    )(q, kv, bias, o, do, lse)


def gather_weight(shard, place):
    near = swap_ylo(shard)
    far = swap_across(shard)
    far_near = swap_ylo(far)
    first = place["ylo"] == 0
    own = in_order(first, shard, near)
    other = in_order(first, far_near, far)
    early = place["section"] == 0
    pairs = (pick(early, own, other), pick(early, other, own))
    return [lax.all_gather(p, "x", axis=0, tiled=True) for p in pairs]


def reduce_weight_x(grad):
    return lax.psum_scatter(grad, "x", scatter_dimension=0, tiled=True)


def reduce_weight_y(parts, place):
    early = place["section"] == 0
    own = pick(early, parts[0], parts[1])
    other = pick(early, parts[1], parts[0])
    first = place["ylo"] == 0
    n = own.shape[0] // 2
    own_keep, own_send = pick(first, own[:n], own[n:]), pick(first, own[n:], own[:n])
    far_send, far_keep = pick(first, other[:n], other[n:]), pick(first, other[n:], other[:n])
    far = far_keep.astype(F32) + swap_ylo(far_send).astype(F32)
    crossed = swap_across(far.astype(BF16))
    near = swap_ylo(own_send)
    return own_keep.astype(F32) + near.astype(F32) + crossed.astype(F32)


def rms(rows):
    return lax.rsqrt(jnp.mean(rows * rows, axis=-1, keepdims=True) + EPS)


def rotate(v):
    lane = lax.broadcasted_iota(jnp.int32, v.shape, 1) % HD
    return jnp.where(lane < HD // 2, -jnp.roll(v, -HD // 2, 1), jnp.roll(v, HD // 2, 1))


def rotate_back(w):
    lane = lax.broadcasted_iota(jnp.int32, w.shape, 1) % HD
    return jnp.where(lane < HD // 2, jnp.roll(w, -HD // 2, 1), -jnp.roll(w, HD // 2, 1))


def norm_back(grad, n, r, gain):
    scaled = grad * gain
    return r * (scaled - n * jnp.mean(scaled * n, axis=-1, keepdims=True))


def halves(w, first):
    n = w.shape[1] // 2
    return pick(first, w[:, :n], w[:, n:]), pick(first, w[:, n:], w[:, :n])


def body(
    block_input,
    out_grad,
    seg_ids,
    attn_gain,
    w_query,
    w_key,
    w_value,
    w_out,
    ffn_gain,
    w_gate,
    w_up,
    w_down,
):
    place = {name: lax.axis_index(name) for name in AXES}
    section, core, tp = place["section"], place["core"], place["tp"]
    even = core == 0

    q_own, q_send = halves(w_query[0], even)
    kv_own = pick(even, w_key[0], w_value[0])
    kv_send = pick(even, w_value[0], w_key[0])
    out_own, out_send = halves(w_out[0].T, even)
    gate_own, gate_send = halves(w_gate[0], even)
    up_own, up_send = halves(w_up[0], even)
    down_own, down_send = halves(w_down[0].T, even)

    def chip_rows(own, send):
        return in_order(even, jnp.concatenate(own, 1), swap_core(jnp.concatenate(send, 1)))

    w_qkv2 = gather_weight(chip_rows([q_own, kv_own], [q_send, kv_send]), place)
    w_out2 = gather_weight(chip_rows([out_own], [out_send]), place)
    w_gu2 = gather_weight(chip_rows([gate_own, up_own], [gate_send, up_send]), place)
    w_dn2 = gather_weight(chip_rows([down_own], [down_send]), place)

    gains = jnp.concatenate([attn_gain, ffn_gain], axis=0)
    gains = lax.all_gather(gains, ("section", "x", "ylo", "core"), axis=0, tiled=False)
    gains = gains.reshape(2, 16, 2, -1).transpose(0, 2, 1, 3).reshape(2, 2, -1).astype(F32)

    micro_rows = block_input.shape[1]
    group = 8 * micro_rows
    block = place["x"] * 2 + place["ylo"]
    seg_row = lax.dynamic_index_in_dim(seg_ids, section, 0, keepdims=False)
    turn = (jnp.arange(4) + tp) % 4
    inner = turn[:, None] * micro_rows + jnp.arange(micro_rows)[None, :]
    inner = inner.reshape(-1)
    cores = jnp.arange(2)
    q_pos = ((cores + core) % 2)[:, None] * (4 * micro_rows) + inner[None, :]
    q_pos = q_pos.reshape(-1) + block * group
    k_pos = cores[:, None] * (4 * micro_rows) + inner[None, :]
    k_pos = (jnp.arange(8) * group)[:, None] + k_pos.reshape(-1)[None, :]
    k_pos = k_pos.reshape(-1)
    q_seg, k_seg = seg_row[q_pos], seg_row[k_pos]
    seen = (k_pos[:, None] <= q_pos[None, :]) & (k_seg[:, None] == q_seg[None, :])
    bias = jnp.where(seen, 0.0, MASKED).astype(F32)

    frequency = 10000.0 ** (-jnp.arange(0, HD, 2, dtype=F32) / HD)
    angles = q_pos.astype(F32)[:, None] * frequency[None, :]
    cos, sin = jnp.cos(angles), jnp.sin(angles)
    cos, sin = (jnp.concatenate([t] * 10, axis=1) for t in (cos, sin))
    plain = (lax.broadcasted_iota(jnp.int32, cos.shape, 1) >= 4 * HD) & (core == 1)
    cos, sin = jnp.where(plain, 1.0, cos), jnp.where(plain, 0.0, sin)
    q_width = 4 * HD
    scale = jnp.where(jnp.arange(cos.shape[1]) < q_width, HD**-0.5, 1.0)

    def forward(x, layer):
        gain_a, gain_f = gains[layer, 0], gains[layer, 1]
        r1 = rms(x)
        a = gather_rows((x * r1 * gain_a).astype(BF16))
        qkv = nn(a, w_qkv2[layer])
        qkv = (qkv * cos + rotate(qkv) * sin).astype(BF16)
        q = qkv[:, :q_width] * jnp.asarray(HD**-0.5, BF16)
        kv = qkv[:, q_width:]
        n = kv.shape[0] // 2
        kv = pick(even, kv, jnp.concatenate([kv[n:], kv[:n]], axis=0))
        kv = gather_kv(in_order(even, kv, swap_core(kv), 1))
        ctx, lse = attend(q, kv, bias)
        mid = x + reduce_rows(nt(ctx, w_out2[layer]))
        r2 = rms(mid)
        b = gather_rows((mid * r2 * gain_f).astype(BF16))
        gu = nn(b, w_gu2[layer])
        units = gu.shape[1] // 2
        gate, up = gu[:, :units], gu[:, units:]
        hidden = (gate / (1.0 + jnp.exp(-gate)) * up).astype(BF16)
        y = mid + reduce_rows(nt(hidden, w_dn2[layer]))
        return y, (x, r1, a, q, kv, ctx, lse, mid, r2, b, gate, up, hidden)

    def backward(dy, kept, layer):
        x, r1, a, q, kv, ctx, lse, mid, r2, b, gate, up, hidden = kept
        gain_a, gain_f = gains[layer, 0], gains[layer, 1]
        dff = gather_rows(dy.astype(BF16))
        g_dn = tn(dff, hidden).astype(BF16)
        dhidden = nn(dff, w_dn2[layer])
        sig = 1.0 / (1.0 + jnp.exp(-gate))
        dgate = dhidden * up * (sig * (1.0 + gate * (1.0 - sig)))
        dup = dhidden * (gate * sig)
        dgu = jnp.concatenate([dgate, dup], axis=1).astype(BF16)
        g_gu = tn(b, dgu).astype(BF16)
        db = reduce_rows(nt(dgu, w_gu2[layer]))
        n2 = mid * r2
        gg_f = jnp.sum(db * n2, axis=0)
        dmid = dy + norm_back(db, n2, r2, gain_f)
        dattn = gather_rows(dmid.astype(BF16))
        g_out = tn(dattn, ctx).astype(BF16)
        do = nn(dattn, w_out2[layer]).astype(BF16)
        dq, dkv = attend_back(q, kv, bias, ctx, do, lse)
        dkv = reduce_kv(dkv)
        n = dkv.shape[0] // 2
        dkv_own = pick(even, dkv[:, :HD], dkv[:, HD:])
        dkv_send = pick(even, dkv[:, HD:], dkv[:, :HD])
        dkv = dkv_own + swap_core(dkv_send.astype(BF16)).astype(F32)
        dkv = pick(even, dkv, jnp.concatenate([dkv[n:], dkv[:n]], axis=0))
        dqkv = jnp.concatenate([dq, dkv], axis=1)
        dqkv = (dqkv * cos + rotate_back(dqkv * sin)).astype(BF16)
        g_qkv = tn(a, dqkv).astype(BF16)
        da = reduce_rows(nt(dqkv, w_qkv2[layer]))
        n1 = x * r1
        gg_a = jnp.sum(da * n1, axis=0)
        dx = dmid + norm_back(da, n1, r1, gain_a)
        return dx, (g_qkv, g_out, g_gu, g_dn), (gg_a, gg_f)

    x0 = lax.dynamic_index_in_dim(block_input, section, 0, keepdims=False).astype(F32)
    y0, kept0 = forward(x0, 0)
    y0_low = y0.astype(BF16)
    y1, kept1 = forward(y0_low.astype(F32), 1)
    y1_low = y1.astype(BF16)
    dy1 = lax.dynamic_index_in_dim(out_grad, section, 0, keepdims=False).astype(F32)
    dx1, mats1, gg1 = backward(dy1, kept1, 1)
    parts1 = [reduce_weight_x(g) for g in mats1]
    dx0, mats0, gg0 = backward(dx1.astype(BF16).astype(F32), kept0, 0)
    parts0 = [reduce_weight_x(g) for g in mats0]

    early = section == 0

    def both_micros(layer0, layer1, dtype):
        own = pick(early, layer0, layer1)
        other = swap_section(pick(early, layer1, layer0).astype(BF16)).astype(dtype)
        return in_order(early, own.astype(dtype)[None], other[None])[None]

    block_output = both_micros(y0_low, y1_low, BF16)
    input_grad = both_micros(dx0, dx1, F32)

    def finish(parts):
        chip = reduce_weight_y(parts, place)
        n = chip.shape[0] // 2
        own, send = pick(even, chip[:n], chip[n:]), pick(even, chip[n:], chip[:n])
        other = swap_core(send.astype(BF16)).astype(F32)
        return own, other

    def across(own, other):
        return in_order(even, own, other, 1)

    g_qkv, g_out, g_gu, g_dn = [finish(p) for p in zip(parts0, parts1)]
    w = q_width
    grad_query = across(g_qkv[0][:, :w], g_qkv[1][:, :w])
    grad_key = pick(even, g_qkv[0][:, w:], g_qkv[1][:, w:])
    grad_value = pick(even, g_qkv[1][:, w:], g_qkv[0][:, w:])
    grad_out = across(*g_out).T
    u = g_gu[0].shape[1] // 2
    grad_gate = across(g_gu[0][:, :u], g_gu[1][:, :u])
    grad_up = across(g_gu[0][:, u:], g_gu[1][:, u:])
    grad_down = across(*g_dn).T

    own = pick(early, jnp.stack(gg0), jnp.stack(gg1))
    other = pick(early, jnp.stack(gg1), jnp.stack(gg0))
    own = own + swap_section(other)
    blocks = own.reshape(2, 64, -1).transpose(1, 0, 2)
    gain_sums = jnp.sum(
        lax.all_to_all(blocks, ("x", "ylo", "core", "tp"), 0, 0, tiled=True), axis=0
    )
    return (
        block_output,
        input_grad,
        gain_sums[0][None],
        grad_query[None],
        grad_key[None],
        grad_value[None],
        grad_out[None],
        gain_sums[1][None],
        grad_gate[None],
        grad_up[None],
        grad_down[None],
    )


def solution(mesh):
    fine = Mesh(mesh.devices.reshape(2, 4, 2, 2, 4), AXES)
    wide = ("x", "ylo", "core")
    rows = P(None, (*wide, "tp"), None)
    into = P("section", wide, "tp")
    out_of = P("section", "tp", wide)
    grown = P("section", None, (*wide, "tp"), None)
    gain_grad = P("section", (*wide, "tp"))
    return jax.shard_map(
        body,
        mesh=fine,
        in_specs=(
            rows, rows, P(), P("section", wide), into, into, into, out_of,
            P("section", wide), into, into, out_of,
        ),
        out_specs=(
            grown, grown, gain_grad, into, into, into, out_of, gain_grad, into, into, out_of,
        ),
        check_vma=False,
    )
```

```python
import functools
import math

import jax
import jax.numpy as jnp
from jax import lax
from jax.experimental import pallas as pl
from jax.experimental.pallas import tpu as pltpu
from jax.sharding import Mesh, PartitionSpec as P

HD = 64
GAIN_ROWS = 16
EPS = 1e-05
MASKED = -1e30
KEYS_STEP = 512
AXES = ("section", "x", "ylo", "core", "tp")
SECTION, X, YLO, CORE, TP = range(5)
BF16 = jnp.bfloat16
F32 = jnp.float32
VMEM = pl.BlockSpec(memory_space=pltpu.VMEM)
SMEM = pl.BlockSpec(memory_space=pltpu.SMEM)
HBM = pl.BlockSpec(memory_space=pltpu.HBM)
DMA = pltpu.SemaphoreType.DMA


def nn(a, b):
    return jnp.dot(a, b, preferred_element_type=F32)


def nt(a, b):
    return lax.dot_general(a, b, (((1,), (1,)), ((), ())), preferred_element_type=F32)


def tn(a, b):
    return lax.dot_general(a, b, (((0,), (0,)), ((), ())), preferred_element_type=F32)


def shape(dims, dtype=BF16):
    return jax.ShapeDtypeStruct(tuple(dims), dtype)


SHORT = pl.CostEstimate(flops=1, bytes_accessed=1, transcendentals=0)


def call(kernel, outs, args, scratch=(), room=8, spec=VMEM, out_spec=VMEM):
    specs = []
    for a in args:
        own = SMEM if not isinstance(a, list) and a.dtype == jnp.int32 else spec
        specs += [HBM] * len(a) if isinstance(a, list) else [own]
    args = [v for a in args for v in (a if isinstance(a, list) else [a])]
    held = [m for m in scratch if isinstance(m, pltpu.VMEM((8, 128), F32).__class__)]
    room = room * 2**20 + sum(
        math.prod(m.shape) * jnp.dtype(m.dtype).itemsize for m in held if m.dtype in (BF16, F32)
    )
    return pl.pallas_call(
        kernel,
        out_shape=tuple(outs),
        in_specs=specs,
        out_specs=(out_spec,) * len(outs),
        scratch_shapes=list(scratch),
        compiler_params=pltpu.CompilerParams(vmem_limit_bytes=room),
        cost_estimate=SHORT,
        name=getattr(kernel, "func", kernel).__name__,
    )(*args)


def from_z(rows, by):
    return lax.ppermute(rows, "tp", [((i + by) % 4, i) for i in range(4)])


def from_x(v, by):
    return lax.ppermute(v, "x", [((i + by) % 4, i) for i in range(4)])


def swap_core(v):
    return lax.ppermute(v, "core", [(0, 1), (1, 0)])


def swap_ylo(v):
    return lax.ppermute(v, "ylo", [(0, 1), (1, 0)])


def swap_section(v):
    return lax.ppermute(v, "section", [(0, 1), (1, 0)])


def swap_across(v):
    return lax.ppermute(v, ("section", "ylo"), [(0, 3), (3, 0), (1, 2), (2, 1)])


def after(value, *others):
    return lax.optimization_barrier((value, *others))[0]


def y_exchange(v):
    return swap_ylo(v), swap_across(v), swap_section(v)


def gather_rows(rows):
    pieces = [rows] + [from_z(rows, k) for k in (1, 2, 3)]
    return pieces + [swap_core(p) for p in pieces]


def gather_kv(half):
    copies = jnp.broadcast_to(half[None], (8, *half.shape))
    own = lax.all_to_all(copies, ("x", "ylo"), 0, 0, tiled=True).reshape(-1, half.shape[1])
    return own, swap_core(own)


def reduce_rows(send, mine):
    own, *pieces = split(mine, swap_core(send))
    return [own] + [from_z(p, -k) for k, p in zip((1, 2, 3), pieces)]


def gather_x(block):
    return lax.all_gather(block, "x", axis=0, tiled=True)


def reduce_x(grad):
    return lax.psum_scatter(grad, "x", scatter_dimension=0, tiled=True)


def pack_attn_kernel(place, q_ref, k_ref, v_ref, o_ref, ga_ref, gf_ref, own_ref, send_ref):
    n, rows = q_ref.shape[1] // 2, q_ref.shape[0]
    m = n + 2 * HD
    kv = jnp.concatenate([k_ref[...], v_ref[...]], axis=1)
    o = o_ref[...].T
    odd = place[CORE] == 1
    row = lax.broadcasted_iota(jnp.int32, (GAIN_ROWS, ga_ref.shape[1]), 0)
    ga, gf = (jnp.broadcast_to(g[...].astype(F32), row.shape) for g in (ga_ref, gf_ref))
    gains = jnp.where(row == 0, ga, jnp.where(row == 1, gf, 0.0)).astype(BF16)
    rest = jnp.zeros((GAIN_ROWS, own_ref.shape[1] - gains.shape[1]), BF16)
    for ref, high in ((own_ref, odd), (send_ref, jnp.logical_not(odd))):
        ref[:rows, :n] = jnp.where(high, q_ref[:, n:], q_ref[:, :n])
        ref[:rows, n:m] = kv
        ref[:rows, m:] = jnp.where(high, o[:, n:], o[:, :n])
        ref[rows:, :] = jnp.concatenate([gains, rest], axis=1)


def pack_ffn_kernel(place, d_ref, g_ref, u_ref, own_ref, send_ref):
    odd = place[CORE] == 1
    d = d_ref[...].T
    n = d.shape[1] // 2
    spare = jnp.zeros((own_ref.shape[0], own_ref.shape[1] - 3 * n), BF16)
    low, high = (
        jnp.concatenate([w[:, at] for w in (g_ref[...], u_ref[...], d)] + [spare], axis=1)
        for at in (slice(0, n), slice(n, 2 * n))
    )
    own_ref[...] = jnp.where(odd, high, low)
    send_ref[...] = jnp.where(odd, low, high)


def chip_rows_kernel(place, own_ref, other_ref, out_ref):
    n = own_ref.shape[0]
    core = place[CORE]
    out_ref[pl.ds(pl.multiple_of(core * n, n), n), :] = own_ref[...]
    out_ref[pl.ds(pl.multiple_of((1 - core) * n, n), n), :] = other_ref[...]


def chip_rows(place, own, other):
    n, c = own.shape
    return call(chip_rows_kernel, [shape((2 * n, c))], [place, own, other])[0]


def chip_attn_kernel(place, own_ref, other_ref, out_ref):
    n = own_ref.shape[0] - GAIN_ROWS
    core = place[CORE]
    odd = core == 1
    out_ref[pl.ds(pl.multiple_of(core * n, n), n), :] = own_ref[:n, :]
    out_ref[pl.ds(pl.multiple_of((1 - core) * n, n), n), :] = other_ref[:n, :]
    own, other = own_ref[n:, :n], other_ref[n:, :n]
    rest = jnp.zeros((GAIN_ROWS, out_ref.shape[1] - 2 * n), BF16)
    out_ref[2 * n :, :] = jnp.concatenate(
        [jnp.where(odd, other, own), jnp.where(odd, own, other), rest], axis=1
    )


def pairs_kernel(place, own_ref, near_ref, far_ref, straight_ref, p0_ref, p1_ref):
    n = own_ref.shape[0]
    here = pl.ds(pl.multiple_of(place[YLO] * n, n), n)
    there = pl.ds(pl.multiple_of((1 - place[YLO]) * n, n), n)

    def fill(mine, other):
        mine[here, :] = own_ref[...]
        mine[there, :] = near_ref[...]
        other[here, :] = straight_ref[...]
        other[there, :] = far_ref[...]

    @pl.when(place[SECTION] == 0)
    def _():
        fill(p0_ref, p1_ref)

    @pl.when(place[SECTION] == 1)
    def _():
        fill(p1_ref, p0_ref)


def pairs(place, own, others):
    n, c = own.shape
    out = shape((2 * n, c))
    return call(pairs_kernel, [out, out], [place, own, *others])


def fetch(pieces, whole, sems):
    n = pieces[0].shape[0]
    copies = [
        pltpu.make_async_copy(p, whole.at[pl.ds(i * n, n), :], sems.at[i])
        for i, p in enumerate(pieces)
    ]
    for c in copies:
        c.start()

    def wait():
        for c in copies:
            c.wait()

    return wait


def rms(rows):
    return lax.rsqrt(jnp.mean(rows * rows, axis=-1, keepdims=True) + EPS)


def turned(v, by):
    return pltpu.roll(v, by % v.shape[1], 1)


def low_half(v):
    return lax.broadcasted_iota(jnp.int32, v.shape, 1) % HD < HD // 2


def rope(v, cos, sin):
    half = HD // 2
    return v * cos + jnp.where(low_half(v), -turned(v, -half), turned(v, half)) * sin


def rope_back(u, cos, sin):
    half, w = HD // 2, u * sin
    return u * cos + jnp.where(low_half(w), turned(w, -half), -turned(w, half))


def halves_out(partial, send_ref, mine_ref):
    n = send_ref.shape[0]
    send_ref[...] = partial[n:].astype(BF16)
    mine_ref[...] = partial[:n]


def split_kernel(mine_ref, other_ref, own_ref, *piece_refs):
    n = own_ref.shape[0]
    own_ref[...] = mine_ref[:n, :] + other_ref[:n, :].astype(F32)
    for k, ref in enumerate(piece_refs, 1):
        at = slice(k * n, (k + 1) * n)
        ref[...] = (mine_ref[at, :] + other_ref[at, :].astype(F32)).astype(BF16)


def split(mine, other):
    n, d = mine.shape[0] // 4, mine.shape[1]
    return call(split_kernel, [shape((n, d), F32)] + [shape((n, d))] * 3, [mine, other])


def total_of(refs):
    return sum((r[...].astype(F32) for r in refs[1:]), refs[0][...])


def add_norm_kernel(a, b, c, d, x_ref, gain_ref, mid_ref, low_ref):
    mid = x_ref[...].astype(F32) + total_of((a, b, c, d))
    mid_ref[...] = mid
    low_ref[...] = (mid * rms(mid) * gain_ref[...]).astype(BF16)


def add_kernel(a, b, c, d, mid_ref, y_ref):
    y_ref[...] = (mid_ref[...] + total_of((a, b, c, d))).astype(BF16)


def norm_back_kernel(a, b, c, d, after_ref, x_ref, gain_ref, dx_ref, low_ref, gain_grad_ref):
    grad = total_of((a, b, c, d))
    x = x_ref[...].astype(F32)
    r = rms(x)
    n = x * r
    gain_grad_ref[...] = jnp.sum(grad * n, axis=0, keepdims=True)
    scaled = grad * gain_ref[...]
    dx = after_ref[...].astype(F32) + r * (
        scaled - n * jnp.mean(scaled * n, axis=-1, keepdims=True)
    )
    dx_ref[...] = dx
    low_ref[...] = dx.astype(BF16)


def qkv_kernel(place, *refs, parts):
    pieces, refs = refs[:8], refs[8:]
    weights, refs = refs[:parts], refs[parts:]
    cos_ref, sin_ref, x_ref, a_ref, q_ref, kv_ref, w_ref, wo_ref, ga_ref, gf_ref, *refs = refs
    gains_ref, x_sems, w_sems = refs
    rows_there = fetch(pieces, x_ref, x_sems)
    n = w_ref.shape[0] // 8
    step = n + GAIN_ROWS

    def copies(i, block):
        src, at = (weights[0], i * step) if parts == 1 else (weights[i // 2], i % 2 * step)
        rows = pl.ds(pl.multiple_of(block * n, n), n)
        cols, m = w_ref.shape[1], wo_ref.shape[1]
        sides = (
            (src.at[pl.ds(at, n), pl.ds(0, cols)], w_ref.at[rows, :]),
            (src.at[pl.ds(at, n), pl.ds(cols, m)], wo_ref.at[rows, :]),
            (src.at[pl.ds(at + n, GAIN_ROWS), pl.ds(0, n)], gains_ref.at[block]),
        )
        return [pltpu.make_async_copy(a, b, w_sems.at[i, j]) for j, (a, b) in enumerate(sides)]

    for i in range(8):
        block = i if parts == 1 else lax.rem(place[X] + i // 2, 4) * 2 + i % 2
        for c in copies(i, block):
            c.start()
    for i in range(8):
        for c in copies(i, i):
            c.wait()
    gains = jnp.concatenate([gains_ref[i] for i in range(8)], axis=1).astype(F32)
    ga_ref[...] = gains[0:1, :]
    gf_ref[...] = gains[1:2, :]
    rows_there()
    x = x_ref[...].astype(F32)
    a = (x * rms(x) * ga_ref[...]).astype(BF16)
    a_ref[...] = a
    out = rope(nn(a, w_ref[...]), cos_ref[...], sin_ref[...])
    width = q_ref.shape[1]
    q_ref[...] = (out[:, :width].astype(BF16).astype(F32) * HD**-0.5).astype(BF16)
    half = out.shape[0] // 2
    k, v = out[:, width : width + HD], out[:, width + HD :]
    keys = jnp.concatenate([k[:half], k[half:]], axis=1)
    values = jnp.concatenate([v[half:], v[:half]], axis=1)
    kv_ref[...] = jnp.where(place[CORE] == 1, values, keys).astype(BF16)


def key_step(ref, t):
    per = ref.shape[0] // KEYS_STEP
    return pl.ds(t % per * KEYS_STEP, KEYS_STEP), slice(t // per * HD, (t // per + 1) * HD)


def attend_kernel(place, q_ref, own_ref, other_ref, bias_ref, w_hbm, *refs):
    o_ref, lse_ref, k_ref, v_ref, send_ref, mine_ref, s_ref, w_ref, sem = refs
    load = pltpu.make_async_copy(w_hbm, w_ref, sem)
    load.start()
    odd = place[CORE] == 1
    k_ref[...] = jnp.where(odd, other_ref[...], own_ref[...])
    v_ref[...] = jnp.where(odd, own_ref[...], other_ref[...])
    rows, width = q_ref.shape
    heads = width // HD
    steps = 2 * k_ref.shape[0] // KEYS_STEP
    tops = [jnp.full((1, rows), MASKED, F32) for _ in range(heads)]
    for t in range(steps):
        at = pl.ds(t * KEYS_STEP, KEYS_STEP)
        part, cols = key_step(k_ref, t)
        k = k_ref[part, cols]
        bias = bias_ref[at, :]
        for h in range(heads):
            s = nt(k, q_ref[:, h * HD : (h + 1) * HD]) + bias
            s_ref[h, at, :] = s
            tops[h] = jnp.maximum(tops[h], jnp.max(s, axis=0, keepdims=True))
    sums = [jnp.zeros((1, rows), F32) for _ in range(heads)]
    outs = [jnp.zeros((HD, rows), F32) for _ in range(heads)]
    for t in range(steps):
        at = pl.ds(t * KEYS_STEP, KEYS_STEP)
        part, cols = key_step(v_ref, t)
        v_t = v_ref[part, :].T[cols, :]
        for h in range(heads):
            e = jnp.exp(s_ref[h, at, :] - tops[h])
            sums[h] = sums[h] + jnp.sum(e, axis=0, keepdims=True)
            outs[h] = outs[h] + nn(v_t, e.astype(BF16))
    flat = jnp.concatenate([outs[h] / sums[h] for h in range(heads)], axis=0)
    o_ref[...] = flat.T.astype(BF16)
    lse_ref[...] = jnp.concatenate([tops[h] + jnp.log(sums[h]) for h in range(heads)], axis=0)
    load.wait()
    halves_out(nt(o_ref[...], w_ref[...]), send_ref, mine_ref)


def ffn_kernel(*refs):
    pieces, w_hbm, refs = refs[:8], refs[8], refs[9:]
    b_ref, gu_ref, h_ref, send_ref, mine_ref, gu_w, down_w, b_sems, gu_sems, sem = refs
    rows_there = fetch(pieces, b_ref, b_sems)
    steps, n, c = 4, w_hbm.shape[0] // 4, gu_w.shape[1]

    def load(i):
        at = pl.ds(i * n, n)
        return pltpu.make_async_copy(w_hbm.at[at, pl.ds(0, c)], gu_w.at[at, :], gu_sems.at[i])

    for i in range(steps):
        load(i).start()
    down = pltpu.make_async_copy(w_hbm.at[:, pl.ds(c, down_w.shape[1])], down_w, sem)
    down.start()
    rows_there()
    for i in range(steps):
        load(i).wait()
        at = slice(i * n, (i + 1) * n)
        part = nn(b_ref[:, at], gu_w[at, :])
        gu_ref[...] = part if i == 0 else gu_ref[...] + part
    units = gu_ref.shape[1] // 2
    gate, up = gu_ref[:, :units], gu_ref[:, units:]
    h_ref[:, :units] = (gate / (1.0 + jnp.exp(-gate)) * up).astype(BF16)
    spare = h_ref.shape[1] - units
    h_ref[:, units:] = jnp.zeros((h_ref.shape[0], spare), BF16)
    down.wait()
    halves_out(nt(h_ref[...], down_w[...]), send_ref, mine_ref)


def ffn_back_kernel(*refs):
    pieces, w_hbm, act_hbm, refs = refs[:8], refs[8], refs[9], refs[10:]
    dff_ref, dgu_ref, send_ref, mine_ref, gu_w, down_w, gu_ref, r_sems, gu_sems = refs
    rows_there = fetch(pieces, dff_ref, r_sems)
    c = gu_w.shape[1]
    down = pltpu.make_async_copy(w_hbm.at[:, pl.ds(c, down_w.shape[1])], down_w, gu_sems.at[2])
    down.start()
    act = pltpu.make_async_copy(act_hbm, gu_ref, gu_sems.at[0])
    act.start()
    load = pltpu.make_async_copy(w_hbm.at[:, pl.ds(0, c)], gu_w, gu_sems.at[1])
    load.start()
    rows_there()
    down.wait()
    units = gu_ref.shape[1] // 2
    dh = nn(dff_ref[...], down_w[...])[:, :units]
    act.wait()
    gate, up = gu_ref[:, :units], gu_ref[:, units:]
    sig = 1.0 / (1.0 + jnp.exp(-gate))
    dgate = dh * up * (sig * (1.0 + gate * (1.0 - sig)))
    dgu_ref[...] = jnp.concatenate([dgate, dh * (gate * sig)], axis=1).astype(BF16)
    load.wait()
    halves_out(nt(dgu_ref[...], gu_w[...]), send_ref, mine_ref)


def attend_back_kernel(place, *refs):
    pieces, refs = refs[:8], refs[8:]
    w_hbm, q_ref, k_ref, v_ref, bias_ref, o_ref, lse_ref, cos_ref, sin_ref, *refs = refs
    dattn_ref, dq_ref, own_ref, send_ref, w_ref, do_ref, dk_ref, dv_ref, sem, r_sems = refs
    rows_there = fetch(pieces, dattn_ref, r_sems)
    load = pltpu.make_async_copy(w_hbm, w_ref, sem)
    load.start()
    rows, width = q_ref.shape
    heads = width // HD
    steps = 2 * k_ref.shape[0] // KEYS_STEP
    rows_there()
    load.wait()
    do = nn(dattn_ref[...], w_ref[...])
    do_ref[...] = do.astype(BF16)
    both = (do_ref[...].astype(F32) * o_ref[...].astype(F32)).T
    deltas = [
        jnp.sum(both[h * HD : (h + 1) * HD, :], axis=0, keepdims=True) for h in range(heads)
    ]
    dq_t = [jnp.zeros((HD, rows), F32) for _ in range(heads)]
    for t in range(steps):
        at = pl.ds(t * KEYS_STEP, KEYS_STEP)
        part, cols = key_step(k_ref, t)
        k = k_ref[part, cols]
        v = v_ref[part, cols]
        k_t = k_ref[part, :].T[cols, :]
        bias = bias_ref[at, :]
        dk = jnp.zeros((KEYS_STEP, HD), F32)
        dv = jnp.zeros((KEYS_STEP, HD), F32)
        for h in range(heads):
            q_h = q_ref[:, h * HD : (h + 1) * HD]
            do_h = do_ref[:, h * HD : (h + 1) * HD]
            p = jnp.exp(nt(k, q_h) + bias - lse_ref[h : h + 1, :])
            ds = (p * (nt(v, do_h) - deltas[h])).astype(BF16)
            dv = dv + nn(p.astype(BF16), do_h)
            dk = dk + nn(ds, q_h)
            dq_t[h] = dq_t[h] + nn(k_t, ds)
        dk_ref[part, cols] = dk
        dv_ref[part, cols] = dv
    dq = jnp.concatenate(dq_t, axis=0).T * HD**-0.5
    dq_ref[...] = rope_back(dq, cos_ref[:, :width], sin_ref[:, :width]).astype(BF16)
    odd = place[CORE] == 1
    own_ref[...] = jnp.where(odd, dv_ref[...], dk_ref[...])
    send_ref[...] = jnp.where(odd, dk_ref[...], dv_ref[...]).astype(BF16)


def kv_add_kernel(own_ref, other_ref, out_ref):
    out_ref[...] = (own_ref[...] + other_ref[...].astype(F32)).astype(BF16)


def qkv_back_kernel(place, w_hbm, x_hbm, dq_ref, kv_ref, cos_ref, sin_ref, *refs):
    dqkv_ref, send_ref, mine_ref, gain_grad_ref, w_ref, x_ref, sems = refs
    load = pltpu.make_async_copy(w_hbm, w_ref, sems.at[0])
    load.start()
    rows_there = pltpu.make_async_copy(x_hbm, x_ref, sems.at[1])
    rows_there.start()
    width, odd = dq_ref.shape[1], place[CORE] == 1
    both = sum((kv_ref[i].astype(F32) for i in range(1, 8)), kv_ref[0].astype(F32))
    first, second = both[:, :HD], both[:, HD:]
    dk = jnp.concatenate([first, second], axis=0)
    dv = jnp.concatenate([second, first], axis=0)
    spare = jnp.zeros_like(dk)
    dkv = jnp.where(
        odd, jnp.concatenate([spare, dv], axis=1), jnp.concatenate([dk, spare], axis=1)
    )
    dkv = rope_back(dkv, cos_ref[:, width:], sin_ref[:, width:])
    dqkv_ref[:, :width] = dq_ref[...]
    dqkv_ref[:, width:] = dkv.astype(BF16)
    load.wait()
    da = nt(dqkv_ref[...], w_ref[...])
    halves_out(da, send_ref, mine_ref)
    rows_there.wait()
    x = x_ref[...].astype(F32)
    gain_grad_ref[...] = jnp.sum(da * (x * rms(x)), axis=0, keepdims=True)


def ffn_product_kernel(b_ref, dgu_ref, dff_ref, h_ref, out_ref):
    n = dgu_ref.shape[1]
    out_ref[:, :n] = tn(b_ref[...], dgu_ref[...]).astype(BF16)
    out_ref[:, n:] = tn(dff_ref[...], h_ref[...]).astype(BF16)


def ffn_products(b, dgu, dff, hidden):
    rows, d = b.shape
    n, wide = 256, dgu.shape[1] + hidden.shape[1]
    left = pl.BlockSpec((rows, n), lambda i: (0, i))
    return pl.pallas_call(
        ffn_product_kernel,
        out_shape=shape((d, wide)),
        grid=(d // n,),
        in_specs=[
            left,
            pl.BlockSpec(dgu.shape, lambda i: (0, 0)),
            left,
            pl.BlockSpec(hidden.shape, lambda i: (0, 0)),
        ],
        out_specs=pl.BlockSpec((n, wide), lambda i: (i, 0)),
        compiler_params=pltpu.CompilerParams(vmem_limit_bytes=16 * 1024 * 1024),
        cost_estimate=SHORT,
        name="ffn_product_kernel",
    )(b, dgu, dff, hidden)


def attn_product_kernel(dattn, a, gg_a, gg_f, ctx, dqkv, out):
    m = ctx.shape[1]
    wide = m + dqkv.shape[1]
    out[:, :m] = tn(dattn[...], ctx[...]).astype(BF16)
    out[:, m:wide] = tn(a[...], dqkv[...]).astype(BF16)
    row = lax.broadcasted_iota(jnp.int32, (out.shape[1] - wide, a.shape[1]), 0)
    ga, gf = (jnp.broadcast_to(g[...], row.shape) for g in (gg_a, gg_f))
    out[:, wide:] = jnp.where(row == 0, ga, jnp.where(row == 1, gf, 0.0)).T.astype(BF16)


def attn_products(dattn, ctx, a, dqkv, gg_a, gg_f):
    rows, d = a.shape
    n, wide = 512, ctx.shape[1] + dqkv.shape[1] + 128
    by_columns = [pl.BlockSpec((v.shape[0], n), lambda i: (0, i)) for v in (dattn, a, gg_a, gg_f)]
    return pl.pallas_call(
        attn_product_kernel,
        out_shape=shape((d, wide)),
        grid=(d // n,),
        in_specs=by_columns + [pl.BlockSpec(v.shape, lambda i: (0, 0)) for v in (ctx, dqkv)],
        out_specs=pl.BlockSpec((n, wide), lambda i: (i, 0)),
        compiler_params=pltpu.CompilerParams(vmem_limit_bytes=16 * 1024 * 1024),
        cost_estimate=SHORT,
        name="attn_product_kernel",
    )(dattn, a, gg_a, gg_f, ctx, dqkv)


def y_split_kernel(place, r0_ref, r1_ref, keep_ref, near_ref, far_ref, straight_ref):
    n = keep_ref.shape[0]
    here = pl.ds(pl.multiple_of(place[YLO] * n, n), n)
    there = pl.ds(pl.multiple_of((1 - place[YLO]) * n, n), n)

    def fill(mine, other):
        keep_ref[...] = mine[here, :]
        near_ref[...] = mine[there, :]
        straight_ref[...] = other[here, :]
        far_ref[...] = other[there, :]

    @pl.when(place[SECTION] == 0)
    def _():
        fill(r0_ref, r1_ref)

    @pl.when(place[SECTION] == 1)
    def _():
        fill(r1_ref, r0_ref)


def by_core_kernel(place, *refs):
    *parts, own_ref, send_ref = refs
    n = own_ref.shape[0]
    here = pl.ds(pl.multiple_of(place[CORE] * n, n), n)
    there = pl.ds(pl.multiple_of((1 - place[CORE]) * n, n), n)
    own_ref[...] = sum(p[here, :].astype(F32) for p in parts)
    send_ref[...] = sum(p[there, :].astype(F32) for p in parts).astype(BF16)


def by_core(parts, place):
    n, c = parts[0].shape[0] // 2, parts[0].shape[1]
    own, send = call(by_core_kernel, [shape((n, c), F32), shape((n, c))], [place, *parts])
    return own, swap_core(send)


def reduce_y(r0, r1, place):
    n, c = r0.shape[0] // 2, r0.shape[1]
    keep, near, far, straight = call(y_split_kernel, [shape((n, c))] * 4, [place, r0, r1])
    return [keep, swap_ylo(near), swap_across(far), swap_section(straight)]


def ordered(odd, own, other):
    other = other.astype(F32)
    return jnp.concatenate(
        [jnp.where(odd, other, own), jnp.where(odd, own, other)], axis=1
    )


def attn_grads_kernel(place, own_ref, other_ref, o_ref, q_ref, k_ref, v_ref, *gain_refs):
    odd = place[CORE] == 1
    m = n = q_ref.shape[1] // 2
    own, other = own_ref[:, :m].T, other_ref[:, :m].astype(F32).T
    o_ref[:m, :] = jnp.where(odd, other, own)
    o_ref[m:, :] = jnp.where(odd, own, other)
    q_ref[...] = ordered(odd, own_ref[:, m : m + n], other_ref[:, m : m + n])
    both = own_ref[:, m + n :] + other_ref[:, m + n :].astype(F32)
    k_ref[...] = both[:, :HD]
    v_ref[...] = both[:, HD : 2 * HD]
    rows = gain_refs[0].shape[0]
    gain_refs[-1][...] = both[:, 2 * HD :]
    for k, ref in enumerate(gain_refs[:-1]):
        at = lax.rem(place[TP] + k, 4) * rows
        ref[...] = gain_refs[-1][pl.ds(pl.multiple_of(at, rows), rows), :]


def ffn_grads_kernel(place, own_ref, other_ref, gate_ref, up_ref, down_ref):
    odd = place[CORE] == 1
    n = gate_ref.shape[1] // 2
    gate_ref[...] = ordered(odd, own_ref[:, :n], other_ref[:, :n])
    up_ref[...] = ordered(odd, own_ref[:, n : 2 * n], other_ref[:, n : 2 * n])
    own, other = own_ref[:, 2 * n :].T[:n], other_ref[:, 2 * n :].astype(F32).T[:n]
    down_ref[:n, :] = jnp.where(odd, other, own)
    down_ref[n:, :] = jnp.where(odd, own, other)


def body(
    block_input,
    out_grad,
    seg_ids,
    attn_gain,
    w_query,
    w_key,
    w_value,
    w_out,
    ffn_gain,
    w_gate,
    w_up,
    w_down,
):
    at = {name: lax.axis_index(name) for name in AXES}
    section, core, tp = at["section"], at["core"], at["tp"]
    place = jnp.stack([at[name] for name in AXES]).astype(jnp.int32)
    d = block_input.shape[2]
    micro_rows = block_input.shape[1]
    group = 8 * micro_rows
    q_width = w_query.shape[2] // 2
    units = w_gate.shape[2] // 2
    own_rows = w_query.shape[1]

    padded = units + (-units) % 128
    attn_dims = (own_rows + GAIN_ROWS, 2 * q_width + 2 * HD)
    attn_own, attn_send = call(
        pack_attn_kernel,
        [shape(attn_dims)] * 2,
        [place, w_query[0], w_key[0], w_value[0], w_out[0], attn_gain, ffn_gain],
        spec=pl.BlockSpec(),
    )
    attn_shard = call(
        chip_attn_kernel,
        [shape((2 * own_rows + GAIN_ROWS, attn_dims[1]))],
        [place, attn_own, swap_core(attn_send)],
    )[0]
    attn_y = y_exchange(attn_shard)
    attn_pairs = pairs(place, attn_shard, attn_y)
    attn0 = [attn_pairs[0]] + [from_x(attn_pairs[0], k) for k in (1, 2, 3)]

    ffn_own, ffn_send = call(
        pack_ffn_kernel,
        [shape((own_rows, 2 * units + padded))] * 2,
        [place, w_down[0], after(w_gate, attn_y[0])[0], w_up[0]],
        room=12,
        spec=pl.BlockSpec(),
    )
    ffn_shard = chip_rows(place, ffn_own, swap_core(ffn_send))
    ffn_y = y_exchange(after(ffn_shard, attn_pairs[0]))

    block = at["x"] * 2 + at["ylo"]
    seg_row = lax.dynamic_index_in_dim(seg_ids, section, 0, keepdims=False)
    def arranged(row):
        v = row.reshape(8, 2, 4, micro_rows)
        return lax.dynamic_slice_in_dim(jnp.concatenate([v, v], axis=2), tp, 4, 2)

    def keys_of(row):
        return arranged(row).transpose(1, 0, 2, 3).reshape(-1)

    def queries_of(row):
        v = lax.dynamic_index_in_dim(arranged(row), block, 0, keepdims=False)
        return jnp.where(core == 0, v, v[::-1]).reshape(-1)

    places = jnp.arange(seg_row.shape[0], dtype=jnp.int32)
    k_pos, k_seg = keys_of(places), keys_of(seg_row)
    q_pos, q_seg = queries_of(places), queries_of(seg_row)
    seen = (k_pos[:, None] <= q_pos[None, :]) & (k_seg[:, None] == q_seg[None, :])
    bias = jnp.where(seen, 0.0, MASKED).astype(F32)

    frequency = 10000.0 ** (-jnp.arange(0, HD, 2, dtype=F32) / HD)
    angles = q_pos.astype(F32)[:, None] * frequency[None, :]
    wide = q_width + 2 * HD
    plain = lax.broadcasted_iota(jnp.int32, (group, wide), 1) >= q_width + HD
    cos, sin = (jnp.concatenate([t] * 12, axis=1) for t in (jnp.cos(angles), jnp.sin(angles)))
    cos, sin = jnp.where(plain, 1.0, cos), jnp.where(plain, 0.0, sin)

    rows_low, rows_f32 = shape((micro_rows, d)), shape((micro_rows, d), F32)
    all_low = shape((group, d))
    partials = [shape((group // 2, d)), shape((group // 2, d), F32)]
    heads, keys = q_width // HD, seg_row.shape[0]
    gain_row = shape((1, d), F32)

    def project(x, qkv_w):
        return call(
            functools.partial(qkv_kernel, parts=len(qkv_w)),
            [all_low, all_low, shape((group, q_width)), shape((group // 2, 2 * HD))]
            + [shape((d, wide)), shape((d, q_width)), gain_row, gain_row],
            [place, gather_rows(x) + qkv_w, cos, sin],
            [
                pltpu.VMEM((8, GAIN_ROWS, d // 8), BF16),
                DMA((8,)),
                DMA((8, 3)),
            ],
            room=14,
        )

    both_kv = shape((keys // 2, 2 * HD))

    def attention(q, kv, w_out):
        return call(
            attend_kernel,
            [shape((group, q_width)), shape((heads, group), F32), both_kv, both_kv, *partials],
            [place, q, *kv, bias, [w_out]],
            [
                pltpu.VMEM((heads, keys, group), F32),
                pltpu.VMEM((d, q_width), BF16),
                DMA,
            ],
            room=12,
        )

    def feed_forward(b, w_ffn):
        return call(
            ffn_kernel,
            [all_low, shape((group, 2 * units), F32), shape((group, padded)), *partials],
            [[*gather_rows(b), w_ffn]],
            [
                pltpu.VMEM((d, 2 * units), BF16),
                pltpu.VMEM((d, padded), BF16),
                DMA((8,)),
                DMA((4,)),
                DMA,
            ],
            room=12,
        )

    def backward(dy, kept, early=()):
        x, rows, qkv_w, a, q, k, v, ctx, lse, mid, b, gu, hidden, gain_a, gain_f, w_ffn, w_out = kept
        dff, dgu, send, mine = call(
            ffn_back_kernel,
            [all_low, shape((group, 2 * units)), *partials],
            [[*gather_rows(dy), w_ffn, gu]],
            [
                pltpu.VMEM((d, 2 * units), BF16),
                pltpu.VMEM((d, padded), BF16),
                pltpu.VMEM((group, 2 * units), F32),
                DMA((8,)),
                DMA((3,)),
            ],
            room=12,
        )
        g_ffn = ffn_products(b, dgu, dff, hidden)
        dmid, dattn, gg_f = call(
            norm_back_kernel,
            [rows_f32, rows_low, gain_row],
            [*reduce_rows(send, mine), dy, mid, gain_f],
        )
        dattn = after(dattn, g_ffn, *early)
        dattn, dq, dkv, dkv_send = call(
            attend_back_kernel,
            [all_low, shape((group, q_width)), shape((keys // 2, 2 * HD), F32), both_kv],
            [place, gather_rows(dattn) + [w_out], q, k, v, bias, ctx, lse, cos, sin],
            [
                pltpu.VMEM((d, q_width), BF16),
                pltpu.VMEM((group, q_width), BF16),
                pltpu.VMEM((keys // 2, 2 * HD), F32),
                pltpu.VMEM((keys // 2, 2 * HD), F32),
                DMA,
                DMA((8,)),
            ],
            room=18,
        )
        dkv = call(kv_add_kernel, [both_kv], [dkv, swap_core(dkv_send)])[0]
        arrived = lax.all_to_all(
            dkv.reshape(8, group // 2, 2 * HD), ("x", "ylo"), 0, 0, tiled=True
        )
        dqkv, send, mine, gg_a = call(
            qkv_back_kernel,
            [shape((group, wide)), *partials, gain_row],
            [place, [qkv_w, rows], dq, arrived, cos, sin],
            [pltpu.VMEM((d, wide), BF16), pltpu.VMEM((group, d), BF16), DMA((2,))],
            room=16,
        )
        g_attn = attn_products(dattn, ctx, a, dqkv, gg_a, gg_f)
        dx, dx_low, _ = call(
            norm_back_kernel,
            [rows_f32, rows_low, gain_row],
            [*reduce_rows(send, mine), dmid, x, gain_a],
        )
        return dx, after(dx_low, g_attn), g_attn, g_ffn

    x0 = lax.dynamic_index_in_dim(block_input, section, 0, keepdims=False)
    dy1 = lax.dynamic_index_in_dim(out_grad, section, 0, keepdims=False)

    rows0, a0, q0, kv0, w_qkv0, w_out0, ga0, gf0 = project(x0, attn0)
    ffn_pairs = pairs(place, ffn_shard, [after(v, a0) for v in ffn_y])
    w_ffn0 = gather_x(ffn_pairs[0])
    kv0 = gather_kv(kv0)
    ctx0, lse0, k0, v0, send, mine = attention(q0, kv0, w_out0)
    attn1 = gather_x(after(attn_pairs[1], ctx0))
    mid0, b = call(add_norm_kernel, [rows_f32, rows_low], [*reduce_rows(send, mine), x0, gf0])
    w_ffn1 = gather_x(after(ffn_pairs[1], b))
    b0, up0, hidden0, send, mine = feed_forward(b, w_ffn0)
    y0 = call(add_kernel, [rows_low], [*reduce_rows(send, mine), mid0])[0]
    kept0 = (x0, rows0, w_qkv0, a0, q0, k0, v0, ctx0, lse0, mid0, b0, up0, hidden0, ga0, gf0, w_ffn0, w_out0)
    rows1, a1, q1, kv1, w_qkv1, w_out1, ga1, gf1 = project(y0, [attn1])
    ctx1, lse1, k1, v1, send, mine = attention(q1, gather_kv(kv1), w_out1)
    mid1, b = call(add_norm_kernel, [rows_f32, rows_low], [*reduce_rows(send, mine), y0, gf1])
    b1, up1, hidden1, send, mine = feed_forward(b, w_ffn1)
    y1 = call(add_kernel, [rows_low], [*reduce_rows(send, mine), mid1])[0]
    kept1 = (y0, rows1, w_qkv1, a1, q1, k1, v1, ctx1, lse1, mid1, b1, up1, hidden1, ga1, gf1, w_ffn1, w_out1)

    dx1, dx1_low, g_attn1, g_ffn1 = backward(dy1, kept1)
    ffn1, r_attn1 = reduce_x(g_ffn1), reduce_x(g_attn1)
    dx0, dx0_low, g_attn0, g_ffn0 = backward(dx1_low, kept0, [ffn1])
    ffn_y = reduce_y(reduce_x(g_ffn0), ffn1, place)
    dx0 = after(dx0, r_attn1, *ffn_y)
    early = section == 0

    ffn_parts = by_core(ffn_y, place)
    attn_parts = by_core(reduce_y(reduce_x(g_attn0), r_attn1, place), place)

    def finish(kernel, dims, parts):
        return call(kernel, [shape(s, F32) for s in dims], [place, *parts], room=12)

    own = own_rows
    grad_out, grad_query, grad_key, grad_value, *gain_pieces, _ = finish(
        attn_grads_kernel,
        [(2 * q_width, own), (own, 2 * q_width), (own, HD), (own, HD)]
        + [(micro_rows, 128)] * 4
        + [(own, 128)],
        attn_parts,
    )
    grad_gate, grad_up, grad_down = finish(
        ffn_grads_kernel, [(own, 2 * units)] * 2 + [(2 * units, own)], ffn_parts
    )
    gain_sums = gain_pieces[0]
    for k in (1, 2, 3):
        gain_sums = gain_sums + from_z(gain_pieces[k], -k)
    gain_sums = gain_sums[:, :2].T

    def both_micros(layer0, layer1, dtype):
        mine = jnp.where(early, layer0, layer1).astype(dtype)
        other = jnp.where(early, layer1, layer0).astype(BF16)
        other = swap_section(other).astype(dtype)
        return jnp.stack([jnp.where(early, mine, other), jnp.where(early, other, mine)])[None]

    block_output = both_micros(y0, y1, BF16)
    input_grad = both_micros(dx0, dx1, F32)

    return (
        block_output,
        input_grad,
        gain_sums[0][None],
        grad_query[None],
        grad_key[None],
        grad_value[None],
        grad_out[None],
        gain_sums[1][None],
        grad_gate[None],
        grad_up[None],
        grad_down[None],
    )


def solution(mesh):
    fine = Mesh(mesh.devices.reshape(2, 4, 2, 2, 4), AXES)
    wide = ("x", "ylo", "core")
    rows = P(None, (*wide, "tp"), None)
    into = P("section", wide, "tp")
    out_of = P("section", "tp", wide)
    grown = P("section", None, (*wide, "tp"), None)
    gain_grad = P("section", (*wide, "tp"))
    return jax.shard_map(
        body,
        mesh=fine,
        in_specs=(
            rows, rows, P(), P("section", wide), into, into, into, out_of,
            P("section", wide), into, into, out_of,
        ),
        out_specs=(
            grown, grown, gain_grad, into, into, into, out_of, gain_grad, into, into, out_of,
        ),
        check_vma=False,
    )
```

```python
import functools
import math

import jax
import jax.numpy as jnp
from jax import lax
from jax.experimental import pallas as pl
from jax.experimental.pallas import tpu as pltpu
from jax.sharding import Mesh, PartitionSpec as P

HD = 64
GAIN_ROWS = 16
EPS = 1e-05
MASKED = -1e30
KEYS_STEP = 512
AXES = ("section", "x", "ylo", "core", "tp")
SECTION, _, YLO, CORE, TP = range(5)
BF16 = jnp.bfloat16
F32 = jnp.float32
VMEM = pl.BlockSpec(memory_space=pltpu.VMEM)
SMEM = pl.BlockSpec(memory_space=pltpu.SMEM)
HBM = pl.BlockSpec(memory_space=pltpu.HBM)
DMA = pltpu.SemaphoreType.DMA


def nn(a, b):
    return jnp.dot(a, b, preferred_element_type=F32)


def nt(a, b):
    return lax.dot_general(a, b, (((1,), (1,)), ((), ())), preferred_element_type=F32)


def tn(a, b):
    return lax.dot_general(a, b, (((0,), (0,)), ((), ())), preferred_element_type=F32)


def shape(dims, dtype=BF16):
    return jax.ShapeDtypeStruct(tuple(dims), dtype)


SHORT = pl.CostEstimate(flops=1, bytes_accessed=1, transcendentals=0)


def held(dims, dtype=BF16):
    return pltpu.HBM(tuple(dims), dtype)


def pinned(v):
    return pltpu.with_memory_space_constraint(v, pltpu.HBM)


def call(kernel, outs, args, scratch=(), room=8, out_spec=None):
    specs, values = [], []
    for a in args:
        if isinstance(a, (list, tuple)):
            specs += [HBM if isinstance(a, list) else pl.BlockSpec()] * len(a)
            values += [pinned(v) for v in a]
        else:
            specs.append(SMEM if a.dtype == jnp.int32 else VMEM)
            values.append(a)
    mine = [m for m in scratch if isinstance(m, type(pltpu.VMEM((8, 128), F32)))]
    room = room * 2**20 + sum(
        math.prod(m.shape) * jnp.dtype(m.dtype).itemsize for m in mine if m.dtype in (BF16, F32)
    )
    return pl.pallas_call(
        kernel,
        out_shape=tuple(outs),
        in_specs=specs,
        out_specs=tuple(
            VMEM if isinstance(o, jax.ShapeDtypeStruct) else out_spec or pl.BlockSpec() for o in outs
        ),
        scratch_shapes=list(scratch),
        compiler_params=pltpu.CompilerParams(vmem_limit_bytes=room),
        cost_estimate=SHORT,
        name=getattr(kernel, "func", kernel).__name__,
    )(*values)


def from_z(rows, by):
    return lax.ppermute(rows, "tp", [((i + by) % 4, i) for i in range(4)])


def swap_core(v):
    return lax.ppermute(v, "core", [(0, 1), (1, 0)])


def swap_ylo(v):
    return lax.ppermute(v, "ylo", [(0, 1), (1, 0)])


def swap_section(v):
    return lax.ppermute(v, "section", [(0, 1), (1, 0)])


def swap_across(v):
    return lax.ppermute(v, ("section", "ylo"), [(0, 3), (3, 0), (1, 2), (2, 1)])


def after(value, *others):
    return lax.optimization_barrier((value, *others))[0]


def y_exchange(v):
    return swap_ylo(v), swap_across(v), swap_section(v)


def gather_rows(rows):
    pieces = [rows] + [from_z(rows, k) for k in (1, 2, 3)]
    return pieces + [swap_core(p) for p in pieces]


def gather_kv(half):
    copies = jnp.broadcast_to(half[None], (8, *half.shape))
    own = lax.all_to_all(copies, ("x", "ylo"), 0, 0, tiled=True).reshape(-1, half.shape[1])
    return own, swap_core(own)


def reduce_rows(send, mine):
    own, *pieces = split(mine, swap_core(send))
    return [own] + [from_z(p, -k) for k, p in zip((1, 2, 3), pieces)]


def summands(send, mine):
    own, *others = reduce_rows(send, mine)
    return [(own,), *others]


def gather_x(block):
    return lax.all_gather(block, "x", axis=0, tiled=True)


def reduce_x(grad):
    return lax.psum_scatter(grad, "x", scatter_dimension=0, tiled=True)


def pack_attn_kernel(place, q_ref, k_ref, v_ref, o_ref, ga_ref, gf_ref, own_ref, send_ref):
    n, rows = q_ref.shape[1] // 2, q_ref.shape[0]
    m = n + 2 * HD
    kv = jnp.concatenate([k_ref[...], v_ref[...]], axis=1)
    o = o_ref[...].T
    odd = place[CORE] == 1
    row = lax.broadcasted_iota(jnp.int32, (GAIN_ROWS, ga_ref.shape[1]), 0)
    ga, gf = (jnp.broadcast_to(g[...].astype(F32), row.shape) for g in (ga_ref, gf_ref))
    gains = jnp.where(row == 0, ga, jnp.where(row == 1, gf, 0.0)).astype(BF16)
    rest = jnp.zeros((GAIN_ROWS, own_ref.shape[1] - gains.shape[1]), BF16)
    for ref, high in ((own_ref, odd), (send_ref, jnp.logical_not(odd))):
        ref[:rows, :n] = jnp.where(high, q_ref[:, n:], q_ref[:, :n])
        ref[:rows, n:m] = kv
        ref[:rows, m:] = jnp.where(high, o[:, n:], o[:, :n])
        ref[rows:, :] = jnp.concatenate([gains, rest], axis=1)


def pack_ffn_kernel(place, d_ref, g_ref, u_ref, own_ref, send_ref):
    odd = place[CORE] == 1
    d = d_ref[...].T
    n = d.shape[1] // 2
    spare = jnp.zeros((own_ref.shape[0], own_ref.shape[1] - 3 * n), BF16)
    low, high = (
        jnp.concatenate([w[:, at] for w in (g_ref[...], u_ref[...], d)] + [spare], axis=1)
        for at in (slice(0, n), slice(n, 2 * n))
    )
    own_ref[...] = jnp.where(odd, high, low)
    send_ref[...] = jnp.where(odd, low, high)


def chip_rows_kernel(place, own_ref, other_ref, out_ref):
    n = own_ref.shape[0]
    core = place[CORE]
    out_ref[pl.ds(pl.multiple_of(core * n, n), n), :] = own_ref[...]
    out_ref[pl.ds(pl.multiple_of((1 - core) * n, n), n), :] = other_ref[...]


def chip_rows(place, own, other):
    n, c = own.shape
    return call(chip_rows_kernel, [held((2 * n, c))], [place, (own, other)], room=12)[0]


def chip_attn_kernel(place, own_ref, other_ref, out_ref):
    n = own_ref.shape[0] - GAIN_ROWS
    core = place[CORE]
    odd = core == 1
    out_ref[pl.ds(pl.multiple_of(core * n, n), n), :] = own_ref[:n, :]
    out_ref[pl.ds(pl.multiple_of((1 - core) * n, n), n), :] = other_ref[:n, :]
    own, other = own_ref[n:, :n], other_ref[n:, :n]
    rest = jnp.zeros((GAIN_ROWS, out_ref.shape[1] - 2 * n), BF16)
    out_ref[2 * n :, :] = jnp.concatenate(
        [jnp.where(odd, other, own), jnp.where(odd, own, other), rest], axis=1
    )


def pairs_kernel(place, own_ref, near_ref, far_ref, straight_ref, p0_ref, p1_ref):
    n = own_ref.shape[0]
    here = pl.ds(pl.multiple_of(place[YLO] * n, n), n)
    there = pl.ds(pl.multiple_of((1 - place[YLO]) * n, n), n)

    def fill(mine, other):
        mine[here, :] = own_ref[...]
        mine[there, :] = near_ref[...]
        other[here, :] = straight_ref[...]
        other[there, :] = far_ref[...]

    @pl.when(place[SECTION] == 0)
    def _():
        fill(p0_ref, p1_ref)

    @pl.when(place[SECTION] == 1)
    def _():
        fill(p1_ref, p0_ref)


def both_pairs_kernel(place, own_ref, near_ref, far_ref, straight_ref, out_ref):
    n = own_ref.shape[0]
    mine, other, here = 2 * place[SECTION], 2 - 2 * place[SECTION], place[YLO]
    for src, at in (
        (own_ref, mine + here),
        (near_ref, mine + 1 - here),
        (straight_ref, other + here),
        (far_ref, other + 1 - here),
    ):
        out_ref[pl.ds(pl.multiple_of(at * n, n), n), :] = src[...]


def both_pairs(place, own, others):
    n, c = own.shape
    return call(both_pairs_kernel, [held((4 * n, c))], [place, (own, *others)], room=16)[0]


def pairs(place, own, others):
    n, c = own.shape
    out = held((2 * n, c))
    return call(pairs_kernel, [out, out], [place, (own, *others)], room=20)


def fetch(pieces, whole, sems):
    n = pieces[0].shape[0]
    copies = [
        pltpu.make_async_copy(p, whole.at[pl.ds(i * n, n), :], sems.at[i])
        for i, p in enumerate(pieces)
    ]
    for c in copies:
        c.start()

    def wait():
        for c in copies:
            c.wait()

    return wait


def block_row(pack, layer, i):
    return (i // 2 * 4 + 2 * layer + i % 2) * (pack.shape[0] // 16)


def fetch_blocks(pack, layer, column, whole, sems):
    n, c = whole.shape[0] // 8, whole.shape[1]
    copies = [
        pltpu.make_async_copy(
            pack.at[pl.ds(block_row(pack, layer, i), n), pl.ds(column, c)],
            whole.at[pl.ds(i * n, n), :],
            sems.at[i],
        )
        for i in range(8)
    ]
    for c in copies:
        c.start()

    def wait():
        for c in copies:
            c.wait()

    return wait


def rms(rows):
    return lax.rsqrt(jnp.mean(rows * rows, axis=-1, keepdims=True) + EPS)


def turned(v, by):
    return pltpu.roll(v, by % v.shape[1], 1)


def low_half(v):
    return lax.broadcasted_iota(jnp.int32, v.shape, 1) % HD < HD // 2


def rope(v, cos, sin):
    half = HD // 2
    return v * cos + jnp.where(low_half(v), -turned(v, -half), turned(v, half)) * sin


def rope_back(u, cos, sin):
    half, w = HD // 2, u * sin
    return u * cos + jnp.where(low_half(w), turned(w, -half), -turned(w, half))


def halves_out(partial, send_ref, mine_ref):
    n = send_ref.shape[0]
    send_ref[...] = partial[n:].astype(BF16)
    mine_ref[...] = partial[:n]


def split_kernel(mine_ref, other_ref, own_ref, *piece_refs):
    n = own_ref.shape[0]
    own_ref[...] = mine_ref[:n, :] + other_ref[:n, :].astype(F32)
    for k, ref in enumerate(piece_refs, 1):
        at = slice(k * n, (k + 1) * n)
        ref[...] = (mine_ref[at, :] + other_ref[at, :].astype(F32)).astype(BF16)


def split(mine, other):
    n, d = mine.shape[0] // 4, mine.shape[1]
    return call(split_kernel, [held((n, d), F32)] + [shape((n, d))] * 3, [(mine,), other])


def total_of(refs):
    return sum((r[...].astype(F32) for r in refs[1:]), refs[0][...])


def add_norm_kernel(a, b, c, d, x_ref, gain_ref, mid_ref, low_ref):
    mid = x_ref[...].astype(F32) + total_of((a, b, c, d))
    mid_ref[...] = mid
    low_ref[...] = (mid * rms(mid) * gain_ref[...]).astype(BF16)


def add_kernel(a, b, c, d, mid_ref, y_ref):
    y_ref[...] = (mid_ref[...] + total_of((a, b, c, d))).astype(BF16)


def norm_back_kernel(a, b, c, d, after_ref, x_ref, gain_ref, dx_ref, low_ref, gain_grad_ref):
    grad = total_of((a, b, c, d))
    x = x_ref[...].astype(F32)
    r = rms(x)
    n = x * r
    gain_grad_ref[...] = jnp.sum(grad * n, axis=0, keepdims=True)
    scaled = grad * gain_ref[...]
    dx = after_ref[...].astype(F32) + r * (
        scaled - n * jnp.mean(scaled * n, axis=-1, keepdims=True)
    )
    dx_ref[...] = dx
    low_ref[...] = dx.astype(BF16)


def qkv_kernel(place, *refs, layer):
    pieces, pack, refs = refs[:8], refs[8], refs[9:]
    cos_ref, sin_ref, x_ref, a_ref, q_ref, kv_ref, ga_ref, gf_ref, *refs = refs
    w_ref, gains_ref, x_sems, w_sems, g_sems = refs
    rows_there = fetch(pieces, x_ref, x_sems)
    n = w_ref.shape[0] // 8
    gain_copies = [
        pltpu.make_async_copy(
            pack.at[pl.ds(block_row(pack, layer, i) + n, GAIN_ROWS), pl.ds(0, n)],
            gains_ref.at[i],
            g_sems.at[i],
        )
        for i in range(8)
    ]
    for c in gain_copies:
        c.start()
    weights_there = fetch_blocks(pack, layer, 0, w_ref, w_sems)
    for c in gain_copies:
        c.wait()
    gains = jnp.concatenate([gains_ref[i] for i in range(8)], axis=1).astype(F32)
    ga_ref[...] = gains[0:1, :]
    gf_ref[...] = gains[1:2, :]
    rows_there()
    x = x_ref[...].astype(F32)
    a = (x * rms(x) * ga_ref[...]).astype(BF16)
    a_ref[...] = a
    weights_there()
    out = rope(nn(a, w_ref[...]), cos_ref[...], sin_ref[...])
    width = q_ref.shape[1]
    q_ref[...] = (out[:, :width].astype(BF16).astype(F32) * HD**-0.5).astype(BF16)
    half = out.shape[0] // 2
    k, v = out[:, width : width + HD], out[:, width + HD :]
    keys = jnp.concatenate([k[:half], k[half:]], axis=1)
    values = jnp.concatenate([v[half:], v[:half]], axis=1)
    kv_ref[...] = jnp.where(place[CORE] == 1, values, keys).astype(BF16)


def key_step(ref, t):
    per = ref.shape[0] // KEYS_STEP
    return pl.ds(t % per * KEYS_STEP, KEYS_STEP), slice(t // per * HD, (t // per + 1) * HD)


def attend_kernel(place, q_ref, own_ref, other_ref, bias_ref, pack, *refs, layer):
    o_ref, lse_ref, k_ref, v_ref, send_ref, mine_ref, s_ref, w_ref, sems = refs
    weights_there = fetch_blocks(pack, layer, pack.shape[1] - w_ref.shape[1], w_ref, sems)
    odd = place[CORE] == 1
    k_ref[...] = jnp.where(odd, other_ref[...], own_ref[...])
    v_ref[...] = jnp.where(odd, own_ref[...], other_ref[...])
    rows, width = q_ref.shape
    heads = width // HD
    steps = 2 * k_ref.shape[0] // KEYS_STEP
    tops = [jnp.full((1, rows), MASKED, F32) for _ in range(heads)]
    for t in range(steps):
        at = pl.ds(t * KEYS_STEP, KEYS_STEP)
        part, cols = key_step(k_ref, t)
        k = k_ref[part, cols]
        bias = bias_ref[at, :]
        for h in range(heads):
            s = nt(k, q_ref[:, h * HD : (h + 1) * HD]) + bias
            s_ref[h, at, :] = s
            tops[h] = jnp.maximum(tops[h], jnp.max(s, axis=0, keepdims=True))
    sums = [jnp.zeros((1, rows), F32) for _ in range(heads)]
    outs = [jnp.zeros((HD, rows), F32) for _ in range(heads)]
    for t in range(steps):
        at = pl.ds(t * KEYS_STEP, KEYS_STEP)
        part, cols = key_step(v_ref, t)
        v_t = v_ref[part, :].T[cols, :]
        for h in range(heads):
            e = jnp.exp(s_ref[h, at, :] - tops[h])
            sums[h] = sums[h] + jnp.sum(e, axis=0, keepdims=True)
            outs[h] = outs[h] + nn(v_t, e.astype(BF16))
    flat = jnp.concatenate([outs[h] / sums[h] for h in range(heads)], axis=0)
    o_ref[...] = flat.T.astype(BF16)
    lse_ref[...] = jnp.concatenate([tops[h] + jnp.log(sums[h]) for h in range(heads)], axis=0)
    weights_there()
    halves_out(nt(o_ref[...], w_ref[...]), send_ref, mine_ref)


def ffn_kernel(*refs):
    pieces, w_hbm, refs = refs[:8], refs[8], refs[9:]
    b_ref, gu_ref, h_ref, send_ref, mine_ref, gu_w, down_w, b_sems, gu_sems, sem = refs
    rows_there = fetch(pieces, b_ref, b_sems)
    steps, n, c = 4, w_hbm.shape[0] // 4, gu_w.shape[1]

    def load(i):
        at = pl.ds(i * n, n)
        return pltpu.make_async_copy(w_hbm.at[at, pl.ds(0, c)], gu_w.at[at, :], gu_sems.at[i])

    for i in range(steps):
        load(i).start()
    down = pltpu.make_async_copy(w_hbm.at[:, pl.ds(c, down_w.shape[1])], down_w, sem)
    down.start()
    rows_there()
    for i in range(steps):
        load(i).wait()
        at = slice(i * n, (i + 1) * n)
        part = nn(b_ref[:, at], gu_w[at, :])
        gu_ref[...] = part if i == 0 else gu_ref[...] + part
    units = gu_ref.shape[1] // 2
    gate, up = gu_ref[:, :units], gu_ref[:, units:]
    h_ref[:, :units] = (gate / (1.0 + jnp.exp(-gate)) * up).astype(BF16)
    spare = h_ref.shape[1] - units
    h_ref[:, units:] = jnp.zeros((h_ref.shape[0], spare), BF16)
    down.wait()
    halves_out(nt(h_ref[...], down_w[...]), send_ref, mine_ref)


def ffn_back_kernel(*refs):
    pieces, w_hbm, act_hbm, refs = refs[:8], refs[8], refs[9], refs[10:]
    dff_ref, dgu_ref, send_ref, mine_ref, gu_w, down_w, gu_ref, r_sems, gu_sems = refs
    rows_there = fetch(pieces, dff_ref, r_sems)
    c = gu_w.shape[1]
    down = pltpu.make_async_copy(w_hbm.at[:, pl.ds(c, down_w.shape[1])], down_w, gu_sems.at[2])
    down.start()
    act = pltpu.make_async_copy(act_hbm, gu_ref, gu_sems.at[0])
    act.start()
    load = pltpu.make_async_copy(w_hbm.at[:, pl.ds(0, c)], gu_w, gu_sems.at[1])
    load.start()
    rows_there()
    down.wait()
    units = gu_ref.shape[1] // 2
    dh = nn(dff_ref[...], down_w[...])[:, :units]
    act.wait()
    gate, up = gu_ref[:, :units], gu_ref[:, units:]
    sig = 1.0 / (1.0 + jnp.exp(-gate))
    dgate = dh * up * (sig * (1.0 + gate * (1.0 - sig)))
    dgu_ref[...] = jnp.concatenate([dgate, dh * (gate * sig)], axis=1).astype(BF16)
    load.wait()
    halves_out(nt(dgu_ref[...], gu_w[...]), send_ref, mine_ref)


def attend_back_kernel(place, *refs, layer):
    pieces, refs = refs[:8], refs[8:]
    pack, q_ref, k_ref, v_ref, bias_ref, o_ref, lse_ref, cos_ref, sin_ref, *refs = refs
    dattn_ref, dq_ref, own_ref, send_ref, w_ref, do_ref, dk_ref, dv_ref, sems, r_sems = refs
    rows_there = fetch(pieces, dattn_ref, r_sems)
    weights_there = fetch_blocks(pack, layer, pack.shape[1] - w_ref.shape[1], w_ref, sems)
    rows, width = q_ref.shape
    heads = width // HD
    steps = 2 * k_ref.shape[0] // KEYS_STEP
    rows_there()
    weights_there()
    do = nn(dattn_ref[...], w_ref[...])
    do_ref[...] = do.astype(BF16)
    both = (do_ref[...].astype(F32) * o_ref[...].astype(F32)).T
    deltas = [
        jnp.sum(both[h * HD : (h + 1) * HD, :], axis=0, keepdims=True) for h in range(heads)
    ]
    dq_t = [jnp.zeros((HD, rows), F32) for _ in range(heads)]
    for t in range(steps):
        at = pl.ds(t * KEYS_STEP, KEYS_STEP)
        part, cols = key_step(k_ref, t)
        k = k_ref[part, cols]
        v = v_ref[part, cols]
        k_t = k_ref[part, :].T[cols, :]
        bias = bias_ref[at, :]
        dk = jnp.zeros((KEYS_STEP, HD), F32)
        dv = jnp.zeros((KEYS_STEP, HD), F32)
        for h in range(heads):
            q_h = q_ref[:, h * HD : (h + 1) * HD]
            do_h = do_ref[:, h * HD : (h + 1) * HD]
            p = jnp.exp(nt(k, q_h) + bias - lse_ref[h : h + 1, :])
            ds = (p * (nt(v, do_h) - deltas[h])).astype(BF16)
            dv = dv + nn(p.astype(BF16), do_h)
            dk = dk + nn(ds, q_h)
            dq_t[h] = dq_t[h] + nn(k_t, ds)
        dk_ref[part, cols] = dk
        dv_ref[part, cols] = dv
    dq = jnp.concatenate(dq_t, axis=0).T * HD**-0.5
    dq_ref[...] = rope_back(dq, cos_ref[:, :width], sin_ref[:, :width]).astype(BF16)
    odd = place[CORE] == 1
    own_ref[...] = jnp.where(odd, dv_ref[...], dk_ref[...])
    send_ref[...] = jnp.where(odd, dk_ref[...], dv_ref[...]).astype(BF16)


def kv_add_kernel(own_ref, other_ref, out_ref):
    out_ref[...] = (own_ref[...] + other_ref[...].astype(F32)).astype(BF16)


def qkv_back_kernel(place, pack, x_hbm, dq_ref, kv_ref, cos_ref, sin_ref, *refs, layer):
    dqkv_ref, send_ref, mine_ref, gain_grad_ref, w_ref, x_ref, sems, x_sem = refs
    weights_there = fetch_blocks(pack, layer, 0, w_ref, sems)
    rows_there = pltpu.make_async_copy(x_hbm, x_ref, x_sem)
    rows_there.start()
    width, odd = dq_ref.shape[1], place[CORE] == 1
    both = sum((kv_ref[i].astype(F32) for i in range(1, 8)), kv_ref[0].astype(F32))
    first, second = both[:, :HD], both[:, HD:]
    dk = jnp.concatenate([first, second], axis=0)
    dv = jnp.concatenate([second, first], axis=0)
    spare = jnp.zeros_like(dk)
    dkv = jnp.where(
        odd, jnp.concatenate([spare, dv], axis=1), jnp.concatenate([dk, spare], axis=1)
    )
    dkv = rope_back(dkv, cos_ref[:, width:], sin_ref[:, width:])
    dqkv_ref[:, :width] = dq_ref[...]
    dqkv_ref[:, width:] = dkv.astype(BF16)
    weights_there()
    da = nt(dqkv_ref[...], w_ref[...])
    halves_out(da, send_ref, mine_ref)
    rows_there.wait()
    x = x_ref[...].astype(F32)
    gain_grad_ref[...] = jnp.sum(da * (x * rms(x)), axis=0, keepdims=True)


def ffn_product_kernel(b_ref, dgu_ref, dff_ref, h_ref, out, whole, sems):
    n, steps = dgu_ref.shape[1], sems.shape[0]
    rows = whole.shape[0] // steps
    copies = []
    for i in range(steps):
        at = slice(i * rows, (i + 1) * rows)
        whole[at, :n] = tn(b_ref[:, at], dgu_ref[...]).astype(BF16)
        whole[at, n:] = tn(dff_ref[:, at], h_ref[...]).astype(BF16)
        here = pl.ds(i * rows, rows)
        copies.append(pltpu.make_async_copy(whole.at[here, :], out.at[here, :], sems.at[i]))
        copies[-1].start()
    for c in copies:
        c.wait()


def ffn_products(b, dgu, dff, hidden):
    dims = (b.shape[1], dgu.shape[1] + hidden.shape[1])
    return call(
        ffn_product_kernel,
        [pltpu.HBM(dims, BF16)],
        [(b, dgu, dff, hidden)],
        [pltpu.VMEM(dims, BF16), DMA((8,))],
        room=14,
        out_spec=HBM,
    )[0]


def attn_product_kernel(dattn, a, gg_a, gg_f, ctx, dqkv, out, whole, sems):
    m, steps = ctx.shape[1], sems.shape[0]
    wide = m + dqkv.shape[1]
    rows = whole.shape[0] // steps
    row = lax.broadcasted_iota(jnp.int32, (whole.shape[1] - wide, rows), 0)
    copies = []
    for i in range(steps):
        at = slice(i * rows, (i + 1) * rows)
        whole[at, :m] = tn(dattn[:, at], ctx[...]).astype(BF16)
        whole[at, m:wide] = tn(a[:, at], dqkv[...]).astype(BF16)
        ga, gf = (jnp.broadcast_to(g[:, at], row.shape) for g in (gg_a, gg_f))
        gains = jnp.where(row == 0, ga, jnp.where(row == 1, gf, 0.0))
        whole[at, wide:] = gains.T.astype(BF16)
        here = pl.ds(i * rows, rows)
        copies.append(pltpu.make_async_copy(whole.at[here, :], out.at[here, :], sems.at[i]))
        copies[-1].start()
    for c in copies:
        c.wait()


def attn_products(dattn, ctx, a, dqkv, gg_a, gg_f):
    dims = (a.shape[1], ctx.shape[1] + dqkv.shape[1] + 128)
    return call(
        attn_product_kernel,
        [pltpu.HBM(dims, BF16)],
        [(dattn, a, gg_a, gg_f, ctx, dqkv)],
        [pltpu.VMEM(dims, BF16), DMA((4,))],
        room=14,
        out_spec=HBM,
    )[0]


def y_split_kernel(place, r0_ref, r1_ref, keep_ref, near_ref, far_ref, straight_ref):
    n = keep_ref.shape[0]
    here = pl.ds(pl.multiple_of(place[YLO] * n, n), n)
    there = pl.ds(pl.multiple_of((1 - place[YLO]) * n, n), n)

    def fill(mine, other):
        keep_ref[...] = mine[here, :]
        near_ref[...] = mine[there, :]
        straight_ref[...] = other[here, :]
        far_ref[...] = other[there, :]

    @pl.when(place[SECTION] == 0)
    def _():
        fill(r0_ref, r1_ref)

    @pl.when(place[SECTION] == 1)
    def _():
        fill(r1_ref, r0_ref)


def by_core_kernel(place, *refs):
    *parts, own_ref, send_ref = refs
    n = own_ref.shape[0]
    here = pl.ds(pl.multiple_of(place[CORE] * n, n), n)
    there = pl.ds(pl.multiple_of((1 - place[CORE]) * n, n), n)
    own_ref[...] = sum(p[here, :].astype(F32) for p in parts)
    send_ref[...] = sum(p[there, :].astype(F32) for p in parts).astype(BF16)


def by_core(parts, place):
    n, c = parts[0].shape[0] // 2, parts[0].shape[1]
    own, send = call(
        by_core_kernel, [held((n, c), F32), shape((n, c))], [place, tuple(parts)], room=16
    )
    return own, swap_core(send)


def reduce_y(r0, r1, place):
    n, c = r0.shape[0] // 2, r0.shape[1]
    keep, near, far, straight = call(y_split_kernel, [held((n, c))] * 4, [place, (r0, r1)], room=16)
    return [keep, swap_ylo(near), swap_across(far), swap_section(straight)]


def ordered(odd, own, other):
    other = other.astype(F32)
    return jnp.concatenate(
        [jnp.where(odd, other, own), jnp.where(odd, own, other)], axis=1
    )


def attn_grads_kernel(place, own_ref, other_ref, o_ref, q_ref, k_ref, v_ref, *gain_refs):
    odd = place[CORE] == 1
    m = n = q_ref.shape[1] // 2
    own, other = own_ref[:, :m].T, other_ref[:, :m].astype(F32).T
    o_ref[:m, :] = jnp.where(odd, other, own)
    o_ref[m:, :] = jnp.where(odd, own, other)
    q_ref[...] = ordered(odd, own_ref[:, m : m + n], other_ref[:, m : m + n])
    both = own_ref[:, m + n :] + other_ref[:, m + n :].astype(F32)
    k_ref[...] = both[:, :HD]
    v_ref[...] = both[:, HD : 2 * HD]
    rows = gain_refs[0].shape[0]
    gain_refs[-1][...] = both[:, 2 * HD :]
    for k, ref in enumerate(gain_refs[:-1]):
        at = lax.rem(place[TP] + k, 4) * rows
        ref[...] = gain_refs[-1][pl.ds(pl.multiple_of(at, rows), rows), :]


def ffn_grads_kernel(place, own_ref, other_ref, gate_ref, up_ref, down_ref):
    odd = place[CORE] == 1
    n = gate_ref.shape[1] // 2
    gate_ref[...] = ordered(odd, own_ref[:, :n], other_ref[:, :n])
    up_ref[...] = ordered(odd, own_ref[:, n : 2 * n], other_ref[:, n : 2 * n])
    own, other = own_ref[:, 2 * n :].T[:n], other_ref[:, 2 * n :].astype(F32).T[:n]
    down_ref[:n, :] = jnp.where(odd, other, own)
    down_ref[n:, :] = jnp.where(odd, own, other)


def body(
    block_input,
    out_grad,
    seg_ids,
    attn_gain,
    w_query,
    w_key,
    w_value,
    w_out,
    ffn_gain,
    w_gate,
    w_up,
    w_down,
):
    at = {name: lax.axis_index(name) for name in AXES}
    section, core, tp = at["section"], at["core"], at["tp"]
    place = jnp.stack([at[name] for name in AXES]).astype(jnp.int32)
    d = block_input.shape[2]
    micro_rows = block_input.shape[1]
    group = 8 * micro_rows
    q_width = w_query.shape[2] // 2
    units = w_gate.shape[2] // 2
    own_rows = w_query.shape[1]

    padded = units + (-units) % 128
    attn_dims = (own_rows + GAIN_ROWS, 2 * q_width + 2 * HD)
    attn_own, attn_send = call(
        pack_attn_kernel,
        [shape(attn_dims)] * 2,
        [place, (w_query[0], w_key[0], w_value[0], w_out[0], attn_gain, ffn_gain)],
    )
    attn_shard = call(
        chip_attn_kernel,
        [held((2 * own_rows + GAIN_ROWS, attn_dims[1]))],
        [place, (attn_own, swap_core(attn_send))],
    )[0]
    ffn_own, ffn_send = call(
        pack_ffn_kernel,
        [shape((own_rows, 2 * units + padded))] * 2,
        [place, (w_down[0], w_gate[0], w_up[0])],
        room=16,
    )
    ffn_shard = chip_rows(place, ffn_own, swap_core(ffn_send))
    attn_y = y_exchange(after(attn_shard, ffn_shard))
    w_attn = gather_x(both_pairs(place, attn_shard, attn_y))
    ffn_y = y_exchange(ffn_shard)

    block = at["x"] * 2 + at["ylo"]
    seg_row = lax.dynamic_index_in_dim(seg_ids, section, 0, keepdims=False)
    def arranged(row):
        v = row.reshape(8, 2, 4, micro_rows)
        return lax.dynamic_slice_in_dim(jnp.concatenate([v, v], axis=2), tp, 4, 2)

    def keys_of(row):
        return arranged(row).transpose(1, 0, 2, 3).reshape(-1)

    def queries_of(row):
        v = lax.dynamic_index_in_dim(arranged(row), block, 0, keepdims=False)
        return jnp.where(core == 0, v, v[::-1]).reshape(-1)

    places = jnp.arange(seg_row.shape[0], dtype=jnp.int32)
    k_pos, k_seg = keys_of(places), keys_of(seg_row)
    q_pos, q_seg = queries_of(places), queries_of(seg_row)
    seen = (k_pos[:, None] <= q_pos[None, :]) & (k_seg[:, None] == q_seg[None, :])
    bias = jnp.where(seen, 0.0, MASKED).astype(F32)

    frequency = 10000.0 ** (-jnp.arange(0, HD, 2, dtype=F32) / HD)
    angles = q_pos.astype(F32)[:, None] * frequency[None, :]
    wide = q_width + 2 * HD
    plain = lax.broadcasted_iota(jnp.int32, (group, wide), 1) >= q_width + HD
    cos, sin = (jnp.concatenate([t] * 12, axis=1) for t in (jnp.cos(angles), jnp.sin(angles)))
    cos, sin = jnp.where(plain, 1.0, cos), jnp.where(plain, 0.0, sin)

    rows_low = shape((micro_rows, d))
    mid_outs = [held((micro_rows, d), F32), rows_low]
    partials = [shape((group // 2, d)), held((group // 2, d), F32)]
    heads, keys = q_width // HD, seg_row.shape[0]
    gain_row = shape((1, d), F32)

    def project(x, layer):
        return call(
            functools.partial(qkv_kernel, layer=layer),
            [held((group, d))] * 2
            + [shape((group, q_width)), shape((group // 2, 2 * HD))]
            + [gain_row, gain_row],
            [place, gather_rows(x) + [w_attn], cos, sin],
            [
                pltpu.VMEM((d, wide), BF16),
                pltpu.VMEM((8, GAIN_ROWS, d // 8), BF16),
                DMA((8,)),
                DMA((8,)),
                DMA((8,)),
            ],
            room=18,
        )

    both_kv = held((keys // 2, 2 * HD))

    def attention(q, kv, layer):
        return call(
            functools.partial(attend_kernel, layer=layer),
            [held((group, q_width)), held((heads, group), F32), both_kv, both_kv, *partials],
            [place, q, *kv, bias, [w_attn]],
            [
                pltpu.VMEM((heads, keys, group), F32),
                pltpu.VMEM((d, q_width), BF16),
                DMA((8,)),
            ],
            room=12,
        )

    def feed_forward(b, w_ffn):
        return call(
            ffn_kernel,
            [held((group, d)), held((group, 2 * units), F32), held((group, padded)), *partials],
            [[*gather_rows(b), w_ffn]],
            [
                pltpu.VMEM((d, 2 * units), BF16),
                pltpu.VMEM((d, padded), BF16),
                DMA((8,)),
                DMA((4,)),
                DMA,
            ],
            room=16,
        )

    def backward(dy, kept, layer, pending=None):
        x, rows, a, q, k, v, ctx, lse, mid, b, gu, hidden, gain_a, gain_f, w_ffn = kept
        other = pending and reduce_x(after(pending[0], *pending[1:], dy))
        dff, dgu, send, mine = call(
            ffn_back_kernel,
            [held((group, d)), held((group, 2 * units)), *partials],
            [[*gather_rows(dy), w_ffn, gu]],
            [
                pltpu.VMEM((d, 2 * units), BF16),
                pltpu.VMEM((d, padded), BF16),
                pltpu.VMEM((group, 2 * units), F32),
                DMA((8,)),
                DMA((3,)),
            ],
            room=16,
        )
        g_ffn = ffn_products(b, dgu, dff, hidden)
        dmid, dattn, gg_f = call(
            norm_back_kernel,
            [held((micro_rows, d), F32), rows_low, held((1, d), F32)],
            [*summands(send, mine), (dy, mid), gain_f],
        )
        dattn = after(dattn, g_ffn)
        dattn, dq, dkv, dkv_send = call(
            functools.partial(attend_back_kernel, layer=layer),
            [
                held((group, d)),
                shape((group, q_width)),
                shape((keys // 2, 2 * HD), F32),
                shape((keys // 2, 2 * HD)),
            ],
            [place, gather_rows(dattn) + [w_attn], (q, k, v), bias, (ctx, lse), cos, sin],
            [
                pltpu.VMEM((d, q_width), BF16),
                pltpu.VMEM((group, q_width), BF16),
                pltpu.VMEM((keys // 2, 2 * HD), F32),
                pltpu.VMEM((keys // 2, 2 * HD), F32),
                DMA((8,)),
                DMA((8,)),
            ],
            room=18,
        )
        dkv = after(dkv, other) if pending else dkv
        dkv = call(kv_add_kernel, [shape(dkv.shape)], [dkv, swap_core(dkv_send)])[0]
        arrived = lax.all_to_all(
            dkv.reshape(8, group // 2, 2 * HD), ("x", "ylo"), 0, 0, tiled=True
        )
        dqkv, send, mine, gg_a = call(
            functools.partial(qkv_back_kernel, layer=layer),
            [held((group, wide)), *partials, held((1, d), F32)],
            [place, [w_attn, rows], dq, arrived, cos, sin],
            [pltpu.VMEM((d, wide), BF16), pltpu.VMEM((group, d), BF16), DMA((8,)), DMA],
            room=16,
        )
        g_attn = attn_products(dattn, ctx, a, dqkv, gg_a, gg_f)
        dx, dx_low, _ = call(
            norm_back_kernel,
            [held((micro_rows, d), F32), rows_low, held((1, d), F32)],
            [*summands(send, mine), (dmid, x), gain_a],
        )
        return dx, after(dx_low, g_attn), g_attn, g_ffn, other

    x0 = lax.dynamic_index_in_dim(block_input, section, 0, keepdims=False)
    dy1 = lax.dynamic_index_in_dim(out_grad, section, 0, keepdims=False)

    rows0, a0, q0, kv0, ga0, gf0 = project(x0, 0)
    ffn_pairs = pairs(place, ffn_shard, ffn_y)
    w_ffn0 = gather_x(ffn_pairs[0])
    kv0 = gather_kv(kv0)
    ctx0, lse0, k0, v0, send, mine = attention(q0, kv0, 0)
    mid0, b = call(add_norm_kernel, mid_outs, [*summands(send, mine), x0, gf0])
    w_ffn1 = gather_x(after(ffn_pairs[1], b))
    b0, up0, hidden0, send, mine = feed_forward(b, w_ffn0)
    y0 = call(add_kernel, [rows_low], [*summands(send, mine), (mid0,)])[0]
    kept0 = (x0, rows0, a0, q0, k0, v0, ctx0, lse0, mid0, b0, up0, hidden0, ga0, gf0, w_ffn0)
    rows1, a1, q1, kv1, ga1, gf1 = project(y0, 1)
    ctx1, lse1, k1, v1, send, mine = attention(q1, gather_kv(kv1), 1)
    mid1, b = call(add_norm_kernel, mid_outs, [*summands(send, mine), y0, gf1])
    b1, up1, hidden1, send, mine = feed_forward(b, w_ffn1)
    y1 = call(add_kernel, [rows_low], [*summands(send, mine), (mid1,)])[0]
    kept1 = (y0, rows1, a1, q1, k1, v1, ctx1, lse1, mid1, b1, up1, hidden1, ga1, gf1, w_ffn1)

    early = section == 0

    def both_micros(layer0, layer1, dtype):
        mine = jnp.where(early, layer0, layer1).astype(dtype)
        other = jnp.where(early, layer1, layer0).astype(BF16)
        other = swap_section(other).astype(dtype)
        return jnp.stack([jnp.where(early, mine, other), jnp.where(early, other, mine)])[None]

    block_output = both_micros(y0, y1, BF16)

    dx1, dx1_low, g_attn1, g_ffn1, _ = backward(dy1, kept1, 1)
    ffn1 = reduce_x(g_ffn1)
    dx0, dx0_low, g_attn0, g_ffn0, r_attn1 = backward(dx1_low, kept0, 0, (g_attn1, ffn1, block_output))
    input_grad = both_micros(dx0, dx1, F32)
    ffn_y = reduce_y(after(reduce_x(g_ffn0), input_grad), ffn1, place)

    attn_y = reduce_y(reduce_x(g_attn0), r_attn1, place)
    ffn_parts = by_core([after(ffn_y[0], attn_y[0]), *ffn_y[1:]], place)
    attn_parts = by_core(attn_y, place)

    def finish(kernel, dims, parts):
        return call(kernel, [held(s, F32) for s in dims], [place, parts], room=20)

    own = own_rows
    grad_out, grad_query, grad_key, grad_value, *gain_pieces, _ = finish(
        attn_grads_kernel,
        [(2 * q_width, own), (own, 2 * q_width), (own, HD), (own, HD)]
        + [(micro_rows, 128)] * 4
        + [(own, 128)],
        attn_parts,
    )
    grad_gate, grad_up, grad_down = finish(
        ffn_grads_kernel, [(own, 2 * units)] * 2 + [(2 * units, own)], ffn_parts
    )
    gain_sums = gain_pieces[0]
    for k in (1, 2, 3):
        gain_sums = gain_sums + from_z(gain_pieces[k], -k)
    gain_sums = gain_sums[:, :2].T


    return (
        block_output,
        input_grad,
        gain_sums[0][None],
        grad_query[None],
        grad_key[None],
        grad_value[None],
        grad_out[None],
        gain_sums[1][None],
        grad_gate[None],
        grad_up[None],
        grad_down[None],
    )


def solution(mesh):
    fine = Mesh(mesh.devices.reshape(2, 4, 2, 2, 4), AXES)
    wide = ("x", "ylo", "core")
    rows = P(None, (*wide, "tp"), None)
    into = P("section", wide, "tp")
    out_of = P("section", "tp", wide)
    grown = P("section", None, (*wide, "tp"), None)
    gain_grad = P("section", (*wide, "tp"))
    return jax.shard_map(
        body,
        mesh=fine,
        in_specs=(
            rows, rows, P(), P("section", wide), into, into, into, out_of,
            P("section", wide), into, into, out_of,
        ),
        out_specs=(
            grown, grown, gain_grad, into, into, into, out_of, gain_grad, into, into, out_of,
        ),
        check_vma=False,
    )
```

```python
import functools
import math

import jax
import jax.numpy as jnp
from jax import lax
from jax.experimental import pallas as pl
from jax.experimental.pallas import tpu as pltpu
from jax.sharding import Mesh, PartitionSpec as P

HD = 64
GAIN_ROWS = 16
EPS = 1e-05
MASKED = -1e30
KEYS_STEP = 512
AXES = ("section", "x", "ylo", "core", "tp")
SECTION, X, YLO, CORE, TP = range(5)
BF16 = jnp.bfloat16
F32 = jnp.float32
VMEM = pl.BlockSpec(memory_space=pltpu.VMEM)
SMEM = pl.BlockSpec(memory_space=pltpu.SMEM)
HBM = pl.BlockSpec(memory_space=pltpu.HBM)
DMA = pltpu.SemaphoreType.DMA


def nn(a, b):
    return jnp.dot(a, b, preferred_element_type=F32)


def nt(a, b):
    return lax.dot_general(a, b, (((1,), (1,)), ((), ())), preferred_element_type=F32)


def tn(a, b):
    return lax.dot_general(a, b, (((0,), (0,)), ((), ())), preferred_element_type=F32)


def shape(dims, dtype=BF16):
    return jax.ShapeDtypeStruct(tuple(dims), dtype)


SHORT = pl.CostEstimate(flops=1, bytes_accessed=1, transcendentals=0)


def held(dims, dtype=BF16):
    return pltpu.HBM(tuple(dims), dtype)


def pinned(v):
    return pltpu.with_memory_space_constraint(v, pltpu.HBM)


def call(kernel, outs, args, scratch=(), room=8, out_spec=None, moved=0):
    specs, values = [], []
    for a in args:
        if isinstance(a, (list, tuple)):
            specs += [HBM if isinstance(a, list) else pl.BlockSpec()] * len(a)
            values += [pinned(v) for v in a]
        else:
            specs.append(SMEM if a.dtype == jnp.int32 else VMEM)
            values.append(a)
    mine = [m for m in scratch if isinstance(m, type(pltpu.VMEM((8, 128), F32)))]
    room = room * 2**20 + sum(
        math.prod(m.shape) * jnp.dtype(m.dtype).itemsize for m in mine if m.dtype in (BF16, F32)
    )
    return pl.pallas_call(
        kernel,
        out_shape=tuple(outs),
        in_specs=specs,
        out_specs=tuple(
            VMEM if isinstance(o, jax.ShapeDtypeStruct) else out_spec or pl.BlockSpec() for o in outs
        ),
        scratch_shapes=list(scratch),
        compiler_params=pltpu.CompilerParams(vmem_limit_bytes=room),
        cost_estimate=pl.CostEstimate(flops=moved, bytes_accessed=moved, transcendentals=0)
        if moved
        else SHORT,
        name=getattr(kernel, "func", kernel).__name__,
    )(*values)


def from_z(rows, by):
    return lax.ppermute(rows, "tp", [((i + by) % 4, i) for i in range(4)])


def from_x(v, by):
    return lax.ppermute(v, "x", [((i + by) % 4, i) for i in range(4)])


def swap_core(v):
    return lax.ppermute(v, "core", [(0, 1), (1, 0)])


def swap_ylo(v):
    return lax.ppermute(v, "ylo", [(0, 1), (1, 0)])


def swap_section(v):
    return lax.ppermute(v, "section", [(0, 1), (1, 0)])


def swap_across(v):
    return lax.ppermute(v, ("section", "ylo"), [(0, 3), (3, 0), (1, 2), (2, 1)])


def after(value, *others):
    return lax.optimization_barrier((value, *others))[0]


def y_exchange(v):
    return swap_ylo(v), swap_across(v), swap_section(v)


def y_exchange_on(v):
    near, far = swap_ylo(v), swap_across(v)
    n = v.shape[0] // 2
    return near, far, swap_ylo(far[:n]), swap_across(near[n:])


def gather_rows(rows):
    pieces = [rows] + [from_z(rows, k) for k in (1, 2, 3)]
    return pieces + [swap_core(p) for p in pieces]


def gather_kv(half):
    copies = jnp.broadcast_to(half[None], (8, *half.shape))
    own = lax.all_to_all(copies, ("x", "ylo"), 0, 0, tiled=True).reshape(-1, half.shape[1])
    return own, swap_core(own)


def reduce_rows(send, mine):
    own, *pieces = split(mine, swap_core(send))
    return [own] + [from_z(p, -k) for k, p in zip((1, 2, 3), pieces)]


def gather_x(block):
    return lax.all_gather(block, "x", axis=0, tiled=True)


def reduce_x(grad):
    return lax.psum_scatter(grad, "x", scatter_dimension=0, tiled=True)


def pack_attn_kernel(place, q_ref, k_ref, v_ref, o_ref, ga_ref, gf_ref, own_ref, send_ref):
    n, rows = q_ref.shape[1] // 2, q_ref.shape[0]
    m = n + 2 * HD
    kv = jnp.concatenate([k_ref[...], v_ref[...]], axis=0).T
    o = o_ref[...].T
    odd = place[CORE] == 1
    row = lax.broadcasted_iota(jnp.int32, (GAIN_ROWS, ga_ref.shape[1]), 0)
    ga, gf = (jnp.broadcast_to(g[...].astype(F32), row.shape) for g in (ga_ref, gf_ref))
    gains = jnp.where(row == 0, ga, jnp.where(row == 1, gf, 0.0)).astype(BF16)
    rest = jnp.zeros((GAIN_ROWS, own_ref.shape[1] - gains.shape[1]), BF16)
    for ref, high in ((own_ref, odd), (send_ref, jnp.logical_not(odd))):
        ref[:rows, :n] = jnp.where(high, q_ref[:, n:], q_ref[:, :n])
        ref[:rows, n:m] = kv
        ref[:rows, m:] = jnp.where(high, o[:, n:], o[:, :n])
        ref[rows:, :] = jnp.concatenate([gains, rest], axis=1)


def pack_ffn_kernel(place, d_ref, g_ref, u_ref, own_ref, send_ref):
    odd = place[CORE] == 1
    d = d_ref[...].T
    n = d.shape[1] // 2
    spare = jnp.zeros((own_ref.shape[0], own_ref.shape[1] - 3 * n), BF16)
    low, high = (
        jnp.concatenate([w[:, at] for w in (g_ref[...], u_ref[...], d)] + [spare], axis=1)
        for at in (slice(0, n), slice(n, 2 * n))
    )
    own_ref[...] = jnp.where(odd, high, low)
    send_ref[...] = jnp.where(odd, low, high)


def chip_rows_kernel(place, own_ref, other_ref, out_ref):
    n = own_ref.shape[0]
    core = place[CORE]
    out_ref[pl.ds(pl.multiple_of(core * n, n), n), :] = own_ref[...]
    out_ref[pl.ds(pl.multiple_of((1 - core) * n, n), n), :] = other_ref[...]


def chip_rows(place, own, other):
    n, c = own.shape
    return call(chip_rows_kernel, [held((2 * n, c))], [place, (own, other)], room=12)[0]


def chip_attn_kernel(place, own_ref, other_ref, out_ref):
    n = own_ref.shape[0] - GAIN_ROWS
    core = place[CORE]
    odd = core == 1
    out_ref[pl.ds(pl.multiple_of(core * n, n), n), :] = own_ref[:n, :]
    out_ref[pl.ds(pl.multiple_of((1 - core) * n, n), n), :] = other_ref[:n, :]
    own, other = own_ref[n:, :n], other_ref[n:, :n]
    rest = jnp.zeros((GAIN_ROWS, out_ref.shape[1] - 2 * n), BF16)
    out_ref[2 * n :, :] = jnp.concatenate(
        [jnp.where(odd, other, own), jnp.where(odd, own, other), rest], axis=1
    )


def pairs_kernel(place, own_ref, near_ref, far_ref, *refs):
    *straight_refs, p0_ref, p1_ref = refs
    n, part = own_ref.shape[0], straight_refs[0].shape[0]
    here = pl.ds(pl.multiple_of(place[YLO] * n, n), n)
    there = pl.ds(pl.multiple_of((1 - place[YLO]) * n, n), n)

    def fill(mine, other):
        mine[here, :] = own_ref[...]
        mine[there, :] = near_ref[...]
        for i, ref in enumerate(straight_refs):
            at = pl.multiple_of(place[YLO] * n + i * part, part)
            other[pl.ds(at, part), :] = ref[...]
        other[there, :] = far_ref[...]

    @pl.when(place[SECTION] == 0)
    def _():
        fill(p0_ref, p1_ref)

    @pl.when(place[SECTION] == 1)
    def _():
        fill(p1_ref, p0_ref)


def pairs(place, own, others):
    n, c = own.shape
    out = held((2 * n, c))
    return call(pairs_kernel, [out, out], [place, (own, *others)], room=20)


def fetch(pieces, whole, sems):
    n = pieces[0].shape[0]
    copies = [
        pltpu.make_async_copy(p, whole.at[pl.ds(i * n, n), :], sems.at[i])
        for i, p in enumerate(pieces)
    ]
    for c in copies:
        c.start()

    def wait():
        for c in copies:
            c.wait()

    return wait


def block_of(packs, place, i):
    step = sum(p.shape[0] for p in packs) // 8
    if len(packs) == 1:
        return packs[0], i * step, i
    return packs[i // 2], i % 2 * step, lax.rem(place[X] + i // 2, 4) * 2 + i % 2


def fetch_blocks(packs, place, column, whole, sems):
    n, c = whole.shape[0] // 8, whole.shape[1]

    def copy(i, pack, row, block):
        rows = pl.ds(pl.multiple_of(block * n, n), n)
        return pltpu.make_async_copy(
            pack.at[pl.ds(row, n), pl.ds(column, c)], whole.at[rows, :], sems.at[i]
        )

    for i in range(8):
        copy(i, *block_of(packs, place, i)).start()

    def wait():
        for i in range(8):
            pack, row, _ = block_of(packs, place, i)
            copy(i, pack, row, i).wait()

    return wait


def rms(rows):
    return lax.rsqrt(jnp.mean(rows * rows, axis=-1, keepdims=True) + EPS)


def turned(v, by):
    return pltpu.roll(v, by % v.shape[1], 1)


def low_half(v):
    return lax.broadcasted_iota(jnp.int32, v.shape, 1) % HD < HD // 2


def rope(v, cos, sin):
    half = HD // 2
    return v * cos + jnp.where(low_half(v), -turned(v, -half), turned(v, half)) * sin


def rope_back(u, cos, sin):
    half, w = HD // 2, u * sin
    return u * cos + jnp.where(low_half(w), turned(w, -half), -turned(w, half))


def halves_out(partial, send_ref, mine_ref):
    n = send_ref.shape[0]
    send_ref[...] = partial[n:].astype(BF16)
    mine_ref[...] = partial[:n]


def split_kernel(mine_ref, other_ref, own_ref, *piece_refs):
    n = own_ref.shape[0]
    own_ref[...] = mine_ref[:n, :] + other_ref[:n, :].astype(F32)
    for k, ref in enumerate(piece_refs, 1):
        at = slice(k * n, (k + 1) * n)
        ref[...] = (mine_ref[at, :] + other_ref[at, :].astype(F32)).astype(BF16)


def split(mine, other):
    n, d = mine.shape[0] // 4, mine.shape[1]
    return call(split_kernel, [shape((n, d), F32)] + [shape((n, d))] * 3, [mine, other])


def total_of(refs):
    return sum((r[...].astype(F32) for r in refs[1:]), refs[0][...])


def add_norm_kernel(a, b, c, d, x_ref, gain_ref, mid_ref, low_ref):
    mid = x_ref[...].astype(F32) + total_of((a, b, c, d))
    mid_ref[...] = mid
    low_ref[...] = (mid * rms(mid) * gain_ref[...]).astype(BF16)


def add_kernel(a, b, c, d, mid_ref, y_ref):
    y_ref[...] = (mid_ref[...] + total_of((a, b, c, d))).astype(BF16)


def norm_back_kernel(a, b, c, d, after_ref, x_ref, gain_ref, dx_ref, low_ref, gain_grad_ref):
    grad = total_of((a, b, c, d))
    x = x_ref[...].astype(F32)
    r = rms(x)
    n = x * r
    gain_grad_ref[...] = jnp.sum(grad * n, axis=0, keepdims=True)
    scaled = grad * gain_ref[...]
    dx = after_ref[...].astype(F32) + r * (
        scaled - n * jnp.mean(scaled * n, axis=-1, keepdims=True)
    )
    dx_ref[...] = dx
    low_ref[...] = dx.astype(BF16)


def qkv_kernel(place, *refs, parts):
    pieces, packs, refs = refs[:8], refs[8 : 8 + parts], refs[8 + parts :]
    cos_ref, sin_ref, x_ref, a_ref, q_ref, kv_ref, ga_ref, gf_ref, *refs = refs
    w_ref, gains_ref, x_sems, w_sems, g_sems = refs
    rows_there = fetch(pieces, x_ref, x_sems)
    n = w_ref.shape[0] // 8

    def gain_copy(i, pack, row, block):
        return pltpu.make_async_copy(
            pack.at[pl.ds(row + n, GAIN_ROWS), pl.ds(0, n)], gains_ref.at[block], g_sems.at[i]
        )

    for i in range(8):
        gain_copy(i, *block_of(packs, place, i)).start()
    weights_there = fetch_blocks(packs, place, 0, w_ref, w_sems)
    for i in range(8):
        pack, row, _ = block_of(packs, place, i)
        gain_copy(i, pack, row, i).wait()
    gains = jnp.concatenate([gains_ref[i] for i in range(8)], axis=1).astype(F32)
    ga_ref[...] = gains[0:1, :]
    gf_ref[...] = gains[1:2, :]
    rows_there()
    x = x_ref[...].astype(F32)
    a = (x * rms(x) * ga_ref[...]).astype(BF16)
    a_ref[...] = a
    weights_there()
    out = rope(nn(a, w_ref[...]), cos_ref[...], sin_ref[...])
    width = q_ref.shape[1]
    q_ref[...] = (out[:, :width].astype(BF16).astype(F32) * HD**-0.5).astype(BF16)
    half = out.shape[0] // 2
    k, v = out[:, width : width + HD], out[:, width + HD :]
    keys = jnp.concatenate([k[:half], k[half:]], axis=1)
    values = jnp.concatenate([v[half:], v[:half]], axis=1)
    kv_ref[...] = jnp.where(place[CORE] == 1, values, keys).astype(BF16)


def key_step(ref, t):
    per = ref.shape[0] // KEYS_STEP
    return pl.ds(t % per * KEYS_STEP, KEYS_STEP), slice(t // per * HD, (t // per + 1) * HD)


def attend_kernel(place, q_ref, own_ref, other_ref, bias_ref, *refs, parts):
    packs, refs = refs[:parts], refs[parts:]
    o_ref, lse_ref, k_ref, v_ref, send_ref, mine_ref, s_ref, w_ref, sems = refs
    weights_there = fetch_blocks(packs, place, packs[0].shape[1] - w_ref.shape[1], w_ref, sems)
    odd = place[CORE] == 1
    k_ref[...] = jnp.where(odd, other_ref[...], own_ref[...])
    v_ref[...] = jnp.where(odd, own_ref[...], other_ref[...])
    rows, width = q_ref.shape
    heads = width // HD
    steps = 2 * k_ref.shape[0] // KEYS_STEP
    tops = [jnp.full((1, rows), MASKED, F32) for _ in range(heads)]
    for t in range(steps):
        at = pl.ds(t * KEYS_STEP, KEYS_STEP)
        part, cols = key_step(k_ref, t)
        k = k_ref[part, cols]
        bias = bias_ref[at, :]
        for h in range(heads):
            s = nt(k, q_ref[:, h * HD : (h + 1) * HD]) + bias
            s_ref[h, at, :] = s
            tops[h] = jnp.maximum(tops[h], jnp.max(s, axis=0, keepdims=True))
    sums = [jnp.zeros((1, rows), F32) for _ in range(heads)]
    outs = [jnp.zeros((HD, rows), F32) for _ in range(heads)]
    for t in range(steps):
        at = pl.ds(t * KEYS_STEP, KEYS_STEP)
        part, cols = key_step(v_ref, t)
        v_t = v_ref[part, :].T[cols, :]
        for h in range(heads):
            e = jnp.exp(s_ref[h, at, :] - tops[h])
            sums[h] = sums[h] + jnp.sum(e, axis=0, keepdims=True)
            outs[h] = outs[h] + nn(v_t, e.astype(BF16))
    flat = jnp.concatenate([outs[h] / sums[h] for h in range(heads)], axis=0)
    o_ref[...] = flat.T.astype(BF16)
    lse_ref[...] = jnp.concatenate([tops[h] + jnp.log(sums[h]) for h in range(heads)], axis=0)
    weights_there()
    halves_out(nt(o_ref[...], w_ref[...]), send_ref, mine_ref)


def ffn_kernel(*refs):
    pieces, w_hbm, refs = refs[:8], refs[8], refs[9:]
    b_ref, gu_ref, h_ref, send_ref, mine_ref, gu_w, down_w, b_sems, gu_sems, sem = refs
    rows_there = fetch(pieces, b_ref, b_sems)
    steps, n, c = 4, w_hbm.shape[0] // 4, gu_w.shape[1]

    def load(i):
        at = pl.ds(i * n, n)
        return pltpu.make_async_copy(w_hbm.at[at, pl.ds(0, c)], gu_w.at[at, :], gu_sems.at[i])

    for i in range(steps):
        load(i).start()
    down = pltpu.make_async_copy(w_hbm.at[:, pl.ds(c, down_w.shape[1])], down_w, sem)
    down.start()
    rows_there()
    for i in range(steps):
        load(i).wait()
        at = slice(i * n, (i + 1) * n)
        part = nn(b_ref[:, at], gu_w[at, :])
        gu_ref[...] = part if i == 0 else gu_ref[...] + part
    units = gu_ref.shape[1] // 2
    gate, up = gu_ref[:, :units], gu_ref[:, units:]
    h_ref[:, :units] = (gate / (1.0 + jnp.exp(-gate)) * up).astype(BF16)
    spare = h_ref.shape[1] - units
    h_ref[:, units:] = jnp.zeros((h_ref.shape[0], spare), BF16)
    down.wait()
    halves_out(nt(h_ref[...], down_w[...]), send_ref, mine_ref)


def ffn_back_kernel(*refs):
    pieces, w_hbm, act_hbm, refs = refs[:8], refs[8], refs[9], refs[10:]
    dff_ref, dgu_ref, send_ref, mine_ref, gu_w, down_w, gu_ref, r_sems, gu_sems = refs
    rows_there = fetch(pieces, dff_ref, r_sems)
    c = gu_w.shape[1]
    down = pltpu.make_async_copy(w_hbm.at[:, pl.ds(c, down_w.shape[1])], down_w, gu_sems.at[2])
    down.start()
    act = pltpu.make_async_copy(act_hbm, gu_ref, gu_sems.at[0])
    act.start()
    load = pltpu.make_async_copy(w_hbm.at[:, pl.ds(0, c)], gu_w, gu_sems.at[1])
    load.start()
    rows_there()
    down.wait()
    units = gu_ref.shape[1] // 2
    dh = nn(dff_ref[...], down_w[...])[:, :units]
    act.wait()
    gate, up = gu_ref[:, :units], gu_ref[:, units:]
    sig = 1.0 / (1.0 + jnp.exp(-gate))
    dgate = dh * up * (sig * (1.0 + gate * (1.0 - sig)))
    dgu_ref[...] = jnp.concatenate([dgate, dh * (gate * sig)], axis=1).astype(BF16)
    load.wait()
    halves_out(nt(dgu_ref[...], gu_w[...]), send_ref, mine_ref)


def attend_back_kernel(place, *refs, parts):
    pieces, packs, refs = refs[:8], refs[8 : 8 + parts], refs[8 + parts :]
    q_ref, k_ref, v_ref, bias_ref, o_ref, lse_ref, cos_ref, sin_ref, *refs = refs
    dattn_ref, dq_ref, own_ref, send_ref, w_ref, do_ref, dk_ref, dv_ref, sems, r_sems = refs
    rows_there = fetch(pieces, dattn_ref, r_sems)
    weights_there = fetch_blocks(packs, place, packs[0].shape[1] - w_ref.shape[1], w_ref, sems)
    rows, width = q_ref.shape
    heads = width // HD
    steps = 2 * k_ref.shape[0] // KEYS_STEP
    rows_there()
    weights_there()
    do = nn(dattn_ref[...], w_ref[...])
    do_ref[...] = do.astype(BF16)
    both = (do_ref[...].astype(F32) * o_ref[...].astype(F32)).T
    deltas = [
        jnp.sum(both[h * HD : (h + 1) * HD, :], axis=0, keepdims=True) for h in range(heads)
    ]
    dq_t = [jnp.zeros((HD, rows), F32) for _ in range(heads)]
    for t in range(steps):
        at = pl.ds(t * KEYS_STEP, KEYS_STEP)
        part, cols = key_step(k_ref, t)
        k = k_ref[part, cols]
        v = v_ref[part, cols]
        k_t = k_ref[part, :].T[cols, :]
        bias = bias_ref[at, :]
        dk = jnp.zeros((KEYS_STEP, HD), F32)
        dv = jnp.zeros((KEYS_STEP, HD), F32)
        for h in range(heads):
            q_h = q_ref[:, h * HD : (h + 1) * HD]
            do_h = do_ref[:, h * HD : (h + 1) * HD]
            p = jnp.exp(nt(k, q_h) + bias - lse_ref[h : h + 1, :])
            ds = (p * (nt(v, do_h) - deltas[h])).astype(BF16)
            dv = dv + nn(p.astype(BF16), do_h)
            dk = dk + nn(ds, q_h)
            dq_t[h] = dq_t[h] + nn(k_t, ds)
        dk_ref[part, cols] = dk
        dv_ref[part, cols] = dv
    dq = jnp.concatenate(dq_t, axis=0).T * HD**-0.5
    dq_ref[...] = rope_back(dq, cos_ref[:, :width], sin_ref[:, :width]).astype(BF16)
    odd = place[CORE] == 1
    own_ref[...] = jnp.where(odd, dv_ref[...], dk_ref[...])
    send_ref[...] = jnp.where(odd, dk_ref[...], dv_ref[...]).astype(BF16)


def kv_add_kernel(own_ref, other_ref, out_ref):
    out_ref[...] = (own_ref[...] + other_ref[...].astype(F32)).astype(BF16)


def qkv_back_kernel(place, *refs, parts):
    packs, (x_hbm, dq_ref, kv_ref, cos_ref, sin_ref, *refs) = refs[:parts], refs[parts:]
    dqkv_ref, send_ref, mine_ref, gain_grad_ref, w_ref, x_ref, sems, x_sem = refs
    weights_there = fetch_blocks(packs, place, 0, w_ref, sems)
    rows_there = pltpu.make_async_copy(x_hbm, x_ref, x_sem)
    rows_there.start()
    width, odd = dq_ref.shape[1], place[CORE] == 1
    both = sum((kv_ref[i].astype(F32) for i in range(1, 8)), kv_ref[0].astype(F32))
    first, second = both[:, :HD], both[:, HD:]
    dk = jnp.concatenate([first, second], axis=0)
    dv = jnp.concatenate([second, first], axis=0)
    spare = jnp.zeros_like(dk)
    dkv = jnp.where(
        odd, jnp.concatenate([spare, dv], axis=1), jnp.concatenate([dk, spare], axis=1)
    )
    dkv = rope_back(dkv, cos_ref[:, width:], sin_ref[:, width:])
    dqkv_ref[:, :width] = dq_ref[...]
    dqkv_ref[:, width:] = dkv.astype(BF16)
    weights_there()
    da = nt(dqkv_ref[...], w_ref[...])
    halves_out(da, send_ref, mine_ref)
    rows_there.wait()
    x = x_ref[...].astype(F32)
    gain_grad_ref[...] = jnp.sum(da * (x * rms(x)), axis=0, keepdims=True)


def ffn_product_kernel(b_ref, dgu_ref, dff_ref, h_ref, out, whole, sems):
    n, steps = dgu_ref.shape[1], sems.shape[0]
    rows = whole.shape[0] // steps
    copies = []
    for i in range(steps):
        at = slice(i * rows, (i + 1) * rows)
        whole[at, :n] = tn(b_ref[:, at], dgu_ref[...]).astype(BF16)
        whole[at, n:] = tn(dff_ref[:, at], h_ref[...]).astype(BF16)
        here = pl.ds(i * rows, rows)
        copies.append(pltpu.make_async_copy(whole.at[here, :], out.at[here, :], sems.at[i]))
        copies[-1].start()
    for c in copies:
        c.wait()


def ffn_products(b, dgu, dff, hidden):
    dims = (b.shape[1], dgu.shape[1] + hidden.shape[1])
    return call(
        ffn_product_kernel,
        [pltpu.HBM(dims, BF16)],
        [(b, dgu, dff, hidden)],
        [pltpu.VMEM(dims, BF16), DMA((8,))],
        room=14,
        moved=20_000_000,
        out_spec=HBM,
    )[0]


def attn_product_kernel(dattn, a, gg_a, gg_f, ctx, dqkv, out, whole, sems):
    m, steps = ctx.shape[1], sems.shape[0]
    wide = m + dqkv.shape[1]
    rows = whole.shape[0] // steps
    row = lax.broadcasted_iota(jnp.int32, (whole.shape[1] - wide, rows), 0)
    copies = []
    for i in range(steps):
        at = slice(i * rows, (i + 1) * rows)
        whole[at, :m] = tn(dattn[:, at], ctx[...]).astype(BF16)
        whole[at, m:wide] = tn(a[:, at], dqkv[...]).astype(BF16)
        ga, gf = (jnp.broadcast_to(g[:, at], row.shape) for g in (gg_a, gg_f))
        gains = jnp.where(row == 0, ga, jnp.where(row == 1, gf, 0.0))
        whole[at, wide:] = gains.T.astype(BF16)
        here = pl.ds(i * rows, rows)
        copies.append(pltpu.make_async_copy(whole.at[here, :], out.at[here, :], sems.at[i]))
        copies[-1].start()
    for c in copies:
        c.wait()


def attn_products(dattn, ctx, a, dqkv, gg_a, gg_f):
    dims = (a.shape[1], ctx.shape[1] + dqkv.shape[1] + 128)
    return call(
        attn_product_kernel,
        [pltpu.HBM(dims, BF16)],
        [(dattn, a, gg_a, gg_f, ctx, dqkv)],
        [pltpu.VMEM(dims, BF16), DMA((4,))],
        room=14,
        moved=12_000_000,
        out_spec=HBM,
    )[0]


def y_split_kernel(place, r0_ref, r1_ref, keep_ref, near_ref, far_ref, straight_ref):
    n = keep_ref.shape[0]
    here = pl.ds(pl.multiple_of(place[YLO] * n, n), n)
    there = pl.ds(pl.multiple_of((1 - place[YLO]) * n, n), n)

    def fill(mine, other):
        keep_ref[...] = mine[here, :]
        near_ref[...] = mine[there, :]
        straight_ref[...] = other[here, :]
        far_ref[...] = other[there, :]

    @pl.when(place[SECTION] == 0)
    def _():
        fill(r0_ref, r1_ref)

    @pl.when(place[SECTION] == 1)
    def _():
        fill(r1_ref, r0_ref)


def by_core_kernel(place, *refs):
    *parts, own_ref, send_ref = refs
    n = own_ref.shape[0]
    here = pl.ds(pl.multiple_of(place[CORE] * n, n), n)
    there = pl.ds(pl.multiple_of((1 - place[CORE]) * n, n), n)
    own_ref[...] = sum(p[here, :].astype(F32) for p in parts)
    send_ref[...] = sum(p[there, :].astype(F32) for p in parts).astype(BF16)


def by_core(parts, place):
    n, c = parts[0].shape[0] // 2, parts[0].shape[1]
    own, send = call(
        by_core_kernel, [held((n, c), F32), shape((n, c))], [place, tuple(parts)], room=16
    )
    return own, swap_core(send)


def reduce_y(r0, r1, place):
    n, c = r0.shape[0] // 2, r0.shape[1]
    keep, near, far, straight = call(y_split_kernel, [held((n, c))] * 4, [place, (r0, r1)], room=16)
    return [keep, swap_ylo(near), swap_across(far), swap_section(straight)]


def ordered(odd, own, other):
    other = other.astype(F32)
    return jnp.concatenate(
        [jnp.where(odd, other, own), jnp.where(odd, own, other)], axis=1
    )


def attn_grads_kernel(place, own_ref, other_ref, o_ref, q_ref, k_ref, v_ref, *gain_refs):
    odd = place[CORE] == 1
    m = n = q_ref.shape[1] // 2
    own, other = own_ref[:, :m].T, other_ref[:, :m].astype(F32).T
    o_ref[:m, :] = jnp.where(odd, other, own)
    o_ref[m:, :] = jnp.where(odd, own, other)
    q_ref[...] = ordered(odd, own_ref[:, m : m + n], other_ref[:, m : m + n])
    both = own_ref[:, m + n :] + other_ref[:, m + n :].astype(F32)
    kv = both[:, : 2 * HD].T
    k_ref[...] = kv[:HD, :]
    v_ref[...] = kv[HD:, :]
    rows = gain_refs[0].shape[0]
    gain_refs[-1][...] = both[:, 2 * HD :]
    for k, ref in enumerate(gain_refs[:-1]):
        at = lax.rem(place[TP] + k, 4) * rows
        ref[...] = gain_refs[-1][pl.ds(pl.multiple_of(at, rows), rows), :]


def ffn_grads_kernel(place, own_ref, other_ref, gate_ref, up_ref, down_ref):
    odd = place[CORE] == 1
    n = gate_ref.shape[1] // 2
    gate_ref[...] = ordered(odd, own_ref[:, :n], other_ref[:, :n])
    up_ref[...] = ordered(odd, own_ref[:, n : 2 * n], other_ref[:, n : 2 * n])
    own, other = own_ref[:, 2 * n :].T[:n], other_ref[:, 2 * n :].astype(F32).T[:n]
    down_ref[:n, :] = jnp.where(odd, other, own)
    down_ref[n:, :] = jnp.where(odd, own, other)


def body(
    block_input,
    out_grad,
    seg_ids,
    attn_gain,
    w_query,
    w_key,
    w_value,
    w_out,
    ffn_gain,
    w_gate,
    w_up,
    w_down,
):
    at = {name: lax.axis_index(name) for name in AXES}
    section, core, tp = at["section"], at["core"], at["tp"]
    place = jnp.stack([at[name] for name in AXES]).astype(jnp.int32)
    d = block_input.shape[2]
    micro_rows = block_input.shape[1]
    group = 8 * micro_rows
    q_width = w_query.shape[2] // 2
    units = w_gate.shape[2] // 2
    own_rows = w_query.shape[1]

    padded = units + (-units) % 128
    attn_dims = (own_rows + GAIN_ROWS, 2 * q_width + 2 * HD)
    attn_own, attn_send = call(
        pack_attn_kernel,
        [shape(attn_dims)] * 2,
        [place, (w_query[0], w_key[0].T, w_value[0].T, w_out[0], attn_gain, ffn_gain)],
    )
    attn_shard = call(
        chip_attn_kernel,
        [held((2 * own_rows + GAIN_ROWS, attn_dims[1]))],
        [place, (attn_own, swap_core(attn_send))],
    )[0]
    ffn_own, ffn_send = call(
        pack_ffn_kernel,
        [shape((own_rows, 2 * units + padded))] * 2,
        [place, (w_down[0], w_gate[0], w_up[0])],
        room=16,
    )
    ffn_shard = chip_rows(place, ffn_own, swap_core(ffn_send))
    attn_y = y_exchange(after(attn_shard, ffn_shard))
    attn_pairs = pairs(place, attn_shard, attn_y)
    attn0 = [attn_pairs[0]] + [from_x(attn_pairs[0], k) for k in (1, 2, 3)]
    attn1 = [gather_x(attn_pairs[1])]
    ffn_y = y_exchange_on(after(ffn_shard, *attn_y))

    block = at["x"] * 2 + at["ylo"]
    seg_row = lax.dynamic_index_in_dim(seg_ids, section, 0, keepdims=False)
    def arranged(row):
        v = row.reshape(8, 2, 4, micro_rows)
        return lax.dynamic_slice_in_dim(jnp.concatenate([v, v], axis=2), tp, 4, 2)

    def keys_of(row):
        return arranged(row).transpose(1, 0, 2, 3).reshape(-1)

    def queries_of(row):
        v = lax.dynamic_index_in_dim(arranged(row), block, 0, keepdims=False)
        return jnp.where(core == 0, v, v[::-1]).reshape(-1)

    places = jnp.arange(seg_row.shape[0], dtype=jnp.int32)
    k_pos, k_seg = keys_of(places), keys_of(seg_row)
    q_pos, q_seg = queries_of(places), queries_of(seg_row)
    seen = (k_pos[:, None] <= q_pos[None, :]) & (k_seg[:, None] == q_seg[None, :])
    bias = jnp.where(seen, 0.0, MASKED).astype(F32)

    frequency = 10000.0 ** (-jnp.arange(0, HD, 2, dtype=F32) / HD)
    angles = q_pos.astype(F32)[:, None] * frequency[None, :]
    wide = q_width + 2 * HD
    plain = lax.broadcasted_iota(jnp.int32, (group, wide), 1) >= q_width + HD
    cos, sin = (jnp.concatenate([t] * 12, axis=1) for t in (jnp.cos(angles), jnp.sin(angles)))
    cos, sin = jnp.where(plain, 1.0, cos), jnp.where(plain, 0.0, sin)

    rows_low = shape((micro_rows, d))
    rows_f32 = shape((micro_rows, d), F32)
    mid_outs = [rows_f32, rows_low]
    partials = [shape((group // 2, d)), shape((group // 2, d), F32)]
    heads, keys = q_width // HD, seg_row.shape[0]
    gain_row = shape((1, d), F32)

    def project(x, packs):
        return call(
            functools.partial(qkv_kernel, parts=len(packs)),
            [held((group, d))] * 2
            + [shape((group, q_width)), shape((group // 2, 2 * HD))]
            + [gain_row, gain_row],
            [place, gather_rows(x) + packs, cos, sin],
            [
                pltpu.VMEM((d, wide), BF16),
                pltpu.VMEM((8, GAIN_ROWS, d // 8), BF16),
                DMA((8,)),
                DMA((8,)),
                DMA((8,)),
            ],
            room=18,
        )

    both_kv = held((keys // 2, 2 * HD))

    def attention(q, kv, packs):
        return call(
            functools.partial(attend_kernel, parts=len(packs)),
            [held((group, q_width)), held((heads, group), F32), both_kv, both_kv, *partials],
            [place, q, *kv, bias, packs],
            [
                pltpu.VMEM((heads, keys, group), F32),
                pltpu.VMEM((d, q_width), BF16),
                DMA((8,)),
            ],
            room=12,
        )

    def feed_forward(b, w_ffn):
        return call(
            ffn_kernel,
            [held((group, d)), held((group, 2 * units), F32), held((group, padded)), *partials],
            [[*gather_rows(b), w_ffn]],
            [
                pltpu.VMEM((d, 2 * units), BF16),
                pltpu.VMEM((d, padded), BF16),
                DMA((8,)),
                DMA((4,)),
                DMA,
            ],
            room=16,
        )

    def backward(dy, kept, pending=None):
        x, rows, a, q, k, v, ctx, lse, mid, b, gu, hidden, gain_a, gain_f, w_ffn, packs = kept
        other = pending and reduce_x(after(pending[0], *pending[1:], dy))
        dff, dgu, send, mine = call(
            ffn_back_kernel,
            [held((group, d)), held((group, 2 * units)), *partials],
            [[*gather_rows(dy), w_ffn, gu]],
            [
                pltpu.VMEM((d, 2 * units), BF16),
                pltpu.VMEM((d, padded), BF16),
                pltpu.VMEM((group, 2 * units), F32),
                DMA((8,)),
                DMA((3,)),
            ],
            room=16,
        )
        g_ffn = ffn_products(b, dgu, dff, hidden)
        dmid, dattn, gg_f = call(
            norm_back_kernel,
            [rows_f32, rows_low, held((1, d), F32)],
            [*reduce_rows(send, mine), dy, mid, gain_f],
        )
        dattn = after(dattn, g_ffn)
        dattn, dq, dkv, dkv_send = call(
            functools.partial(attend_back_kernel, parts=len(packs)),
            [
                held((group, d)),
                shape((group, q_width)),
                shape((keys // 2, 2 * HD), F32),
                shape((keys // 2, 2 * HD)),
            ],
            [place, gather_rows(dattn) + packs, (q, k, v), bias, (ctx, lse), cos, sin],
            [
                pltpu.VMEM((d, q_width), BF16),
                pltpu.VMEM((group, q_width), BF16),
                pltpu.VMEM((keys // 2, 2 * HD), F32),
                pltpu.VMEM((keys // 2, 2 * HD), F32),
                DMA((8,)),
                DMA((8,)),
            ],
            room=18,
        )
        dkv = after(dkv, other) if pending else dkv
        dkv = call(kv_add_kernel, [shape(dkv.shape)], [dkv, swap_core(dkv_send)])[0]
        arrived = lax.all_to_all(
            dkv.reshape(8, group // 2, 2 * HD), ("x", "ylo"), 0, 0, tiled=True
        )
        dqkv, send, mine, gg_a = call(
            functools.partial(qkv_back_kernel, parts=len(packs)),
            [held((group, wide)), *partials, held((1, d), F32)],
            [place, packs + [rows], dq, arrived, cos, sin],
            [pltpu.VMEM((d, wide), BF16), pltpu.VMEM((group, d), BF16), DMA((8,)), DMA],
            room=16,
        )
        g_attn = attn_products(dattn, ctx, a, dqkv, gg_a, gg_f)
        dx, dx_low, _ = call(
            norm_back_kernel,
            [rows_f32, rows_low, held((1, d), F32)],
            [*reduce_rows(send, mine), dmid, x, gain_a],
        )
        return dx, after(dx_low, g_attn), g_attn, g_ffn, other, dqkv

    x0 = lax.dynamic_index_in_dim(block_input, section, 0, keepdims=False)
    dy1 = lax.dynamic_index_in_dim(out_grad, section, 0, keepdims=False)

    rows0, a0, q0, kv0, ga0, gf0 = project(x0, attn0)
    ffn_pairs = pairs(place, ffn_shard, ffn_y)
    w_ffn0 = gather_x(after(ffn_pairs[0], *attn0[1:], *attn1))
    kv0 = gather_kv(kv0)
    ctx0, lse0, k0, v0, send, mine = attention(q0, kv0, attn0)
    mid0, b = call(add_norm_kernel, mid_outs, [*reduce_rows(send, mine), x0, gf0])
    w_ffn1 = gather_x(after(ffn_pairs[1], b))
    b0, up0, hidden0, send, mine = feed_forward(b, w_ffn0)
    y0 = call(add_kernel, [rows_low], [*reduce_rows(send, mine), mid0])[0]
    kept0 = (x0, rows0, a0, q0, k0, v0, ctx0, lse0, mid0, b0, up0, hidden0, ga0, gf0, w_ffn0, attn0)
    rows1, a1, q1, kv1, ga1, gf1 = project(y0, attn1)
    ctx1, lse1, k1, v1, send, mine = attention(q1, gather_kv(kv1), attn1)
    mid1, b = call(add_norm_kernel, mid_outs, [*reduce_rows(send, mine), y0, gf1])
    b1, up1, hidden1, send, mine = feed_forward(b, w_ffn1)
    last = (send, mine, mid1)
    kept1 = (y0, rows1, a1, q1, k1, v1, ctx1, lse1, mid1, b1, up1, hidden1, ga1, gf1, w_ffn1, attn1)

    early = section == 0

    def both_micros(layer0, layer1, dtype):
        mine = jnp.where(early, layer0, layer1).astype(dtype)
        other = jnp.where(early, layer1, layer0).astype(BF16)
        other = swap_section(other).astype(dtype)
        return jnp.stack([jnp.where(early, mine, other), jnp.where(early, other, mine)])[None]

    dx1, dx1_low, g_attn1, g_ffn1, _, _ = backward(dy1, kept1)
    ffn1 = reduce_x(g_ffn1)
    dx0, dx0_low, g_attn0, g_ffn0, r_attn1, dqkv0 = backward(dx1_low, kept0, (g_attn1, ffn1))
    send, mine, mid1 = last
    y1 = call(add_kernel, [rows_low], [*reduce_rows(after(send, dqkv0), mine), mid1])[0]
    block_output = both_micros(y0, y1, BF16)
    input_grad = both_micros(dx0, dx1, F32)
    ffn_y = reduce_y(after(reduce_x(g_ffn0), input_grad, block_output), ffn1, place)

    attn_y = reduce_y(reduce_x(g_attn0), r_attn1, place)
    ffn_parts = by_core([after(ffn_y[0], attn_y[0]), *ffn_y[1:]], place)

    def finish(kernel, dims, parts):
        return call(kernel, [held(s, F32) for s in dims], [place, parts], room=20)

    own = own_rows
    grad_gate, grad_up, grad_down = finish(
        ffn_grads_kernel, [(own, 2 * units)] * 2 + [(2 * units, own)], ffn_parts
    )
    attn_parts = by_core(attn_y, place)
    grad_out, grad_query, grad_key, grad_value, *gain_pieces, _ = finish(
        attn_grads_kernel,
        [(2 * q_width, own), (own, 2 * q_width), (HD, own), (HD, own)]
        + [(micro_rows, 128)] * 4
        + [(own, 128)],
        attn_parts,
    )
    gain_sums = gain_pieces[0]
    for k in (1, 2, 3):
        gain_sums = gain_sums + from_z(gain_pieces[k], -k)
    gain_sums = gain_sums[:, :2].T


    return (
        block_output,
        input_grad,
        gain_sums[0][None],
        grad_query[None],
        grad_key.T[None],
        grad_value.T[None],
        grad_out[None],
        gain_sums[1][None],
        grad_gate[None],
        grad_up[None],
        grad_down[None],
    )


def solution(mesh):
    fine = Mesh(mesh.devices.reshape(2, 4, 2, 2, 4), AXES)
    wide = ("x", "ylo", "core")
    rows = P(None, (*wide, "tp"), None)
    into = P("section", wide, "tp")
    out_of = P("section", "tp", wide)
    grown = P("section", None, (*wide, "tp"), None)
    gain_grad = P("section", (*wide, "tp"))
    return jax.shard_map(
        body,
        mesh=fine,
        in_specs=(
            rows, rows, P(), P("section", wide), into, into, into, out_of,
            P("section", wide), into, into, out_of,
        ),
        out_specs=(
            grown, grown, gain_grad, into, into, into, out_of, gain_grad, into, into, out_of,
        ),
        check_vma=False,
    )
```

```python
import functools
import math

import jax
import jax.numpy as jnp
from jax import lax
from jax.experimental import pallas as pl
from jax.experimental.pallas import tpu as pltpu
from jax.sharding import Mesh, PartitionSpec as P

HD = 64
GAIN_ROWS = 16
EPS = 1e-05
MASKED = -1e30
KEYS_STEP = 512
AXES = ("section", "x", "ylo", "core", "tp")
SECTION, X, YLO, CORE, TP = range(5)
BF16 = jnp.bfloat16
F32 = jnp.float32
VMEM = pl.BlockSpec(memory_space=pltpu.VMEM)
SMEM = pl.BlockSpec(memory_space=pltpu.SMEM)
HBM = pl.BlockSpec(memory_space=pltpu.HBM)
DMA = pltpu.SemaphoreType.DMA


def nn(a, b):
    return jnp.dot(a, b, preferred_element_type=F32)


def nt(a, b):
    return lax.dot_general(a, b, (((1,), (1,)), ((), ())), preferred_element_type=F32)


def tn(a, b):
    return lax.dot_general(a, b, (((0,), (0,)), ((), ())), preferred_element_type=F32)


def shape(dims, dtype=BF16):
    return jax.ShapeDtypeStruct(tuple(dims), dtype)


SHORT = pl.CostEstimate(flops=1, bytes_accessed=1, transcendentals=0)


def held(dims, dtype=BF16):
    return pltpu.HBM(tuple(dims), dtype)


def pinned(v):
    return pltpu.with_memory_space_constraint(v, pltpu.HBM)


def call(kernel, outs, args, scratch=(), room=8, out_spec=None, moved=0, aliases=None):
    specs, values = [], []
    for a in args:
        if isinstance(a, (list, tuple)):
            specs += [HBM if isinstance(a, list) else pl.BlockSpec()] * len(a)
            values += [pinned(v) for v in a]
        else:
            specs.append(SMEM if a.dtype == jnp.int32 else VMEM)
            values.append(a)
    mine = [m for m in scratch if isinstance(m, type(pltpu.VMEM((8, 128), F32)))]
    room = room * 2**20 + sum(
        math.prod(m.shape) * jnp.dtype(m.dtype).itemsize for m in mine if m.dtype in (BF16, F32)
    )
    return pl.pallas_call(
        kernel,
        out_shape=tuple(outs),
        in_specs=specs,
        out_specs=tuple(
            VMEM if isinstance(o, jax.ShapeDtypeStruct) else out_spec or pl.BlockSpec() for o in outs
        ),
        scratch_shapes=list(scratch),
        input_output_aliases=aliases or {},
        compiler_params=pltpu.CompilerParams(vmem_limit_bytes=room),
        cost_estimate=pl.CostEstimate(flops=moved, bytes_accessed=moved, transcendentals=0)
        if moved
        else SHORT,
        name=getattr(kernel, "func", kernel).__name__,
    )(*values)


def from_z(rows, by):
    return lax.ppermute(rows, "tp", [((i + by) % 4, i) for i in range(4)])


def from_x(v, by):
    return lax.ppermute(v, "x", [((i + by) % 4, i) for i in range(4)])


def swap_core(v):
    return lax.ppermute(v, "core", [(0, 1), (1, 0)])


def swap_ylo(v):
    return lax.ppermute(v, "ylo", [(0, 1), (1, 0)])


def swap_section(v):
    return lax.ppermute(v, "section", [(0, 1), (1, 0)])


def swap_across(v):
    return lax.ppermute(v, ("section", "ylo"), [(0, 3), (3, 0), (1, 2), (2, 1)])


def after(value, *others):
    return lax.optimization_barrier((value, *others))[0]


def y_exchange(v):
    return swap_ylo(v), swap_across(v), swap_section(v)


def y_exchange_on(v):
    near, far = swap_ylo(v), swap_across(v)
    n = v.shape[0] // 2
    return near, far, swap_ylo(far[:n]), swap_across(near[n:])


def gather_rows(rows):
    pieces = [rows] + [from_z(rows, k) for k in (1, 2, 3)]
    return pieces + [swap_core(p) for p in pieces]


def gather_kv(half):
    copies = jnp.broadcast_to(half[None], (8, *half.shape))
    own = lax.all_to_all(copies, ("x", "ylo"), 0, 0, tiled=True).reshape(-1, half.shape[1])
    return own, swap_core(own)


def reduce_rows(send, mine):
    own, *pieces = split(mine, swap_core(send))
    return [own] + [from_z(p, -k) for k, p in zip((1, 2, 3), pieces)]


def gather_x(block):
    return lax.all_gather(block, "x", axis=0, tiled=True)


def reduce_x(grad):
    return lax.psum_scatter(grad, "x", scatter_dimension=0, tiled=True)


def pack_attn_kernel(place, q_ref, k_ref, v_ref, o_ref, ga_ref, gf_ref, own_ref, send_ref):
    n, rows = q_ref.shape[1] // 2, q_ref.shape[0]
    m = n + 2 * HD
    kv = jnp.concatenate([k_ref[...], v_ref[...]], axis=0).T
    o = o_ref[...].T
    odd = place[CORE] == 1
    row = lax.broadcasted_iota(jnp.int32, (GAIN_ROWS, ga_ref.shape[1]), 0)
    ga, gf = (jnp.broadcast_to(g[...].astype(F32), row.shape) for g in (ga_ref, gf_ref))
    gains = jnp.where(row == 0, ga, jnp.where(row == 1, gf, 0.0)).astype(BF16)
    rest = jnp.zeros((GAIN_ROWS, own_ref.shape[1] - gains.shape[1]), BF16)
    for ref, high in ((own_ref, odd), (send_ref, jnp.logical_not(odd))):
        ref[:rows, :n] = jnp.where(high, q_ref[:, n:], q_ref[:, :n])
        ref[:rows, n:m] = kv
        ref[:rows, m:] = jnp.where(high, o[:, n:], o[:, :n])
        ref[rows:, :] = jnp.concatenate([gains, rest], axis=1)


def pack_ffn_kernel(place, d_ref, g_ref, u_ref, own_ref, send_ref):
    odd = place[CORE] == 1
    d = d_ref[...].T
    n = d.shape[1] // 2
    spare = jnp.zeros((own_ref.shape[0], own_ref.shape[1] - 3 * n), BF16)
    low, high = (
        jnp.concatenate([w[:, at] for w in (g_ref[...], u_ref[...], d)] + [spare], axis=1)
        for at in (slice(0, n), slice(n, 2 * n))
    )
    own_ref[...] = jnp.where(odd, high, low)
    send_ref[...] = jnp.where(odd, low, high)


def chip_rows_kernel(place, own_ref, other_ref, out_ref):
    n = own_ref.shape[0]
    core = place[CORE]
    out_ref[pl.ds(pl.multiple_of(core * n, n), n), :] = own_ref[...]
    out_ref[pl.ds(pl.multiple_of((1 - core) * n, n), n), :] = other_ref[...]


def chip_rows(place, own, other):
    n, c = own.shape
    return call(chip_rows_kernel, [held((2 * n, c))], [place, (own, other)], room=12)[0]


def chip_attn_kernel(place, own_ref, other_ref, out_ref):
    n = own_ref.shape[0] - GAIN_ROWS
    core = place[CORE]
    odd = core == 1
    out_ref[pl.ds(pl.multiple_of(core * n, n), n), :] = own_ref[:n, :]
    out_ref[pl.ds(pl.multiple_of((1 - core) * n, n), n), :] = other_ref[:n, :]
    own, other = own_ref[n:, :n], other_ref[n:, :n]
    rest = jnp.zeros((GAIN_ROWS, out_ref.shape[1] - 2 * n), BF16)
    out_ref[2 * n :, :] = jnp.concatenate(
        [jnp.where(odd, other, own), jnp.where(odd, own, other), rest], axis=1
    )


def pairs_kernel(place, own_ref, near_ref, far_ref, *refs):
    *straight_refs, p0_ref, p1_ref = refs
    n, part = own_ref.shape[0], straight_refs[0].shape[0]
    here = pl.ds(pl.multiple_of(place[YLO] * n, n), n)
    there = pl.ds(pl.multiple_of((1 - place[YLO]) * n, n), n)

    def fill(mine, other):
        mine[here, :] = own_ref[...]
        mine[there, :] = near_ref[...]
        for i, ref in enumerate(straight_refs):
            at = pl.multiple_of(place[YLO] * n + i * part, part)
            other[pl.ds(at, part), :] = ref[...]
        other[there, :] = far_ref[...]

    @pl.when(place[SECTION] == 0)
    def _():
        fill(p0_ref, p1_ref)

    @pl.when(place[SECTION] == 1)
    def _():
        fill(p1_ref, p0_ref)


def pairs(place, own, others):
    n, c = own.shape
    out = held((2 * n, c))
    return call(pairs_kernel, [out, out], [place, (own, *others)], room=20)


def fetch(pieces, whole, sems):
    n = pieces[0].shape[0]
    copies = [
        pltpu.make_async_copy(p, whole.at[pl.ds(i * n, n), :], sems.at[i])
        for i, p in enumerate(pieces)
    ]
    for c in copies:
        c.start()

    def wait():
        for c in copies:
            c.wait()

    return wait


def block_of(packs, place, i):
    step = sum(p.shape[0] for p in packs) // 8
    if len(packs) == 1:
        return packs[0], i * step, i
    return packs[i // 2], i % 2 * step, lax.rem(place[X] + i // 2, 4) * 2 + i % 2


def fetch_blocks(packs, place, column, whole, sems):
    n, c = whole.shape[0] // 8, whole.shape[1]

    def copy(i, pack, row, block):
        rows = pl.ds(pl.multiple_of(block * n, n), n)
        return pltpu.make_async_copy(
            pack.at[pl.ds(row, n), pl.ds(column, c)], whole.at[rows, :], sems.at[i]
        )

    for i in range(8):
        copy(i, *block_of(packs, place, i)).start()

    def wait():
        for i in range(8):
            pack, row, _ = block_of(packs, place, i)
            copy(i, pack, row, i).wait()

    return wait


def rms(rows):
    return lax.rsqrt(jnp.mean(rows * rows, axis=-1, keepdims=True) + EPS)


def turned(v, by):
    return pltpu.roll(v, by % v.shape[1], 1)


def low_half(v):
    return lax.broadcasted_iota(jnp.int32, v.shape, 1) % HD < HD // 2


def rope(v, cos, sin):
    half = HD // 2
    return v * cos + jnp.where(low_half(v), -turned(v, -half), turned(v, half)) * sin


def rope_back(u, cos, sin):
    half, w = HD // 2, u * sin
    return u * cos + jnp.where(low_half(w), turned(w, -half), -turned(w, half))


def halves_out(partial, send_ref, mine_ref):
    n = send_ref.shape[0]
    send_ref[...] = partial[n:].astype(BF16)
    mine_ref[...] = partial[:n]


def split_kernel(mine_ref, other_ref, own_ref, *piece_refs):
    n = own_ref.shape[0]
    own_ref[...] = mine_ref[:n, :] + other_ref[:n, :].astype(F32)
    for k, ref in enumerate(piece_refs, 1):
        at = slice(k * n, (k + 1) * n)
        ref[...] = (mine_ref[at, :] + other_ref[at, :].astype(F32)).astype(BF16)


def split(mine, other):
    n, d = mine.shape[0] // 4, mine.shape[1]
    return call(split_kernel, [shape((n, d), F32)] + [shape((n, d))] * 3, [mine, other])


def total_of(refs):
    return sum((r[...].astype(F32) for r in refs[1:]), refs[0][...])


def add_norm_kernel(a, b, c, d, x_ref, gain_ref, mid_ref, low_ref):
    mid = x_ref[...].astype(F32) + total_of((a, b, c, d))
    mid_ref[...] = mid
    low_ref[...] = (mid * rms(mid) * gain_ref[...]).astype(BF16)


def add_kernel(a, b, c, d, mid_ref, y_ref):
    y_ref[...] = (mid_ref[...] + total_of((a, b, c, d))).astype(BF16)


def norm_back_kernel(a, b, c, d, after_ref, x_ref, gain_ref, dx_ref, low_ref, gain_grad_ref):
    grad = total_of((a, b, c, d))
    x = x_ref[...].astype(F32)
    r = rms(x)
    n = x * r
    gain_grad_ref[...] = jnp.sum(grad * n, axis=0, keepdims=True)
    scaled = grad * gain_ref[...]
    dx = after_ref[...].astype(F32) + r * (
        scaled - n * jnp.mean(scaled * n, axis=-1, keepdims=True)
    )
    dx_ref[...] = dx
    low_ref[...] = dx.astype(BF16)


def qkv_kernel(place, *refs, parts):
    pieces, packs, refs = refs[:8], refs[8 : 8 + parts], refs[8 + parts :]
    cos_ref, sin_ref, x_ref, a_ref, q_ref, kv_ref, ga_ref, gf_ref, *refs = refs
    w_ref, gains_ref, x_sems, w_sems, g_sems = refs
    rows_there = fetch(pieces, x_ref, x_sems)
    n = w_ref.shape[0] // 8

    def gain_copy(i, pack, row, block):
        return pltpu.make_async_copy(
            pack.at[pl.ds(row + n, GAIN_ROWS), pl.ds(0, n)], gains_ref.at[block], g_sems.at[i]
        )

    for i in range(8):
        gain_copy(i, *block_of(packs, place, i)).start()
    weights_there = fetch_blocks(packs, place, 0, w_ref, w_sems)
    for i in range(8):
        pack, row, _ = block_of(packs, place, i)
        gain_copy(i, pack, row, i).wait()
    gains = jnp.concatenate([gains_ref[i] for i in range(8)], axis=1).astype(F32)
    ga_ref[...] = gains[0:1, :]
    gf_ref[...] = gains[1:2, :]
    rows_there()
    x = x_ref[...].astype(F32)
    a = (x * rms(x) * ga_ref[...]).astype(BF16)
    a_ref[...] = a
    weights_there()
    out = rope(nn(a, w_ref[...]), cos_ref[...], sin_ref[...])
    width = q_ref.shape[1]
    q_ref[...] = (out[:, :width].astype(BF16).astype(F32) * HD**-0.5).astype(BF16)
    half = out.shape[0] // 2
    k, v = out[:, width : width + HD], out[:, width + HD :]
    keys = jnp.concatenate([k[:half], k[half:]], axis=1)
    values = jnp.concatenate([v[half:], v[:half]], axis=1)
    kv_ref[...] = jnp.where(place[CORE] == 1, values, keys).astype(BF16)


def key_step(ref, t):
    per = ref.shape[0] // KEYS_STEP
    return pl.ds(t % per * KEYS_STEP, KEYS_STEP), slice(t // per * HD, (t // per + 1) * HD)


def attend_kernel(place, q_ref, own_ref, other_ref, bias_ref, *refs, parts):
    packs, refs = refs[:parts], refs[parts:]
    o_ref, lse_ref, k_ref, v_ref, send_ref, mine_ref, s_ref, w_ref, sems = refs
    weights_there = fetch_blocks(packs, place, packs[0].shape[1] - w_ref.shape[1], w_ref, sems)
    odd = place[CORE] == 1
    k_ref[...] = jnp.where(odd, other_ref[...], own_ref[...])
    v_ref[...] = jnp.where(odd, own_ref[...], other_ref[...])
    rows, width = q_ref.shape
    heads = width // HD
    steps = 2 * k_ref.shape[0] // KEYS_STEP
    tops = [jnp.full((1, rows), MASKED, F32) for _ in range(heads)]
    for t in range(steps):
        at = pl.ds(t * KEYS_STEP, KEYS_STEP)
        part, cols = key_step(k_ref, t)
        k = k_ref[part, cols]
        bias = bias_ref[at, :]
        for h in range(heads):
            s = nt(k, q_ref[:, h * HD : (h + 1) * HD]) + bias
            s_ref[h, at, :] = s
            tops[h] = jnp.maximum(tops[h], jnp.max(s, axis=0, keepdims=True))
    sums = [jnp.zeros((1, rows), F32) for _ in range(heads)]
    outs = [jnp.zeros((HD, rows), F32) for _ in range(heads)]
    for t in range(steps):
        at = pl.ds(t * KEYS_STEP, KEYS_STEP)
        part, cols = key_step(v_ref, t)
        v_t = v_ref[part, :].T[cols, :]
        for h in range(heads):
            e = jnp.exp(s_ref[h, at, :] - tops[h])
            sums[h] = sums[h] + jnp.sum(e, axis=0, keepdims=True)
            outs[h] = outs[h] + nn(v_t, e.astype(BF16))
    flat = jnp.concatenate([outs[h] / sums[h] for h in range(heads)], axis=0)
    o_ref[...] = flat.T.astype(BF16)
    lse_ref[...] = jnp.concatenate([tops[h] + jnp.log(sums[h]) for h in range(heads)], axis=0)
    weights_there()
    halves_out(nt(o_ref[...], w_ref[...]), send_ref, mine_ref)


def ffn_kernel(*refs):
    pieces, w_hbm, refs = refs[:8], refs[8], refs[9:]
    b_ref, gu_ref, h_ref, send_ref, mine_ref, gu_w, down_w, b_sems, gu_sems, sem = refs
    rows_there = fetch(pieces, b_ref, b_sems)
    steps, n, c = 4, w_hbm.shape[0] // 4, gu_w.shape[1]

    def load(i):
        at = pl.ds(i * n, n)
        return pltpu.make_async_copy(w_hbm.at[at, pl.ds(0, c)], gu_w.at[at, :], gu_sems.at[i])

    for i in range(steps):
        load(i).start()
    down = pltpu.make_async_copy(w_hbm.at[:, pl.ds(c, down_w.shape[1])], down_w, sem)
    down.start()
    rows_there()
    for i in range(steps):
        load(i).wait()
        at = slice(i * n, (i + 1) * n)
        part = nn(b_ref[:, at], gu_w[at, :])
        gu_ref[...] = part if i == 0 else gu_ref[...] + part
    units = gu_ref.shape[1] // 2
    gate, up = gu_ref[:, :units], gu_ref[:, units:]
    h_ref[:, :units] = (gate / (1.0 + jnp.exp(-gate)) * up).astype(BF16)
    spare = h_ref.shape[1] - units
    h_ref[:, units:] = jnp.zeros((h_ref.shape[0], spare), BF16)
    down.wait()
    halves_out(nt(h_ref[...], down_w[...]), send_ref, mine_ref)


def ffn_back_kernel(*refs):
    pieces, w_hbm, act_hbm, refs = refs[:8], refs[8], refs[9], refs[10:]
    dff_ref, dgu_ref, send_ref, mine_ref, gu_w, down_w, gu_ref, r_sems, gu_sems = refs
    rows_there = fetch(pieces, dff_ref, r_sems)
    c = gu_w.shape[1]
    down = pltpu.make_async_copy(w_hbm.at[:, pl.ds(c, down_w.shape[1])], down_w, gu_sems.at[2])
    down.start()
    act = pltpu.make_async_copy(act_hbm, gu_ref, gu_sems.at[0])
    act.start()
    load = pltpu.make_async_copy(w_hbm.at[:, pl.ds(0, c)], gu_w, gu_sems.at[1])
    load.start()
    rows_there()
    down.wait()
    units = gu_ref.shape[1] // 2
    dh = nn(dff_ref[...], down_w[...])[:, :units]
    act.wait()
    gate, up = gu_ref[:, :units], gu_ref[:, units:]
    sig = 1.0 / (1.0 + jnp.exp(-gate))
    dgate = dh * up * (sig * (1.0 + gate * (1.0 - sig)))
    dgu_ref[...] = jnp.concatenate([dgate, dh * (gate * sig)], axis=1).astype(BF16)
    load.wait()
    halves_out(nt(dgu_ref[...], gu_w[...]), send_ref, mine_ref)


def attend_back_kernel(place, *refs, parts):
    pieces, packs, refs = refs[:8], refs[8 : 8 + parts], refs[8 + parts :]
    q_ref, k_ref, v_ref, bias_ref, o_ref, lse_ref, cos_ref, sin_ref, *refs = refs
    dattn_ref, dq_ref, own_ref, send_ref, w_ref, do_ref, dk_ref, dv_ref, sems, r_sems = refs
    rows_there = fetch(pieces, dattn_ref, r_sems)
    weights_there = fetch_blocks(packs, place, packs[0].shape[1] - w_ref.shape[1], w_ref, sems)
    rows, width = q_ref.shape
    heads = width // HD
    steps = 2 * k_ref.shape[0] // KEYS_STEP
    rows_there()
    weights_there()
    do = nn(dattn_ref[...], w_ref[...])
    do_ref[...] = do.astype(BF16)
    both = (do_ref[...].astype(F32) * o_ref[...].astype(F32)).T
    deltas = [
        jnp.sum(both[h * HD : (h + 1) * HD, :], axis=0, keepdims=True) for h in range(heads)
    ]
    dq_t = [jnp.zeros((HD, rows), F32) for _ in range(heads)]
    for t in range(steps):
        at = pl.ds(t * KEYS_STEP, KEYS_STEP)
        part, cols = key_step(k_ref, t)
        k = k_ref[part, cols]
        v = v_ref[part, cols]
        k_t = k_ref[part, :].T[cols, :]
        bias = bias_ref[at, :]
        dk = jnp.zeros((KEYS_STEP, HD), F32)
        dv = jnp.zeros((KEYS_STEP, HD), F32)
        for h in range(heads):
            q_h = q_ref[:, h * HD : (h + 1) * HD]
            do_h = do_ref[:, h * HD : (h + 1) * HD]
            p = jnp.exp(nt(k, q_h) + bias - lse_ref[h : h + 1, :])
            ds = (p * (nt(v, do_h) - deltas[h])).astype(BF16)
            dv = dv + nn(p.astype(BF16), do_h)
            dk = dk + nn(ds, q_h)
            dq_t[h] = dq_t[h] + nn(k_t, ds)
        dk_ref[part, cols] = dk
        dv_ref[part, cols] = dv
    dq = jnp.concatenate(dq_t, axis=0).T * HD**-0.5
    dq_ref[...] = rope_back(dq, cos_ref[:, :width], sin_ref[:, :width]).astype(BF16)
    odd = place[CORE] == 1
    own_ref[...] = jnp.where(odd, dv_ref[...], dk_ref[...])
    send_ref[...] = jnp.where(odd, dk_ref[...], dv_ref[...]).astype(BF16)


def kv_add_kernel(own_ref, other_ref, out_ref):
    out_ref[...] = (own_ref[...] + other_ref[...].astype(F32)).astype(BF16)


def qkv_back_kernel(place, *refs, parts):
    packs, (x_hbm, dq_ref, kv_ref, cos_ref, sin_ref, *refs) = refs[:parts], refs[parts:]
    dqkv_ref, send_ref, mine_ref, gain_grad_ref, w_ref, x_ref, sems, x_sem = refs
    weights_there = fetch_blocks(packs, place, 0, w_ref, sems)
    rows_there = pltpu.make_async_copy(x_hbm, x_ref, x_sem)
    rows_there.start()
    width, odd = dq_ref.shape[1], place[CORE] == 1
    both = sum((kv_ref[i].astype(F32) for i in range(1, 8)), kv_ref[0].astype(F32))
    first, second = both[:, :HD], both[:, HD:]
    dk = jnp.concatenate([first, second], axis=0)
    dv = jnp.concatenate([second, first], axis=0)
    spare = jnp.zeros_like(dk)
    dkv = jnp.where(
        odd, jnp.concatenate([spare, dv], axis=1), jnp.concatenate([dk, spare], axis=1)
    )
    dkv = rope_back(dkv, cos_ref[:, width:], sin_ref[:, width:])
    dqkv_ref[:, :width] = dq_ref[...]
    dqkv_ref[:, width:] = dkv.astype(BF16)
    weights_there()
    da = nt(dqkv_ref[...], w_ref[...])
    halves_out(da, send_ref, mine_ref)
    rows_there.wait()
    x = x_ref[...].astype(F32)
    gain_grad_ref[...] = jnp.sum(da * (x * rms(x)), axis=0, keepdims=True)


def ffn_product_kernel(b_ref, dgu_ref, dff_ref, h_ref, out, whole, sems):
    n, steps = dgu_ref.shape[1], sems.shape[0]
    rows = whole.shape[0] // steps
    copies = []
    for i in range(steps):
        at = slice(i * rows, (i + 1) * rows)
        whole[at, :n] = tn(b_ref[:, at], dgu_ref[...]).astype(BF16)
        whole[at, n:] = tn(dff_ref[:, at], h_ref[...]).astype(BF16)
        here = pl.ds(i * rows, rows)
        copies.append(pltpu.make_async_copy(whole.at[here, :], out.at[here, :], sems.at[i]))
        copies[-1].start()
    for c in copies:
        c.wait()


def ffn_products(b, dgu, dff, hidden):
    dims = (b.shape[1], dgu.shape[1] + hidden.shape[1])
    return call(
        ffn_product_kernel,
        [pltpu.HBM(dims, BF16)],
        [(b, dgu, dff, hidden)],
        [pltpu.VMEM(dims, BF16), DMA((8,))],
        room=14,
        moved=20_000_000,
        out_spec=HBM,
    )[0]


def attn_product_kernel(dattn, a, gg_a, gg_f, ctx, dqkv, *refs, layer):
    *_, out, whole, sems = refs
    cols = pl.ds(layer * whole.shape[1], whole.shape[1])
    m, steps = ctx.shape[1], sems.shape[0]
    wide = m + dqkv.shape[1]
    rows = whole.shape[0] // steps
    row = lax.broadcasted_iota(jnp.int32, (whole.shape[1] - wide, rows), 0)
    copies = []
    for i in range(steps):
        at = slice(i * rows, (i + 1) * rows)
        whole[at, :m] = tn(dattn[:, at], ctx[...]).astype(BF16)
        whole[at, m:wide] = tn(a[:, at], dqkv[...]).astype(BF16)
        ga, gf = (jnp.broadcast_to(g[:, at], row.shape) for g in (gg_a, gg_f))
        gains = jnp.where(row == 0, ga, jnp.where(row == 1, gf, 0.0))
        whole[at, wide:] = gains.T.astype(BF16)
        here = pl.ds(i * rows, rows)
        copies.append(pltpu.make_async_copy(whole.at[here, :], out.at[here, cols], sems.at[i]))
        copies[-1].start()
    for c in copies:
        c.wait()


def attn_products(dattn, ctx, a, dqkv, gg_a, gg_f, layer, filled=None):
    d, wide = a.shape[1], ctx.shape[1] + dqkv.shape[1] + 128
    args = [(dattn, a, gg_a, gg_f, ctx, dqkv)]
    return call(
        functools.partial(attn_product_kernel, layer=layer),
        [pltpu.HBM((d, 2 * wide), BF16)],
        args if filled is None else args + [[filled]],
        [pltpu.VMEM((d, wide), BF16), DMA((4,))],
        room=14,
        out_spec=HBM,
        moved=12_000_000,
        aliases=None if filled is None else {6: 0},
    )[0]


def y_split_both_kernel(place, r_ref, keep_ref, near_ref, far_ref, straight_ref):
    n, c = keep_ref.shape
    here = pl.ds(pl.multiple_of(place[YLO] * n, n), n)
    there = pl.ds(pl.multiple_of((1 - place[YLO]) * n, n), n)

    def fill(mine, other):
        keep_ref[...] = r_ref[here, mine]
        near_ref[...] = r_ref[there, mine]
        straight_ref[...] = r_ref[here, other]
        far_ref[...] = r_ref[there, other]

    @pl.when(place[SECTION] == 0)
    def _():
        fill(slice(0, c), slice(c, 2 * c))

    @pl.when(place[SECTION] == 1)
    def _():
        fill(slice(c, 2 * c), slice(0, c))


def reduce_y_both(r, place):
    dims = (r.shape[0] // 2, r.shape[1] // 2)
    keep, near, far, straight = call(
        y_split_both_kernel, [held(dims)] * 4, [place, (r,)], room=16
    )
    return [keep, swap_ylo(near), swap_across(far), swap_section(straight)]


def y_split_kernel(place, r0_ref, r1_ref, keep_ref, near_ref, far_ref, straight_ref):
    n = keep_ref.shape[0]
    here = pl.ds(pl.multiple_of(place[YLO] * n, n), n)
    there = pl.ds(pl.multiple_of((1 - place[YLO]) * n, n), n)

    def fill(mine, other):
        keep_ref[...] = mine[here, :]
        near_ref[...] = mine[there, :]
        straight_ref[...] = other[here, :]
        far_ref[...] = other[there, :]

    @pl.when(place[SECTION] == 0)
    def _():
        fill(r0_ref, r1_ref)

    @pl.when(place[SECTION] == 1)
    def _():
        fill(r1_ref, r0_ref)


def by_core_kernel(place, *refs):
    *parts, own_ref, send_ref = refs
    n = own_ref.shape[0]
    here = pl.ds(pl.multiple_of(place[CORE] * n, n), n)
    there = pl.ds(pl.multiple_of((1 - place[CORE]) * n, n), n)
    own_ref[...] = sum(p[here, :].astype(F32) for p in parts)
    send_ref[...] = sum(p[there, :].astype(F32) for p in parts).astype(BF16)


def by_core(parts, place):
    n, c = parts[0].shape[0] // 2, parts[0].shape[1]
    own, send = call(
        by_core_kernel, [held((n, c), F32), shape((n, c))], [place, tuple(parts)], room=16
    )
    return own, swap_core(send)


def reduce_y(r0, r1, place):
    n, c = r0.shape[0] // 2, r0.shape[1]
    keep, near, far, straight = call(y_split_kernel, [held((n, c))] * 4, [place, (r0, r1)], room=16)
    return [keep, swap_ylo(near), swap_across(far), swap_section(straight)]


def ordered(odd, own, other):
    other = other.astype(F32)
    return jnp.concatenate(
        [jnp.where(odd, other, own), jnp.where(odd, own, other)], axis=1
    )


def attn_grads_kernel(place, own_ref, other_ref, o_ref, q_ref, k_ref, v_ref, *gain_refs):
    odd = place[CORE] == 1
    m = n = q_ref.shape[1] // 2
    own, other = own_ref[:, :m].T, other_ref[:, :m].astype(F32).T
    o_ref[:m, :] = jnp.where(odd, other, own)
    o_ref[m:, :] = jnp.where(odd, own, other)
    q_ref[...] = ordered(odd, own_ref[:, m : m + n], other_ref[:, m : m + n])
    both = own_ref[:, m + n :] + other_ref[:, m + n :].astype(F32)
    kv = both[:, : 2 * HD].T
    k_ref[...] = kv[:HD, :]
    v_ref[...] = kv[HD:, :]
    rows = gain_refs[0].shape[0]
    gain_refs[-1][...] = both[:, 2 * HD :]
    for k, ref in enumerate(gain_refs[:-1]):
        at = lax.rem(place[TP] + k, 4) * rows
        ref[...] = gain_refs[-1][pl.ds(pl.multiple_of(at, rows), rows), :]


def ffn_grads_kernel(place, own_ref, other_ref, gate_ref, up_ref, down_ref):
    odd = place[CORE] == 1
    n = gate_ref.shape[1] // 2
    gate_ref[...] = ordered(odd, own_ref[:, :n], other_ref[:, :n])
    up_ref[...] = ordered(odd, own_ref[:, n : 2 * n], other_ref[:, n : 2 * n])
    own, other = own_ref[:, 2 * n :].T[:n], other_ref[:, 2 * n :].astype(F32).T[:n]
    down_ref[:n, :] = jnp.where(odd, other, own)
    down_ref[n:, :] = jnp.where(odd, own, other)


def body(
    block_input,
    out_grad,
    seg_ids,
    attn_gain,
    w_query,
    w_key,
    w_value,
    w_out,
    ffn_gain,
    w_gate,
    w_up,
    w_down,
):
    at = {name: lax.axis_index(name) for name in AXES}
    section, core, tp = at["section"], at["core"], at["tp"]
    place = jnp.stack([at[name] for name in AXES]).astype(jnp.int32)
    d = block_input.shape[2]
    micro_rows = block_input.shape[1]
    group = 8 * micro_rows
    q_width = w_query.shape[2] // 2
    units = w_gate.shape[2] // 2
    own_rows = w_query.shape[1]

    padded = units + (-units) % 128
    attn_dims = (own_rows + GAIN_ROWS, 2 * q_width + 2 * HD)
    attn_own, attn_send = call(
        pack_attn_kernel,
        [shape(attn_dims)] * 2,
        [place, (w_query[0], w_key[0].T, w_value[0].T, w_out[0], attn_gain, ffn_gain)],
    )
    attn_shard = call(
        chip_attn_kernel,
        [held((2 * own_rows + GAIN_ROWS, attn_dims[1]))],
        [place, (attn_own, swap_core(attn_send))],
    )[0]
    ffn_own, ffn_send = call(
        pack_ffn_kernel,
        [shape((own_rows, 2 * units + padded))] * 2,
        [place, (w_down[0], w_gate[0], w_up[0])],
        room=16,
    )
    ffn_shard = chip_rows(place, ffn_own, swap_core(ffn_send))
    attn_y = y_exchange(after(attn_shard, ffn_shard))
    attn_pairs = pairs(place, attn_shard, attn_y)
    attn0 = [attn_pairs[0]] + [from_x(attn_pairs[0], k) for k in (1, 2, 3)]
    attn1 = [gather_x(attn_pairs[1])]
    ffn_y = y_exchange_on(after(ffn_shard, *attn_y))

    block = at["x"] * 2 + at["ylo"]
    seg_row = lax.dynamic_index_in_dim(seg_ids, section, 0, keepdims=False)
    def arranged(row):
        v = row.reshape(8, 2, 4, micro_rows)
        return lax.dynamic_slice_in_dim(jnp.concatenate([v, v], axis=2), tp, 4, 2)

    def keys_of(row):
        return arranged(row).transpose(1, 0, 2, 3).reshape(-1)

    def queries_of(row):
        v = lax.dynamic_index_in_dim(arranged(row), block, 0, keepdims=False)
        return jnp.where(core == 0, v, v[::-1]).reshape(-1)

    places = jnp.arange(seg_row.shape[0], dtype=jnp.int32)
    k_pos, k_seg = keys_of(places), keys_of(seg_row)
    q_pos, q_seg = queries_of(places), queries_of(seg_row)
    seen = (k_pos[:, None] <= q_pos[None, :]) & (k_seg[:, None] == q_seg[None, :])
    bias = jnp.where(seen, 0.0, MASKED).astype(F32)

    frequency = 10000.0 ** (-jnp.arange(0, HD, 2, dtype=F32) / HD)
    angles = q_pos.astype(F32)[:, None] * frequency[None, :]
    wide = q_width + 2 * HD
    plain = lax.broadcasted_iota(jnp.int32, (group, wide), 1) >= q_width + HD
    cos, sin = (jnp.concatenate([t] * 12, axis=1) for t in (jnp.cos(angles), jnp.sin(angles)))
    cos, sin = jnp.where(plain, 1.0, cos), jnp.where(plain, 0.0, sin)

    rows_low = shape((micro_rows, d))
    rows_f32 = shape((micro_rows, d), F32)
    mid_outs = [rows_f32, rows_low]
    partials = [shape((group // 2, d)), shape((group // 2, d), F32)]
    heads, keys = q_width // HD, seg_row.shape[0]
    gain_row = shape((1, d), F32)

    def project(x, packs):
        return call(
            functools.partial(qkv_kernel, parts=len(packs)),
            [held((group, d))] * 2
            + [shape((group, q_width)), shape((group // 2, 2 * HD))]
            + [gain_row, gain_row],
            [place, gather_rows(x) + packs, cos, sin],
            [
                pltpu.VMEM((d, wide), BF16),
                pltpu.VMEM((8, GAIN_ROWS, d // 8), BF16),
                DMA((8,)),
                DMA((8,)),
                DMA((8,)),
            ],
            room=18,
        )

    both_kv = held((keys // 2, 2 * HD))

    def attention(q, kv, packs):
        return call(
            functools.partial(attend_kernel, parts=len(packs)),
            [held((group, q_width)), held((heads, group), F32), both_kv, both_kv, *partials],
            [place, q, *kv, bias, packs],
            [
                pltpu.VMEM((heads, keys, group), F32),
                pltpu.VMEM((d, q_width), BF16),
                DMA((8,)),
            ],
            room=12,
        )

    def feed_forward(b, w_ffn):
        return call(
            ffn_kernel,
            [held((group, d)), held((group, 2 * units), F32), held((group, padded)), *partials],
            [[*gather_rows(b), w_ffn]],
            [
                pltpu.VMEM((d, 2 * units), BF16),
                pltpu.VMEM((d, padded), BF16),
                DMA((8,)),
                DMA((4,)),
                DMA,
            ],
            room=16,
        )

    def backward(dy, kept, layer, filled=None, pending=()):
        x, rows, a, q, k, v, ctx, lse, mid, b, gu, hidden, gain_a, gain_f, w_ffn, packs = kept
        dff, dgu, send, mine = call(
            ffn_back_kernel,
            [held((group, d)), held((group, 2 * units)), *partials],
            [[*gather_rows(dy), w_ffn, gu]],
            [
                pltpu.VMEM((d, 2 * units), BF16),
                pltpu.VMEM((d, padded), BF16),
                pltpu.VMEM((group, 2 * units), F32),
                DMA((8,)),
                DMA((3,)),
            ],
            room=16,
        )
        g_ffn = ffn_products(b, dgu, dff, hidden)
        dmid, dattn, gg_f = call(
            norm_back_kernel,
            [rows_f32, rows_low, held((1, d), F32)],
            [*reduce_rows(send, mine), dy, mid, gain_f],
        )
        dattn = after(dattn, g_ffn, *pending)
        dattn, dq, dkv, dkv_send = call(
            functools.partial(attend_back_kernel, parts=len(packs)),
            [
                held((group, d)),
                shape((group, q_width)),
                shape((keys // 2, 2 * HD), F32),
                shape((keys // 2, 2 * HD)),
            ],
            [place, gather_rows(dattn) + packs, (q, k, v), bias, (ctx, lse), cos, sin],
            [
                pltpu.VMEM((d, q_width), BF16),
                pltpu.VMEM((group, q_width), BF16),
                pltpu.VMEM((keys // 2, 2 * HD), F32),
                pltpu.VMEM((keys // 2, 2 * HD), F32),
                DMA((8,)),
                DMA((8,)),
            ],
            room=18,
        )
        dkv = call(kv_add_kernel, [shape(dkv.shape)], [dkv, swap_core(dkv_send)])[0]
        arrived = lax.all_to_all(
            dkv.reshape(8, group // 2, 2 * HD), ("x", "ylo"), 0, 0, tiled=True
        )
        dqkv, send, mine, gg_a = call(
            functools.partial(qkv_back_kernel, parts=len(packs)),
            [held((group, wide)), *partials, held((1, d), F32)],
            [place, packs + [rows], dq, arrived, cos, sin],
            [pltpu.VMEM((d, wide), BF16), pltpu.VMEM((group, d), BF16), DMA((8,)), DMA],
            room=16,
        )
        g_attn = attn_products(dattn, ctx, a, dqkv, gg_a, gg_f, layer, filled)
        dx, dx_low, _ = call(
            norm_back_kernel,
            [rows_f32, rows_low, held((1, d), F32)],
            [*reduce_rows(send, mine), dmid, x, gain_a],
        )
        return dx, after(dx_low, g_attn), g_attn, g_ffn, dqkv

    x0 = lax.dynamic_index_in_dim(block_input, section, 0, keepdims=False)
    dy1 = lax.dynamic_index_in_dim(out_grad, section, 0, keepdims=False)

    rows0, a0, q0, kv0, ga0, gf0 = project(x0, attn0)
    ffn_pairs = pairs(place, ffn_shard, ffn_y)
    w_ffn0 = gather_x(after(ffn_pairs[0], *attn0[1:], *attn1))
    kv0 = gather_kv(kv0)
    ctx0, lse0, k0, v0, send, mine = attention(q0, kv0, attn0)
    mid0, b = call(add_norm_kernel, mid_outs, [*reduce_rows(send, mine), x0, gf0])
    w_ffn1 = gather_x(after(ffn_pairs[1], b))
    b0, up0, hidden0, send, mine = feed_forward(b, w_ffn0)
    y0 = call(add_kernel, [rows_low], [*reduce_rows(send, mine), mid0])[0]
    kept0 = (x0, rows0, a0, q0, k0, v0, ctx0, lse0, mid0, b0, up0, hidden0, ga0, gf0, w_ffn0, attn0)
    rows1, a1, q1, kv1, ga1, gf1 = project(y0, attn1)
    ctx1, lse1, k1, v1, send, mine = attention(q1, gather_kv(kv1), attn1)
    mid1, b = call(add_norm_kernel, mid_outs, [*reduce_rows(send, mine), y0, gf1])
    b1, up1, hidden1, send, mine = feed_forward(b, w_ffn1)
    last = (send, mine, mid1)
    kept1 = (y0, rows1, a1, q1, k1, v1, ctx1, lse1, mid1, b1, up1, hidden1, ga1, gf1, w_ffn1, attn1)

    early = section == 0

    def both_micros(layer0, layer1, dtype):
        mine = jnp.where(early, layer0, layer1).astype(dtype)
        other = jnp.where(early, layer1, layer0).astype(BF16)
        other = swap_section(other).astype(dtype)
        return jnp.stack([jnp.where(early, mine, other), jnp.where(early, other, mine)])[None]

    dx1, dx1_low, g_attn1, g_ffn1, _ = backward(dy1, kept1, 1)
    ffn1 = reduce_x(g_ffn1)
    dx0, dx0_low, g_attn, g_ffn0, dqkv0 = backward(dx1_low, kept0, 0, g_attn1, [ffn1])
    send, mine, mid1 = last
    y1 = call(add_kernel, [rows_low], [*reduce_rows(after(send, dqkv0), mine), mid1])[0]
    block_output = both_micros(y0, y1, BF16)
    input_grad = both_micros(dx0, dx1, F32)
    ffn_y = reduce_y(after(reduce_x(g_ffn0), input_grad, block_output), ffn1, place)

    attn_y = reduce_y_both(reduce_x(g_attn), place)
    ffn_parts = by_core([after(ffn_y[0], attn_y[0]), *ffn_y[1:]], place)

    def finish(kernel, dims, parts):
        return call(kernel, [held(s, F32) for s in dims], [place, parts], room=20)

    own = own_rows
    grad_gate, grad_up, grad_down = finish(
        ffn_grads_kernel, [(own, 2 * units)] * 2 + [(2 * units, own)], ffn_parts
    )
    attn_parts = by_core(attn_y, place)
    grad_out, grad_query, grad_key, grad_value, *gain_pieces, _ = finish(
        attn_grads_kernel,
        [(2 * q_width, own), (own, 2 * q_width), (HD, own), (HD, own)]
        + [(micro_rows, 128)] * 4
        + [(own, 128)],
        attn_parts,
    )
    gain_sums = gain_pieces[0]
    for k in (1, 2, 3):
        gain_sums = gain_sums + from_z(gain_pieces[k], -k)
    gain_sums = gain_sums[:, :2].T


    return (
        block_output,
        input_grad,
        gain_sums[0][None],
        grad_query[None],
        grad_key.T[None],
        grad_value.T[None],
        grad_out[None],
        gain_sums[1][None],
        grad_gate[None],
        grad_up[None],
        grad_down[None],
    )


def solution(mesh):
    fine = Mesh(mesh.devices.reshape(2, 4, 2, 2, 4), AXES)
    wide = ("x", "ylo", "core")
    rows = P(None, (*wide, "tp"), None)
    into = P("section", wide, "tp")
    out_of = P("section", "tp", wide)
    grown = P("section", None, (*wide, "tp"), None)
    gain_grad = P("section", (*wide, "tp"))
    return jax.shard_map(
        body,
        mesh=fine,
        in_specs=(
            rows, rows, P(), P("section", wide), into, into, into, out_of,
            P("section", wide), into, into, out_of,
        ),
        out_specs=(
            grown, grown, gain_grad, into, into, into, out_of, gain_grad, into, into, out_of,
        ),
        check_vma=False,
    )
```

```python
import functools
import math

import jax
import jax.numpy as jnp
from jax import lax
from jax.experimental import pallas as pl
from jax.experimental.pallas import tpu as pltpu
from jax.sharding import Mesh, PartitionSpec as P

HD = 64
GAIN_ROWS = 16
EPS = 1e-05
MASKED = -1e30
KEYS_STEP = 512
AXES = ("section", "x", "ylo", "core", "tp")
SECTION, X, YLO, CORE, TP = range(5)
BF16 = jnp.bfloat16
F32 = jnp.float32
VMEM = pl.BlockSpec(memory_space=pltpu.VMEM)
SMEM = pl.BlockSpec(memory_space=pltpu.SMEM)
HBM = pl.BlockSpec(memory_space=pltpu.HBM)
DMA = pltpu.SemaphoreType.DMA


def nn(a, b):
    return jnp.dot(a, b, preferred_element_type=F32)


def nt(a, b):
    return lax.dot_general(a, b, (((1,), (1,)), ((), ())), preferred_element_type=F32)


def tn(a, b):
    return lax.dot_general(a, b, (((0,), (0,)), ((), ())), preferred_element_type=F32)


def shape(dims, dtype=BF16):
    return jax.ShapeDtypeStruct(tuple(dims), dtype)


SHORT = pl.CostEstimate(flops=1, bytes_accessed=1, transcendentals=0)


def held(dims, dtype=BF16):
    return pltpu.HBM(tuple(dims), dtype)


def pinned(v):
    return pltpu.with_memory_space_constraint(v, pltpu.HBM)


def call(kernel, outs, args, scratch=(), room=8, out_spec=None, moved=0, aliases=None):
    specs, values = [], []
    for a in args:
        if isinstance(a, (list, tuple)):
            specs += [HBM if isinstance(a, list) else pl.BlockSpec()] * len(a)
            values += [pinned(v) for v in a]
        else:
            specs.append(SMEM if a.dtype == jnp.int32 else VMEM)
            values.append(a)
    mine = [m for m in scratch if isinstance(m, type(pltpu.VMEM((8, 128), F32)))]
    room = room * 2**20 + sum(
        math.prod(m.shape) * jnp.dtype(m.dtype).itemsize for m in mine if m.dtype in (BF16, F32)
    )
    return pl.pallas_call(
        kernel,
        out_shape=tuple(outs),
        in_specs=specs,
        out_specs=tuple(
            VMEM if isinstance(o, jax.ShapeDtypeStruct) else out_spec or pl.BlockSpec() for o in outs
        ),
        scratch_shapes=list(scratch),
        input_output_aliases=aliases or {},
        compiler_params=pltpu.CompilerParams(vmem_limit_bytes=room),
        cost_estimate=pl.CostEstimate(flops=moved, bytes_accessed=moved, transcendentals=0)
        if moved
        else SHORT,
        name=getattr(kernel, "func", kernel).__name__,
    )(*values)


def from_z(rows, by):
    return lax.ppermute(rows, "tp", [((i + by) % 4, i) for i in range(4)])


def from_x(v, by):
    return lax.ppermute(v, "x", [((i + by) % 4, i) for i in range(4)])


def swap_core(v):
    return lax.ppermute(v, "core", [(0, 1), (1, 0)])


def swap_ylo(v):
    return lax.ppermute(v, "ylo", [(0, 1), (1, 0)])


def swap_section(v):
    return lax.ppermute(v, "section", [(0, 1), (1, 0)])


def swap_across(v):
    return lax.ppermute(v, ("section", "ylo"), [(0, 3), (3, 0), (1, 2), (2, 1)])


def after(value, *others):
    return lax.optimization_barrier((value, *others))[0]


def y_exchange(v):
    return swap_ylo(v), swap_across(v), swap_section(v)


def y_exchange_on(v):
    near, far = swap_ylo(v), swap_across(v)
    n = v.shape[0] // 2
    return near, far, swap_ylo(far[:n]), swap_across(near[n:])


def gather_rows(rows):
    pieces = [rows] + [from_z(rows, k) for k in (1, 2, 3)]
    return pieces + [swap_core(p) for p in pieces]


def gather_kv(half):
    copies = jnp.broadcast_to(half[None], (8, *half.shape))
    own = lax.all_to_all(copies, ("x", "ylo"), 0, 0, tiled=True).reshape(-1, half.shape[1])
    return own, swap_core(own)


def reduce_rows(send, mine):
    own, *pieces = split(mine, swap_core(send))
    return [own] + [from_z(p, -k) for k, p in zip((1, 2, 3), pieces)]


def gather_x(block):
    return lax.all_gather(block, "x", axis=0, tiled=True)


def reduce_x(grad):
    return lax.psum_scatter(grad, "x", scatter_dimension=0, tiled=True)


def pack_attn_kernel(place, q_ref, k_ref, v_ref, o_ref, ga_ref, gf_ref, own_ref, send_ref):
    n, rows = q_ref.shape[1] // 2, q_ref.shape[0]
    m = n + 2 * HD
    kv = jnp.concatenate([k_ref[...], v_ref[...]], axis=0).T
    o = o_ref[...].T
    odd = place[CORE] == 1
    row = lax.broadcasted_iota(jnp.int32, (GAIN_ROWS, ga_ref.shape[1]), 0)
    ga, gf = (jnp.broadcast_to(g[...].astype(F32), row.shape) for g in (ga_ref, gf_ref))
    gains = jnp.where(row == 0, ga, jnp.where(row == 1, gf, 0.0)).astype(BF16)
    rest = jnp.zeros((GAIN_ROWS, own_ref.shape[1] - gains.shape[1]), BF16)
    for ref, high in ((own_ref, odd), (send_ref, jnp.logical_not(odd))):
        ref[:rows, :n] = jnp.where(high, q_ref[:, n:], q_ref[:, :n])
        ref[:rows, n:m] = kv
        ref[:rows, m:] = jnp.where(high, o[:, n:], o[:, :n])
        ref[rows:, :] = jnp.concatenate([gains, rest], axis=1)


def pack_ffn_kernel(place, d_ref, g_ref, u_ref, own_ref, send_ref):
    odd = place[CORE] == 1
    d = d_ref[...].T
    n = d.shape[1] // 2
    spare = jnp.zeros((own_ref.shape[0], own_ref.shape[1] - 3 * n), BF16)
    low, high = (
        jnp.concatenate([w[:, at] for w in (g_ref[...], u_ref[...], d)] + [spare], axis=1)
        for at in (slice(0, n), slice(n, 2 * n))
    )
    own_ref[...] = jnp.where(odd, high, low)
    send_ref[...] = jnp.where(odd, low, high)


def chip_rows_kernel(place, own_ref, other_ref, out_ref):
    n = own_ref.shape[0]
    core = place[CORE]
    out_ref[pl.ds(pl.multiple_of(core * n, n), n), :] = own_ref[...]
    out_ref[pl.ds(pl.multiple_of((1 - core) * n, n), n), :] = other_ref[...]


def chip_rows(place, own, other):
    n, c = own.shape
    return call(chip_rows_kernel, [held((2 * n, c))], [place, (own, other)], room=12)[0]


def chip_attn_kernel(place, own_ref, other_ref, out_ref):
    n = own_ref.shape[0] - GAIN_ROWS
    core = place[CORE]
    odd = core == 1
    out_ref[pl.ds(pl.multiple_of(core * n, n), n), :] = own_ref[:n, :]
    out_ref[pl.ds(pl.multiple_of((1 - core) * n, n), n), :] = other_ref[:n, :]
    own, other = own_ref[n:, :n], other_ref[n:, :n]
    rest = jnp.zeros((GAIN_ROWS, out_ref.shape[1] - 2 * n), BF16)
    out_ref[2 * n :, :] = jnp.concatenate(
        [jnp.where(odd, other, own), jnp.where(odd, own, other), rest], axis=1
    )


def pairs_kernel(place, own_ref, near_ref, far_ref, *refs):
    *straight_refs, p0_ref, p1_ref = refs
    n, part = own_ref.shape[0], straight_refs[0].shape[0]
    here = pl.ds(pl.multiple_of(place[YLO] * n, n), n)
    there = pl.ds(pl.multiple_of((1 - place[YLO]) * n, n), n)

    def fill(mine, other):
        mine[here, :] = own_ref[...]
        mine[there, :] = near_ref[...]
        for i, ref in enumerate(straight_refs):
            at = pl.multiple_of(place[YLO] * n + i * part, part)
            other[pl.ds(at, part), :] = ref[...]
        other[there, :] = far_ref[...]

    @pl.when(place[SECTION] == 0)
    def _():
        fill(p0_ref, p1_ref)

    @pl.when(place[SECTION] == 1)
    def _():
        fill(p1_ref, p0_ref)


def pairs(place, own, others):
    n, c = own.shape
    out = held((2 * n, c))
    return call(pairs_kernel, [out, out], [place, (own, *others)], room=20)


def fetch(pieces, whole, sems):
    n = pieces[0].shape[0]
    copies = [
        pltpu.make_async_copy(p, whole.at[pl.ds(i * n, n), :], sems.at[i])
        for i, p in enumerate(pieces)
    ]
    for c in copies:
        c.start()

    def wait():
        for c in copies:
            c.wait()

    return wait


def block_of(packs, place, i):
    step = sum(p.shape[0] for p in packs) // 8
    if len(packs) == 1:
        return packs[0], i * step, i
    return packs[i // 2], i % 2 * step, lax.rem(place[X] + i // 2, 4) * 2 + i % 2


def fetch_blocks(packs, place, column, whole, sems):
    n, c = whole.shape[0] // 8, whole.shape[1]

    def copy(i, pack, row, block):
        rows = pl.ds(pl.multiple_of(block * n, n), n)
        return pltpu.make_async_copy(
            pack.at[pl.ds(row, n), pl.ds(column, c)], whole.at[rows, :], sems.at[i]
        )

    for i in range(8):
        copy(i, *block_of(packs, place, i)).start()

    def wait():
        for i in range(8):
            pack, row, _ = block_of(packs, place, i)
            copy(i, pack, row, i).wait()

    return wait


def rms(rows):
    return lax.rsqrt(jnp.mean(rows * rows, axis=-1, keepdims=True) + EPS)


def turned(v, by):
    return pltpu.roll(v, by % v.shape[1], 1)


def low_half(v):
    return lax.broadcasted_iota(jnp.int32, v.shape, 1) % HD < HD // 2


def rope(v, cos, sin):
    half = HD // 2
    return v * cos + jnp.where(low_half(v), -turned(v, -half), turned(v, half)) * sin


def rope_back(u, cos, sin):
    half, w = HD // 2, u * sin
    return u * cos + jnp.where(low_half(w), turned(w, -half), -turned(w, half))


def halves_out(partial, send_ref, mine_ref):
    n = send_ref.shape[0]
    send_ref[...] = partial[n:].astype(BF16)
    mine_ref[...] = partial[:n]


def split_kernel(mine_ref, other_ref, own_ref, *piece_refs):
    n = own_ref.shape[0]
    own_ref[...] = mine_ref[:n, :] + other_ref[:n, :].astype(F32)
    for k, ref in enumerate(piece_refs, 1):
        at = slice(k * n, (k + 1) * n)
        ref[...] = (mine_ref[at, :] + other_ref[at, :].astype(F32)).astype(BF16)


def split(mine, other):
    n, d = mine.shape[0] // 4, mine.shape[1]
    return call(split_kernel, [shape((n, d), F32)] + [shape((n, d))] * 3, [mine, other])


def total_of(refs):
    return sum((r[...].astype(F32) for r in refs[1:]), refs[0][...])


def add_norm_kernel(a, b, c, d, x_ref, gain_ref, mid_ref, low_ref):
    mid = x_ref[...].astype(F32) + total_of((a, b, c, d))
    mid_ref[...] = mid
    low_ref[...] = (mid * rms(mid) * gain_ref[...]).astype(BF16)


def add_kernel(a, b, c, d, mid_ref, y_ref):
    y_ref[...] = (mid_ref[...] + total_of((a, b, c, d))).astype(BF16)


def norm_back_kernel(a, b, c, d, after_ref, x_ref, gain_ref, dx_ref, low_ref, gain_grad_ref):
    grad = total_of((a, b, c, d))
    x = x_ref[...].astype(F32)
    r = rms(x)
    n = x * r
    gain_grad_ref[...] = jnp.sum(grad * n, axis=0, keepdims=True)
    scaled = grad * gain_ref[...]
    dx = after_ref[...].astype(F32) + r * (
        scaled - n * jnp.mean(scaled * n, axis=-1, keepdims=True)
    )
    dx_ref[...] = dx
    low_ref[...] = dx.astype(BF16)


def qkv_kernel(place, *refs, parts):
    pieces, packs, refs = refs[:8], refs[8 : 8 + parts], refs[8 + parts :]
    cos_ref, sin_ref, x_ref, a_ref, q_ref, kv_ref, ga_ref, gf_ref, *refs = refs
    w_ref, gains_ref, x_sems, w_sems, g_sems = refs
    rows_there = fetch(pieces, x_ref, x_sems)
    n = w_ref.shape[0] // 8

    def gain_copy(i, pack, row, block):
        return pltpu.make_async_copy(
            pack.at[pl.ds(row + n, GAIN_ROWS), pl.ds(0, n)], gains_ref.at[block], g_sems.at[i]
        )

    for i in range(8):
        gain_copy(i, *block_of(packs, place, i)).start()
    weights_there = fetch_blocks(packs, place, 0, w_ref, w_sems)
    for i in range(8):
        pack, row, _ = block_of(packs, place, i)
        gain_copy(i, pack, row, i).wait()
    gains = jnp.concatenate([gains_ref[i] for i in range(8)], axis=1).astype(F32)
    ga_ref[...] = gains[0:1, :]
    gf_ref[...] = gains[1:2, :]
    rows_there()
    x = x_ref[...].astype(F32)
    a = (x * rms(x) * ga_ref[...]).astype(BF16)
    a_ref[...] = a
    weights_there()
    out = rope(nn(a, w_ref[...]), cos_ref[...], sin_ref[...])
    width = q_ref.shape[1]
    q_ref[...] = (out[:, :width].astype(BF16).astype(F32) * HD**-0.5).astype(BF16)
    half = out.shape[0] // 2
    k, v = out[:, width : width + HD], out[:, width + HD :]
    keys = jnp.concatenate([k[:half], k[half:]], axis=1)
    values = jnp.concatenate([v[half:], v[:half]], axis=1)
    kv_ref[...] = jnp.where(place[CORE] == 1, values, keys).astype(BF16)


def key_step(ref, t):
    per = ref.shape[0] // KEYS_STEP
    return pl.ds(t % per * KEYS_STEP, KEYS_STEP), slice(t // per * HD, (t // per + 1) * HD)


def attend_kernel(place, q_ref, own_ref, other_ref, bias_ref, *refs, parts):
    packs, refs = refs[:parts], refs[parts:]
    o_ref, lse_ref, k_ref, v_ref, send_ref, mine_ref, s_ref, w_ref, sems = refs
    weights_there = fetch_blocks(packs, place, packs[0].shape[1] - w_ref.shape[1], w_ref, sems)
    odd = place[CORE] == 1
    k_ref[...] = jnp.where(odd, other_ref[...], own_ref[...])
    v_ref[...] = jnp.where(odd, own_ref[...], other_ref[...])
    rows, width = q_ref.shape
    heads = width // HD
    steps = 2 * k_ref.shape[0] // KEYS_STEP
    tops = [jnp.full((1, rows), MASKED, F32) for _ in range(heads)]
    for t in range(steps):
        at = pl.ds(t * KEYS_STEP, KEYS_STEP)
        part, cols = key_step(k_ref, t)
        k = k_ref[part, cols]
        bias = bias_ref[at, :]
        for h in range(heads):
            s = nt(k, q_ref[:, h * HD : (h + 1) * HD]) + bias
            s_ref[h, at, :] = s
            tops[h] = jnp.maximum(tops[h], jnp.max(s, axis=0, keepdims=True))
    sums = [jnp.zeros((1, rows), F32) for _ in range(heads)]
    outs = [jnp.zeros((HD, rows), F32) for _ in range(heads)]
    for t in range(steps):
        at = pl.ds(t * KEYS_STEP, KEYS_STEP)
        part, cols = key_step(v_ref, t)
        v_t = v_ref[part, :].T[cols, :]
        for h in range(heads):
            e = jnp.exp(s_ref[h, at, :] - tops[h])
            sums[h] = sums[h] + jnp.sum(e, axis=0, keepdims=True)
            outs[h] = outs[h] + nn(v_t, e.astype(BF16))
    flat = jnp.concatenate([outs[h] / sums[h] for h in range(heads)], axis=0)
    o_ref[...] = flat.T.astype(BF16)
    lse_ref[...] = jnp.concatenate([tops[h] + jnp.log(sums[h]) for h in range(heads)], axis=0)
    weights_there()
    halves_out(nt(o_ref[...], w_ref[...]), send_ref, mine_ref)


def ffn_kernel(*refs):
    pieces, w_hbm, refs = refs[:8], refs[8], refs[9:]
    b_ref, gu_ref, h_ref, send_ref, mine_ref, gu_w, down_w, b_sems, gu_sems, sem = refs
    rows_there = fetch(pieces, b_ref, b_sems)
    steps, n, c = 4, w_hbm.shape[0] // 4, gu_w.shape[1]

    def load(i):
        at = pl.ds(i * n, n)
        return pltpu.make_async_copy(w_hbm.at[at, pl.ds(0, c)], gu_w.at[at, :], gu_sems.at[i])

    for i in range(steps):
        load(i).start()
    down = pltpu.make_async_copy(w_hbm.at[:, pl.ds(c, down_w.shape[1])], down_w, sem)
    down.start()
    rows_there()
    for i in range(steps):
        load(i).wait()
        at = slice(i * n, (i + 1) * n)
        part = nn(b_ref[:, at], gu_w[at, :])
        gu_ref[...] = part if i == 0 else gu_ref[...] + part
    units = gu_ref.shape[1] // 2
    gate, up = gu_ref[:, :units], gu_ref[:, units:]
    h_ref[:, :units] = (gate / (1.0 + jnp.exp(-gate)) * up).astype(BF16)
    spare = h_ref.shape[1] - units
    h_ref[:, units:] = jnp.zeros((h_ref.shape[0], spare), BF16)
    down.wait()
    halves_out(nt(h_ref[...], down_w[...]), send_ref, mine_ref)


def ffn_back_kernel(*refs):
    pieces, w_hbm, act_hbm, refs = refs[:8], refs[8], refs[9], refs[10:]
    dff_ref, dgu_ref, send_ref, mine_ref, gu_w, down_w, gu_ref, r_sems, gu_sems = refs
    rows_there = fetch(pieces, dff_ref, r_sems)
    c = gu_w.shape[1]
    down = pltpu.make_async_copy(w_hbm.at[:, pl.ds(c, down_w.shape[1])], down_w, gu_sems.at[2])
    down.start()
    act = pltpu.make_async_copy(act_hbm, gu_ref, gu_sems.at[0])
    act.start()
    load = pltpu.make_async_copy(w_hbm.at[:, pl.ds(0, c)], gu_w, gu_sems.at[1])
    load.start()
    rows_there()
    down.wait()
    units = gu_ref.shape[1] // 2
    dh = nn(dff_ref[...], down_w[...])[:, :units]
    act.wait()
    gate, up = gu_ref[:, :units], gu_ref[:, units:]
    sig = 1.0 / (1.0 + jnp.exp(-gate))
    dgate = dh * up * (sig * (1.0 + gate * (1.0 - sig)))
    dgu_ref[...] = jnp.concatenate([dgate, dh * (gate * sig)], axis=1).astype(BF16)
    load.wait()
    halves_out(nt(dgu_ref[...], gu_w[...]), send_ref, mine_ref)


def attend_back_kernel(place, *refs, parts):
    pieces, packs, refs = refs[:8], refs[8 : 8 + parts], refs[8 + parts :]
    q_ref, k_ref, v_ref, bias_ref, o_ref, lse_ref, cos_ref, sin_ref, *refs = refs
    dattn_ref, dq_ref, own_ref, send_ref, w_ref, do_ref, dk_ref, dv_ref, sems, r_sems = refs
    rows_there = fetch(pieces, dattn_ref, r_sems)
    weights_there = fetch_blocks(packs, place, packs[0].shape[1] - w_ref.shape[1], w_ref, sems)
    rows, width = q_ref.shape
    heads = width // HD
    steps = 2 * k_ref.shape[0] // KEYS_STEP
    rows_there()
    weights_there()
    do = nn(dattn_ref[...], w_ref[...])
    do_ref[...] = do.astype(BF16)
    both = (do_ref[...].astype(F32) * o_ref[...].astype(F32)).T
    deltas = [
        jnp.sum(both[h * HD : (h + 1) * HD, :], axis=0, keepdims=True) for h in range(heads)
    ]
    dq_t = [jnp.zeros((HD, rows), F32) for _ in range(heads)]
    for t in range(steps):
        at = pl.ds(t * KEYS_STEP, KEYS_STEP)
        part, cols = key_step(k_ref, t)
        k = k_ref[part, cols]
        v = v_ref[part, cols]
        k_t = k_ref[part, :].T[cols, :]
        bias = bias_ref[at, :]
        dk = jnp.zeros((KEYS_STEP, HD), F32)
        dv = jnp.zeros((KEYS_STEP, HD), F32)
        for h in range(heads):
            q_h = q_ref[:, h * HD : (h + 1) * HD]
            do_h = do_ref[:, h * HD : (h + 1) * HD]
            p = jnp.exp(nt(k, q_h) + bias - lse_ref[h : h + 1, :])
            ds = (p * (nt(v, do_h) - deltas[h])).astype(BF16)
            dv = dv + nn(p.astype(BF16), do_h)
            dk = dk + nn(ds, q_h)
            dq_t[h] = dq_t[h] + nn(k_t, ds)
        dk_ref[part, cols] = dk
        dv_ref[part, cols] = dv
    dq = jnp.concatenate(dq_t, axis=0).T * HD**-0.5
    dq_ref[...] = rope_back(dq, cos_ref[:, :width], sin_ref[:, :width]).astype(BF16)
    odd = place[CORE] == 1
    own_ref[...] = jnp.where(odd, dv_ref[...], dk_ref[...])
    send_ref[...] = jnp.where(odd, dk_ref[...], dv_ref[...]).astype(BF16)


def kv_add_kernel(own_ref, other_ref, out_ref):
    out_ref[...] = (own_ref[...] + other_ref[...].astype(F32)).astype(BF16)


def qkv_back_kernel(place, *refs, parts):
    packs, (x_hbm, dq_ref, kv_ref, cos_ref, sin_ref, *refs) = refs[:parts], refs[parts:]
    dqkv_ref, send_ref, mine_ref, gain_grad_ref, w_ref, x_ref, sems, x_sem = refs
    weights_there = fetch_blocks(packs, place, 0, w_ref, sems)
    rows_there = pltpu.make_async_copy(x_hbm, x_ref, x_sem)
    rows_there.start()
    width, odd = dq_ref.shape[1], place[CORE] == 1
    both = sum((kv_ref[i].astype(F32) for i in range(1, 8)), kv_ref[0].astype(F32))
    first, second = both[:, :HD], both[:, HD:]
    dk = jnp.concatenate([first, second], axis=0)
    dv = jnp.concatenate([second, first], axis=0)
    spare = jnp.zeros_like(dk)
    dkv = jnp.where(
        odd, jnp.concatenate([spare, dv], axis=1), jnp.concatenate([dk, spare], axis=1)
    )
    dkv = rope_back(dkv, cos_ref[:, width:], sin_ref[:, width:])
    dqkv_ref[:, :width] = dq_ref[...]
    dqkv_ref[:, width:] = dkv.astype(BF16)
    weights_there()
    da = nt(dqkv_ref[...], w_ref[...])
    halves_out(da, send_ref, mine_ref)
    rows_there.wait()
    x = x_ref[...].astype(F32)
    gain_grad_ref[...] = jnp.sum(da * (x * rms(x)), axis=0, keepdims=True)


def ffn_product_kernel(b_ref, dgu_ref, dff_ref, h_ref, out, whole, sems):
    n, steps = dgu_ref.shape[1], sems.shape[0]
    rows = whole.shape[0] // steps
    copies = []
    for i in range(steps):
        at = slice(i * rows, (i + 1) * rows)
        whole[at, :n] = tn(b_ref[:, at], dgu_ref[...]).astype(BF16)
        whole[at, n:] = tn(dff_ref[:, at], h_ref[...]).astype(BF16)
        here = pl.ds(i * rows, rows)
        copies.append(pltpu.make_async_copy(whole.at[here, :], out.at[here, :], sems.at[i]))
        copies[-1].start()
    for c in copies:
        c.wait()


def ffn_products(b, dgu, dff, hidden):
    dims = (b.shape[1], dgu.shape[1] + hidden.shape[1])
    return call(
        ffn_product_kernel,
        [pltpu.HBM(dims, BF16)],
        [(b, dgu, dff, hidden)],
        [pltpu.VMEM(dims, BF16), DMA((8,))],
        room=14,
        moved=20_000_000,
        out_spec=HBM,
    )[0]


def attn_product_kernel(dattn, a, gg_a, gg_f, ctx, dqkv, *refs, layer):
    *_, out, whole, sems = refs
    cols = pl.ds(layer * whole.shape[1], whole.shape[1])
    m, steps = ctx.shape[1], sems.shape[0]
    wide = m + dqkv.shape[1]
    rows = whole.shape[0] // steps
    row = lax.broadcasted_iota(jnp.int32, (whole.shape[1] - wide, rows), 0)
    copies = []
    for i in range(steps):
        at = slice(i * rows, (i + 1) * rows)
        whole[at, :m] = tn(dattn[:, at], ctx[...]).astype(BF16)
        whole[at, m:wide] = tn(a[:, at], dqkv[...]).astype(BF16)
        ga, gf = (jnp.broadcast_to(g[:, at], row.shape) for g in (gg_a, gg_f))
        gains = jnp.where(row == 0, ga, jnp.where(row == 1, gf, 0.0))
        whole[at, wide:] = gains.T.astype(BF16)
        here = pl.ds(i * rows, rows)
        copies.append(pltpu.make_async_copy(whole.at[here, :], out.at[here, cols], sems.at[i]))
        copies[-1].start()
    for c in copies:
        c.wait()


def attn_products(dattn, ctx, a, dqkv, gg_a, gg_f, layer, filled=None):
    d, wide = a.shape[1], ctx.shape[1] + dqkv.shape[1] + 128
    args = [(dattn, a, gg_a, gg_f, ctx, dqkv)]
    return call(
        functools.partial(attn_product_kernel, layer=layer),
        [pltpu.HBM((d, 2 * wide), BF16)],
        args if filled is None else args + [[filled]],
        [pltpu.VMEM((d, wide), BF16), DMA((4,))],
        room=14,
        out_spec=HBM,
        moved=12_000_000,
        aliases=None if filled is None else {6: 0},
    )[0]


def y_split_both_kernel(place, r_ref, keep_ref, near_ref, far_ref, straight_ref):
    n, c = keep_ref.shape
    here = pl.ds(pl.multiple_of(place[YLO] * n, n), n)
    there = pl.ds(pl.multiple_of((1 - place[YLO]) * n, n), n)

    def fill(mine, other):
        keep_ref[...] = r_ref[here, mine]
        near_ref[...] = r_ref[there, mine]
        straight_ref[...] = r_ref[here, other]
        far_ref[...] = r_ref[there, other]

    @pl.when(place[SECTION] == 0)
    def _():
        fill(slice(0, c), slice(c, 2 * c))

    @pl.when(place[SECTION] == 1)
    def _():
        fill(slice(c, 2 * c), slice(0, c))


def reduce_y_both(r, place):
    dims = (r.shape[0] // 2, r.shape[1] // 2)
    keep, near, far, straight = call(
        y_split_both_kernel, [held(dims)] * 4, [place, (r,)], room=16
    )
    return [keep, swap_ylo(near), swap_across(far), swap_section(straight)]


def y_split_kernel(place, r0_ref, r1_ref, keep_ref, near_ref, far_ref, straight_ref):
    n = keep_ref.shape[0]
    here = pl.ds(pl.multiple_of(place[YLO] * n, n), n)
    there = pl.ds(pl.multiple_of((1 - place[YLO]) * n, n), n)

    def fill(mine, other):
        keep_ref[...] = mine[here, :]
        near_ref[...] = mine[there, :]
        straight_ref[...] = other[here, :]
        far_ref[...] = other[there, :]

    @pl.when(place[SECTION] == 0)
    def _():
        fill(r0_ref, r1_ref)

    @pl.when(place[SECTION] == 1)
    def _():
        fill(r1_ref, r0_ref)


def by_core_kernel(place, *refs):
    *parts, own_ref, send_ref = refs
    n = own_ref.shape[0]
    here = pl.ds(pl.multiple_of(place[CORE] * n, n), n)
    there = pl.ds(pl.multiple_of((1 - place[CORE]) * n, n), n)
    own_ref[...] = sum(p[here, :].astype(F32) for p in parts)
    send_ref[...] = sum(p[there, :].astype(F32) for p in parts).astype(BF16)


def by_core(parts, place):
    n, c = parts[0].shape[0] // 2, parts[0].shape[1]
    own, send = call(
        by_core_kernel, [held((n, c), F32), shape((n, c))], [place, tuple(parts)], room=16, moved=10_000_000
    )
    return own, swap_core(send)


def reduce_y(r0, r1, place):
    n, c = r0.shape[0] // 2, r0.shape[1]
    keep, near, far, straight = call(y_split_kernel, [held((n, c))] * 4, [place, (r0, r1)], room=16)
    return [keep, swap_ylo(near), swap_across(far), swap_section(straight)]


def ordered(odd, own, other):
    other = other.astype(F32)
    return jnp.concatenate(
        [jnp.where(odd, other, own), jnp.where(odd, own, other)], axis=1
    )


def attn_grads_kernel(place, own_ref, other_ref, o_ref, q_ref, k_ref, v_ref, *gain_refs):
    odd = place[CORE] == 1
    m = n = q_ref.shape[1] // 2
    own, other = own_ref[:, :m].T, other_ref[:, :m].astype(F32).T
    o_ref[:m, :] = jnp.where(odd, other, own)
    o_ref[m:, :] = jnp.where(odd, own, other)
    q_ref[...] = ordered(odd, own_ref[:, m : m + n], other_ref[:, m : m + n])
    both = own_ref[:, m + n :] + other_ref[:, m + n :].astype(F32)
    kv = both[:, : 2 * HD].T
    k_ref[...] = kv[:HD, :]
    v_ref[...] = kv[HD:, :]
    rows = gain_refs[0].shape[0]
    gain_refs[-1][...] = both[:, 2 * HD :]
    for k, ref in enumerate(gain_refs[:-1]):
        at = lax.rem(place[TP] + k, 4) * rows
        ref[...] = gain_refs[-1][pl.ds(pl.multiple_of(at, rows), rows), :]


def ffn_grads_kernel(place, own_ref, other_ref, gate_ref, up_ref, down_ref):
    odd = place[CORE] == 1
    n = gate_ref.shape[1] // 2
    gate_ref[...] = ordered(odd, own_ref[:, :n], other_ref[:, :n])
    up_ref[...] = ordered(odd, own_ref[:, n : 2 * n], other_ref[:, n : 2 * n])
    own, other = own_ref[:, 2 * n :].T[:n], other_ref[:, 2 * n :].astype(F32).T[:n]
    down_ref[:n, :] = jnp.where(odd, other, own)
    down_ref[n:, :] = jnp.where(odd, own, other)


def body(
    block_input,
    out_grad,
    seg_ids,
    attn_gain,
    w_query,
    w_key,
    w_value,
    w_out,
    ffn_gain,
    w_gate,
    w_up,
    w_down,
):
    at = {name: lax.axis_index(name) for name in AXES}
    section, core, tp = at["section"], at["core"], at["tp"]
    place = jnp.stack([at[name] for name in AXES]).astype(jnp.int32)
    d = block_input.shape[2]
    micro_rows = block_input.shape[1]
    group = 8 * micro_rows
    q_width = w_query.shape[2] // 2
    units = w_gate.shape[2] // 2
    own_rows = w_query.shape[1]

    padded = units + (-units) % 128
    attn_dims = (own_rows + GAIN_ROWS, 2 * q_width + 2 * HD)
    attn_own, attn_send = call(
        pack_attn_kernel,
        [shape(attn_dims)] * 2,
        [place, (w_query[0], w_key[0].T, w_value[0].T, w_out[0], attn_gain, ffn_gain)],
    )
    attn_shard = call(
        chip_attn_kernel,
        [held((2 * own_rows + GAIN_ROWS, attn_dims[1]))],
        [place, (attn_own, swap_core(attn_send))],
    )[0]
    ffn_own, ffn_send = call(
        pack_ffn_kernel,
        [shape((own_rows, 2 * units + padded))] * 2,
        [place, (w_down[0], w_gate[0], w_up[0])],
        room=16,
    )
    ffn_shard = chip_rows(place, ffn_own, swap_core(ffn_send))
    attn_y = y_exchange(after(attn_shard, ffn_shard))
    attn_pairs = pairs(place, attn_shard, attn_y)
    attn0 = [attn_pairs[0]] + [from_x(attn_pairs[0], k) for k in (1, 2, 3)]
    attn1 = [gather_x(attn_pairs[1])]
    ffn_y = y_exchange_on(after(ffn_shard, *attn_y))

    block = at["x"] * 2 + at["ylo"]
    seg_row = lax.dynamic_index_in_dim(seg_ids, section, 0, keepdims=False)
    def arranged(row):
        v = row.reshape(8, 2, 4, micro_rows)
        return lax.dynamic_slice_in_dim(jnp.concatenate([v, v], axis=2), tp, 4, 2)

    def keys_of(row):
        return arranged(row).transpose(1, 0, 2, 3).reshape(-1)

    def queries_of(row):
        v = lax.dynamic_index_in_dim(arranged(row), block, 0, keepdims=False)
        return jnp.where(core == 0, v, v[::-1]).reshape(-1)

    places = jnp.arange(seg_row.shape[0], dtype=jnp.int32)
    k_pos, k_seg = keys_of(places), keys_of(seg_row)
    q_pos, q_seg = queries_of(places), queries_of(seg_row)
    seen = (k_pos[:, None] <= q_pos[None, :]) & (k_seg[:, None] == q_seg[None, :])
    bias = jnp.where(seen, 0.0, MASKED).astype(F32)

    frequency = 10000.0 ** (-jnp.arange(0, HD, 2, dtype=F32) / HD)
    angles = q_pos.astype(F32)[:, None] * frequency[None, :]
    wide = q_width + 2 * HD
    plain = lax.broadcasted_iota(jnp.int32, (group, wide), 1) >= q_width + HD
    cos, sin = (jnp.concatenate([t] * 12, axis=1) for t in (jnp.cos(angles), jnp.sin(angles)))
    cos, sin = jnp.where(plain, 1.0, cos), jnp.where(plain, 0.0, sin)

    rows_low = shape((micro_rows, d))
    rows_f32 = shape((micro_rows, d), F32)
    mid_outs = [rows_f32, rows_low]
    partials = [shape((group // 2, d)), shape((group // 2, d), F32)]
    heads, keys = q_width // HD, seg_row.shape[0]
    gain_row = shape((1, d), F32)

    def project(x, packs):
        return call(
            functools.partial(qkv_kernel, parts=len(packs)),
            [held((group, d))] * 2
            + [shape((group, q_width)), shape((group // 2, 2 * HD))]
            + [gain_row, gain_row],
            [place, gather_rows(x) + packs, cos, sin],
            [
                pltpu.VMEM((d, wide), BF16),
                pltpu.VMEM((8, GAIN_ROWS, d // 8), BF16),
                DMA((8,)),
                DMA((8,)),
                DMA((8,)),
            ],
            room=18,
        )

    both_kv = held((keys // 2, 2 * HD))

    def attention(q, kv, packs):
        return call(
            functools.partial(attend_kernel, parts=len(packs)),
            [held((group, q_width)), held((heads, group), F32), both_kv, both_kv, *partials],
            [place, q, *kv, bias, packs],
            [
                pltpu.VMEM((heads, keys, group), F32),
                pltpu.VMEM((d, q_width), BF16),
                DMA((8,)),
            ],
            room=12,
        )

    def feed_forward(b, w_ffn):
        return call(
            ffn_kernel,
            [held((group, d)), held((group, 2 * units), F32), held((group, padded)), *partials],
            [[*gather_rows(b), w_ffn]],
            [
                pltpu.VMEM((d, 2 * units), BF16),
                pltpu.VMEM((d, padded), BF16),
                DMA((8,)),
                DMA((4,)),
                DMA,
            ],
            room=16,
        )

    def backward(dy, kept, layer, filled=None, pending=()):
        x, rows, a, q, k, v, ctx, lse, mid, b, gu, hidden, gain_a, gain_f, w_ffn, packs = kept
        dff, dgu, send, mine = call(
            ffn_back_kernel,
            [held((group, d)), held((group, 2 * units)), *partials],
            [[*gather_rows(dy), w_ffn, gu]],
            [
                pltpu.VMEM((d, 2 * units), BF16),
                pltpu.VMEM((d, padded), BF16),
                pltpu.VMEM((group, 2 * units), F32),
                DMA((8,)),
                DMA((3,)),
            ],
            room=16,
        )
        g_ffn = ffn_products(b, dgu, dff, hidden)
        dmid, dattn, gg_f = call(
            norm_back_kernel,
            [rows_f32, rows_low, held((1, d), F32)],
            [*reduce_rows(send, mine), dy, mid, gain_f],
        )
        dattn = after(dattn, g_ffn, *pending)
        dattn, dq, dkv, dkv_send = call(
            functools.partial(attend_back_kernel, parts=len(packs)),
            [
                held((group, d)),
                shape((group, q_width)),
                shape((keys // 2, 2 * HD), F32),
                shape((keys // 2, 2 * HD)),
            ],
            [place, gather_rows(dattn) + packs, (q, k, v), bias, (ctx, lse), cos, sin],
            [
                pltpu.VMEM((d, q_width), BF16),
                pltpu.VMEM((group, q_width), BF16),
                pltpu.VMEM((keys // 2, 2 * HD), F32),
                pltpu.VMEM((keys // 2, 2 * HD), F32),
                DMA((8,)),
                DMA((8,)),
            ],
            room=18,
        )
        dkv = call(kv_add_kernel, [shape(dkv.shape)], [dkv, swap_core(dkv_send)])[0]
        arrived = lax.all_to_all(
            dkv.reshape(8, group // 2, 2 * HD), ("x", "ylo"), 0, 0, tiled=True
        )
        dqkv, send, mine, gg_a = call(
            functools.partial(qkv_back_kernel, parts=len(packs)),
            [held((group, wide)), *partials, held((1, d), F32)],
            [place, packs + [rows], dq, arrived, cos, sin],
            [pltpu.VMEM((d, wide), BF16), pltpu.VMEM((group, d), BF16), DMA((8,)), DMA],
            room=16,
        )
        g_attn = attn_products(dattn, ctx, a, dqkv, gg_a, gg_f, layer, filled)
        dx, dx_low, _ = call(
            norm_back_kernel,
            [rows_f32, rows_low, held((1, d), F32)],
            [*reduce_rows(send, mine), dmid, x, gain_a],
        )
        return dx, after(dx_low, g_attn), g_attn, g_ffn, dqkv

    x0 = lax.dynamic_index_in_dim(block_input, section, 0, keepdims=False)
    dy1 = lax.dynamic_index_in_dim(out_grad, section, 0, keepdims=False)

    rows0, a0, q0, kv0, ga0, gf0 = project(x0, attn0)
    ffn_pairs = pairs(place, ffn_shard, ffn_y)
    w_ffn0 = gather_x(after(ffn_pairs[0], *attn0[1:], *attn1))
    kv0 = gather_kv(kv0)
    ctx0, lse0, k0, v0, send, mine = attention(q0, kv0, attn0)
    mid0, b = call(add_norm_kernel, mid_outs, [*reduce_rows(send, mine), x0, gf0])
    w_ffn1 = gather_x(after(ffn_pairs[1], b))
    b0, up0, hidden0, send, mine = feed_forward(b, w_ffn0)
    y0 = call(add_kernel, [rows_low], [*reduce_rows(send, mine), mid0])[0]
    kept0 = (x0, rows0, a0, q0, k0, v0, ctx0, lse0, mid0, b0, up0, hidden0, ga0, gf0, w_ffn0, attn0)
    rows1, a1, q1, kv1, ga1, gf1 = project(y0, attn1)
    ctx1, lse1, k1, v1, send, mine = attention(q1, gather_kv(kv1), attn1)
    mid1, b = call(add_norm_kernel, mid_outs, [*reduce_rows(send, mine), y0, gf1])
    b1, up1, hidden1, send, mine = feed_forward(b, w_ffn1)
    last = (send, mine, mid1)
    kept1 = (y0, rows1, a1, q1, k1, v1, ctx1, lse1, mid1, b1, up1, hidden1, ga1, gf1, w_ffn1, attn1)

    early = section == 0

    def both_micros(layer0, layer1, dtype):
        mine = jnp.where(early, layer0, layer1).astype(dtype)
        other = jnp.where(early, layer1, layer0).astype(BF16)
        other = swap_section(other).astype(dtype)
        return jnp.stack([jnp.where(early, mine, other), jnp.where(early, other, mine)])[None]

    dx1, dx1_low, g_attn1, g_ffn1, _ = backward(dy1, kept1, 1)
    ffn1 = reduce_x(g_ffn1)
    dx0, dx0_low, g_attn, g_ffn0, dqkv0 = backward(dx1_low, kept0, 0, g_attn1, [ffn1])
    send, mine, mid1 = last
    y1 = call(add_kernel, [rows_low], [*reduce_rows(after(send, dqkv0), mine), mid1])[0]
    block_output = both_micros(y0, y1, BF16)
    input_grad = both_micros(dx0, dx1, F32)
    ffn_y = reduce_y(after(reduce_x(g_ffn0), input_grad, block_output), ffn1, place)

    attn_y = reduce_y_both(reduce_x(g_attn), place)
    ffn_parts = by_core([after(ffn_y[0], attn_y[0]), *ffn_y[1:]], place)

    def finish(kernel, dims, parts):
        return call(
            kernel, [held(s, F32) for s in dims], [place, parts], room=20, moved=10_000_000
        )

    own = own_rows
    grad_gate, grad_up, grad_down = finish(
        ffn_grads_kernel, [(own, 2 * units)] * 2 + [(2 * units, own)], ffn_parts
    )
    attn_parts = by_core([after(attn_y[0], grad_gate), *attn_y[1:]], place)
    grad_out, grad_query, grad_key, grad_value, *gain_pieces, _ = finish(
        attn_grads_kernel,
        [(2 * q_width, own), (own, 2 * q_width), (HD, own), (HD, own)]
        + [(micro_rows, 128)] * 4
        + [(own, 128)],
        attn_parts,
    )
    gain_sums = gain_pieces[0]
    for k in (1, 2, 3):
        gain_sums = gain_sums + from_z(gain_pieces[k], -k)
    gain_sums = gain_sums[:, :2].T


    return (
        block_output,
        input_grad,
        gain_sums[0][None],
        grad_query[None],
        grad_key.T[None],
        grad_value.T[None],
        grad_out[None],
        gain_sums[1][None],
        grad_gate[None],
        grad_up[None],
        grad_down[None],
    )


def solution(mesh):
    fine = Mesh(mesh.devices.reshape(2, 4, 2, 2, 4), AXES)
    wide = ("x", "ylo", "core")
    rows = P(None, (*wide, "tp"), None)
    into = P("section", wide, "tp")
    out_of = P("section", "tp", wide)
    grown = P("section", None, (*wide, "tp"), None)
    gain_grad = P("section", (*wide, "tp"))
    return jax.shard_map(
        body,
        mesh=fine,
        in_specs=(
            rows, rows, P(), P("section", wide), into, into, into, out_of,
            P("section", wide), into, into, out_of,
        ),
        out_specs=(
            grown, grown, gain_grad, into, into, into, out_of, gain_grad, into, into, out_of,
        ),
        check_vma=False,
    )
```

```python
import functools
import math

import jax
import jax.numpy as jnp
from jax import lax
from jax.experimental import pallas as pl
from jax.experimental.pallas import tpu as pltpu
from jax.sharding import Mesh, PartitionSpec as P

HD = 64
GAIN_ROWS = 16
EPS = 1e-05
MASKED = -1e30
KEYS_STEP = 512
AXES = ("section", "x", "ylo", "core", "tp")
SECTION, X, YLO, CORE, TP = range(5)
BF16 = jnp.bfloat16
F32 = jnp.float32
VMEM = pl.BlockSpec(memory_space=pltpu.VMEM)
SMEM = pl.BlockSpec(memory_space=pltpu.SMEM)
HBM = pl.BlockSpec(memory_space=pltpu.HBM)
DMA = pltpu.SemaphoreType.DMA


def nn(a, b):
    return jnp.dot(a, b, preferred_element_type=F32)


def nt(a, b):
    return lax.dot_general(a, b, (((1,), (1,)), ((), ())), preferred_element_type=F32)


def tn(a, b):
    return lax.dot_general(a, b, (((0,), (0,)), ((), ())), preferred_element_type=F32)


def shape(dims, dtype=BF16):
    return jax.ShapeDtypeStruct(tuple(dims), dtype)


SHORT = pl.CostEstimate(flops=1, bytes_accessed=1, transcendentals=0)


def held(dims, dtype=BF16):
    return pltpu.HBM(tuple(dims), dtype)


def pinned(v):
    return pltpu.with_memory_space_constraint(v, pltpu.HBM)


def call(kernel, outs, args, scratch=(), room=8, out_spec=None, moved=0, aliases=None):
    specs, values = [], []
    for a in args:
        if isinstance(a, (list, tuple)):
            specs += [HBM if isinstance(a, list) else pl.BlockSpec()] * len(a)
            values += [pinned(v) for v in a]
        else:
            specs.append(SMEM if a.dtype == jnp.int32 else VMEM)
            values.append(a)
    mine = [m for m in scratch if isinstance(m, type(pltpu.VMEM((8, 128), F32)))]
    room = room * 2**20 + sum(
        math.prod(m.shape) * jnp.dtype(m.dtype).itemsize for m in mine if m.dtype in (BF16, F32)
    )
    return pl.pallas_call(
        kernel,
        out_shape=tuple(outs),
        in_specs=specs,
        out_specs=tuple(
            VMEM if isinstance(o, jax.ShapeDtypeStruct) else out_spec or pl.BlockSpec() for o in outs
        ),
        scratch_shapes=list(scratch),
        input_output_aliases=aliases or {},
        compiler_params=pltpu.CompilerParams(vmem_limit_bytes=room),
        cost_estimate=pl.CostEstimate(flops=moved, bytes_accessed=moved, transcendentals=0)
        if moved
        else SHORT,
        name=getattr(kernel, "func", kernel).__name__,
    )(*values)


def from_z(rows, by):
    return lax.ppermute(rows, "tp", [((i + by) % 4, i) for i in range(4)])


def from_x(v, by):
    return lax.ppermute(v, "x", [((i + by) % 4, i) for i in range(4)])


def swap_core(v):
    return lax.ppermute(v, "core", [(0, 1), (1, 0)])


def swap_ylo(v):
    return lax.ppermute(v, "ylo", [(0, 1), (1, 0)])


def swap_section(v):
    return lax.ppermute(v, "section", [(0, 1), (1, 0)])


def swap_across(v):
    return lax.ppermute(v, ("section", "ylo"), [(0, 3), (3, 0), (1, 2), (2, 1)])


def after(value, *others):
    return lax.optimization_barrier((value, *others))[0]


def y_exchange(v):
    return swap_ylo(v), swap_across(v), swap_section(v)


def y_exchange_on(v):
    near, far = swap_ylo(v), swap_across(v)
    n = v.shape[0] // 2
    return near, far, swap_ylo(far[:n]), swap_across(near[n:])


def gather_rows(rows):
    pieces = [rows] + [from_z(rows, k) for k in (1, 2, 3)]
    return pieces + [swap_core(p) for p in pieces]


def gather_kv(half):
    copies = jnp.broadcast_to(half[None], (8, *half.shape))
    own = lax.all_to_all(copies, ("x", "ylo"), 0, 0, tiled=True).reshape(-1, half.shape[1])
    return own, swap_core(own)


def reduce_rows(send, mine):
    own, *pieces = split(mine, swap_core(send))
    return [own] + [from_z(p, -k) for k, p in zip((1, 2, 3), pieces)]


def gather_x(block):
    return lax.all_gather(block, "x", axis=0, tiled=True)


def reduce_x(grad):
    return lax.psum_scatter(grad, "x", scatter_dimension=0, tiled=True)


def pack_attn_kernel(place, q_ref, k_ref, v_ref, o_ref, ga_ref, gf_ref, own_ref, send_ref):
    n, rows = q_ref.shape[1] // 2, q_ref.shape[0]
    m = n + 2 * HD
    kv = jnp.concatenate([k_ref[...], v_ref[...]], axis=0).T
    o = o_ref[...].T
    odd = place[CORE] == 1
    row = lax.broadcasted_iota(jnp.int32, (GAIN_ROWS, ga_ref.shape[1]), 0)
    ga, gf = (jnp.broadcast_to(g[...].astype(F32), row.shape) for g in (ga_ref, gf_ref))
    gains = jnp.where(row == 0, ga, jnp.where(row == 1, gf, 0.0)).astype(BF16)
    rest = jnp.zeros((GAIN_ROWS, own_ref.shape[1] - gains.shape[1]), BF16)
    for ref, high in ((own_ref, odd), (send_ref, jnp.logical_not(odd))):
        ref[:rows, :n] = jnp.where(high, q_ref[:, n:], q_ref[:, :n])
        ref[:rows, n:m] = kv
        ref[:rows, m:] = jnp.where(high, o[:, n:], o[:, :n])
        ref[rows:, :] = jnp.concatenate([gains, rest], axis=1)


def pack_ffn_kernel(place, d_ref, g_ref, u_ref, own_ref, send_ref):
    odd = place[CORE] == 1
    d = d_ref[...].T
    n = d.shape[1] // 2
    spare = jnp.zeros((own_ref.shape[0], own_ref.shape[1] - 3 * n), BF16)
    low, high = (
        jnp.concatenate([w[:, at] for w in (g_ref[...], u_ref[...], d)] + [spare], axis=1)
        for at in (slice(0, n), slice(n, 2 * n))
    )
    own_ref[...] = jnp.where(odd, high, low)
    send_ref[...] = jnp.where(odd, low, high)


def chip_rows_kernel(place, own_ref, other_ref, out_ref):
    n = own_ref.shape[0]
    core = place[CORE]
    out_ref[pl.ds(pl.multiple_of(core * n, n), n), :] = own_ref[...]
    out_ref[pl.ds(pl.multiple_of((1 - core) * n, n), n), :] = other_ref[...]


def chip_rows(place, own, other):
    n, c = own.shape
    return call(chip_rows_kernel, [held((2 * n, c))], [place, (own, other)], room=12)[0]


def chip_attn_kernel(place, own_ref, other_ref, out_ref):
    n = own_ref.shape[0] - GAIN_ROWS
    core = place[CORE]
    odd = core == 1
    out_ref[pl.ds(pl.multiple_of(core * n, n), n), :] = own_ref[:n, :]
    out_ref[pl.ds(pl.multiple_of((1 - core) * n, n), n), :] = other_ref[:n, :]
    own, other = own_ref[n:, :n], other_ref[n:, :n]
    rest = jnp.zeros((GAIN_ROWS, out_ref.shape[1] - 2 * n), BF16)
    out_ref[2 * n :, :] = jnp.concatenate(
        [jnp.where(odd, other, own), jnp.where(odd, own, other), rest], axis=1
    )


def pairs_kernel(place, own_ref, near_ref, far_ref, *refs):
    *straight_refs, p0_ref, p1_ref = refs
    n, part = own_ref.shape[0], straight_refs[0].shape[0]
    here = pl.ds(pl.multiple_of(place[YLO] * n, n), n)
    there = pl.ds(pl.multiple_of((1 - place[YLO]) * n, n), n)

    def fill(mine, other):
        mine[here, :] = own_ref[...]
        mine[there, :] = near_ref[...]
        for i, ref in enumerate(straight_refs):
            at = pl.multiple_of(place[YLO] * n + i * part, part)
            other[pl.ds(at, part), :] = ref[...]
        other[there, :] = far_ref[...]

    @pl.when(place[SECTION] == 0)
    def _():
        fill(p0_ref, p1_ref)

    @pl.when(place[SECTION] == 1)
    def _():
        fill(p1_ref, p0_ref)


def pairs(place, own, others):
    n, c = own.shape
    out = held((2 * n, c))
    return call(pairs_kernel, [out, out], [place, (own, *others)], room=20)


def fetch(pieces, whole, sems):
    n = pieces[0].shape[0]
    copies = [
        pltpu.make_async_copy(p, whole.at[pl.ds(i * n, n), :], sems.at[i])
        for i, p in enumerate(pieces)
    ]
    for c in copies:
        c.start()

    def wait():
        for c in copies:
            c.wait()

    return wait


def block_of(packs, place, i):
    step = sum(p.shape[0] for p in packs) // 8
    if len(packs) == 1:
        return packs[0], i * step, i
    return packs[i // 2], i % 2 * step, lax.rem(place[X] + i // 2, 4) * 2 + i % 2


def fetch_blocks(packs, place, column, whole, sems):
    n, c = whole.shape[0] // 8, whole.shape[1]

    def copy(i, pack, row, block):
        rows = pl.ds(pl.multiple_of(block * n, n), n)
        return pltpu.make_async_copy(
            pack.at[pl.ds(row, n), pl.ds(column, c)], whole.at[rows, :], sems.at[i]
        )

    for i in range(8):
        copy(i, *block_of(packs, place, i)).start()

    def wait():
        for i in range(8):
            pack, row, _ = block_of(packs, place, i)
            copy(i, pack, row, i).wait()

    return wait


def rms(rows):
    return lax.rsqrt(jnp.mean(rows * rows, axis=-1, keepdims=True) + EPS)


def turned(v, by):
    return pltpu.roll(v, by % v.shape[1], 1)


def low_half(v):
    return lax.broadcasted_iota(jnp.int32, v.shape, 1) % HD < HD // 2


def rope(v, cos, sin):
    half = HD // 2
    return v * cos + jnp.where(low_half(v), -turned(v, -half), turned(v, half)) * sin


def rope_back(u, cos, sin):
    half, w = HD // 2, u * sin
    return u * cos + jnp.where(low_half(w), turned(w, -half), -turned(w, half))


def halves_out(partial, send_ref, mine_ref):
    n = send_ref.shape[0]
    send_ref[...] = partial[n:].astype(BF16)
    mine_ref[...] = partial[:n]


def split_kernel(mine_ref, other_ref, own_ref, *piece_refs):
    n = own_ref.shape[0]
    own_ref[...] = mine_ref[:n, :] + other_ref[:n, :].astype(F32)
    for k, ref in enumerate(piece_refs, 1):
        at = slice(k * n, (k + 1) * n)
        ref[...] = (mine_ref[at, :] + other_ref[at, :].astype(F32)).astype(BF16)


def split(mine, other):
    n, d = mine.shape[0] // 4, mine.shape[1]
    return call(split_kernel, [shape((n, d), F32)] + [shape((n, d))] * 3, [mine, other])


def total_of(refs):
    return sum((r[...].astype(F32) for r in refs[1:]), refs[0][...])


def add_norm_kernel(a, b, c, d, x_ref, gain_ref, mid_ref, low_ref):
    mid = x_ref[...].astype(F32) + total_of((a, b, c, d))
    mid_ref[...] = mid
    low_ref[...] = (mid * rms(mid) * gain_ref[...]).astype(BF16)


def add_kernel(a, b, c, d, mid_ref, y_ref):
    y_ref[...] = (mid_ref[...] + total_of((a, b, c, d))).astype(BF16)


def norm_back_kernel(a, b, c, d, after_ref, x_ref, gain_ref, dx_ref, low_ref, gain_grad_ref):
    grad = total_of((a, b, c, d))
    x = x_ref[...].astype(F32)
    r = rms(x)
    n = x * r
    gain_grad_ref[...] = jnp.sum(grad * n, axis=0, keepdims=True)
    scaled = grad * gain_ref[...]
    dx = after_ref[...].astype(F32) + r * (
        scaled - n * jnp.mean(scaled * n, axis=-1, keepdims=True)
    )
    dx_ref[...] = dx
    low_ref[...] = dx.astype(BF16)


def qkv_kernel(place, *refs, parts):
    pieces, packs, refs = refs[:8], refs[8 : 8 + parts], refs[8 + parts :]
    cos_ref, sin_ref, x_ref, a_ref, q_ref, kv_ref, ga_ref, gf_ref, *refs = refs
    w_ref, gains_ref, x_sems, w_sems, g_sems = refs
    rows_there = fetch(pieces, x_ref, x_sems)
    n = w_ref.shape[0] // 8

    def gain_copy(i, pack, row, block):
        return pltpu.make_async_copy(
            pack.at[pl.ds(row + n, GAIN_ROWS), pl.ds(0, n)], gains_ref.at[block], g_sems.at[i]
        )

    for i in range(8):
        gain_copy(i, *block_of(packs, place, i)).start()
    weights_there = fetch_blocks(packs, place, 0, w_ref, w_sems)
    for i in range(8):
        pack, row, _ = block_of(packs, place, i)
        gain_copy(i, pack, row, i).wait()
    gains = jnp.concatenate([gains_ref[i] for i in range(8)], axis=1).astype(F32)
    ga_ref[...] = gains[0:1, :]
    gf_ref[...] = gains[1:2, :]
    rows_there()
    x = x_ref[...].astype(F32)
    a = (x * rms(x) * ga_ref[...]).astype(BF16)
    a_ref[...] = a
    weights_there()
    out = rope(nn(a, w_ref[...]), cos_ref[...], sin_ref[...])
    width = q_ref.shape[1]
    q_ref[...] = (out[:, :width].astype(BF16).astype(F32) * HD**-0.5).astype(BF16)
    half = out.shape[0] // 2
    k, v = out[:, width : width + HD], out[:, width + HD :]
    keys = jnp.concatenate([k[:half], k[half:]], axis=1)
    values = jnp.concatenate([v[half:], v[:half]], axis=1)
    kv_ref[...] = jnp.where(place[CORE] == 1, values, keys).astype(BF16)


def key_step(ref, t):
    per = ref.shape[0] // KEYS_STEP
    return pl.ds(t % per * KEYS_STEP, KEYS_STEP), slice(t // per * HD, (t // per + 1) * HD)


def attend_kernel(place, q_ref, own_ref, other_ref, bias_ref, *refs, parts):
    packs, refs = refs[:parts], refs[parts:]
    o_ref, lse_ref, k_ref, v_ref, send_ref, mine_ref, s_ref, w_ref, sems = refs
    weights_there = fetch_blocks(packs, place, packs[0].shape[1] - w_ref.shape[1], w_ref, sems)
    odd = place[CORE] == 1
    k_ref[...] = jnp.where(odd, other_ref[...], own_ref[...])
    v_ref[...] = jnp.where(odd, own_ref[...], other_ref[...])
    rows, width = q_ref.shape
    heads = width // HD
    steps = 2 * k_ref.shape[0] // KEYS_STEP
    tops = [jnp.full((1, rows), MASKED, F32) for _ in range(heads)]
    for t in range(steps):
        at = pl.ds(t * KEYS_STEP, KEYS_STEP)
        part, cols = key_step(k_ref, t)
        k = k_ref[part, cols]
        bias = bias_ref[at, :]
        for h in range(heads):
            s = nt(k, q_ref[:, h * HD : (h + 1) * HD]) + bias
            s_ref[h, at, :] = s
            tops[h] = jnp.maximum(tops[h], jnp.max(s, axis=0, keepdims=True))
    sums = [jnp.zeros((1, rows), F32) for _ in range(heads)]
    outs = [jnp.zeros((HD, rows), F32) for _ in range(heads)]
    for t in range(steps):
        at = pl.ds(t * KEYS_STEP, KEYS_STEP)
        part, cols = key_step(v_ref, t)
        v_t = v_ref[part, :].T[cols, :]
        for h in range(heads):
            e = jnp.exp(s_ref[h, at, :] - tops[h])
            sums[h] = sums[h] + jnp.sum(e, axis=0, keepdims=True)
            outs[h] = outs[h] + nn(v_t, e.astype(BF16))
    flat = jnp.concatenate([outs[h] / sums[h] for h in range(heads)], axis=0)
    o_ref[...] = flat.T.astype(BF16)
    lse_ref[...] = jnp.concatenate([tops[h] + jnp.log(sums[h]) for h in range(heads)], axis=0)
    weights_there()
    halves_out(nt(o_ref[...], w_ref[...]), send_ref, mine_ref)


def ffn_kernel(*refs):
    pieces, w_hbm, refs = refs[:8], refs[8], refs[9:]
    b_ref, gu_ref, h_ref, send_ref, mine_ref, gu_w, down_w, b_sems, gu_sems, sem = refs
    rows_there = fetch(pieces, b_ref, b_sems)
    steps, n, c = 4, w_hbm.shape[0] // 4, gu_w.shape[1]

    def load(i):
        at = pl.ds(i * n, n)
        return pltpu.make_async_copy(w_hbm.at[at, pl.ds(0, c)], gu_w.at[at, :], gu_sems.at[i])

    for i in range(steps):
        load(i).start()
    down = pltpu.make_async_copy(w_hbm.at[:, pl.ds(c, down_w.shape[1])], down_w, sem)
    down.start()
    rows_there()
    for i in range(steps):
        load(i).wait()
        at = slice(i * n, (i + 1) * n)
        part = nn(b_ref[:, at], gu_w[at, :])
        gu_ref[...] = part if i == 0 else gu_ref[...] + part
    units = gu_ref.shape[1] // 2
    gate, up = gu_ref[:, :units], gu_ref[:, units:]
    h_ref[:, :units] = (gate / (1.0 + jnp.exp(-gate)) * up).astype(BF16)
    spare = h_ref.shape[1] - units
    h_ref[:, units:] = jnp.zeros((h_ref.shape[0], spare), BF16)
    down.wait()
    halves_out(nt(h_ref[...], down_w[...]), send_ref, mine_ref)


def ffn_back_kernel(*refs):
    pieces, w_hbm, act_hbm, refs = refs[:8], refs[8], refs[9], refs[10:]
    dff_ref, dgu_ref, send_ref, mine_ref, gu_w, down_w, gu_ref, r_sems, gu_sems = refs
    rows_there = fetch(pieces, dff_ref, r_sems)
    c = gu_w.shape[1]
    down = pltpu.make_async_copy(w_hbm.at[:, pl.ds(c, down_w.shape[1])], down_w, gu_sems.at[2])
    down.start()
    act = pltpu.make_async_copy(act_hbm, gu_ref, gu_sems.at[0])
    act.start()
    load = pltpu.make_async_copy(w_hbm.at[:, pl.ds(0, c)], gu_w, gu_sems.at[1])
    load.start()
    rows_there()
    down.wait()
    units = gu_ref.shape[1] // 2
    dh = nn(dff_ref[...], down_w[...])[:, :units]
    act.wait()
    gate, up = gu_ref[:, :units], gu_ref[:, units:]
    sig = 1.0 / (1.0 + jnp.exp(-gate))
    dgate = dh * up * (sig * (1.0 + gate * (1.0 - sig)))
    dgu_ref[...] = jnp.concatenate([dgate, dh * (gate * sig)], axis=1).astype(BF16)
    load.wait()
    halves_out(nt(dgu_ref[...], gu_w[...]), send_ref, mine_ref)


def attend_back_kernel(place, *refs, parts):
    pieces, packs, refs = refs[:8], refs[8 : 8 + parts], refs[8 + parts :]
    q_ref, k_ref, v_ref, bias_ref, o_ref, lse_ref, cos_ref, sin_ref, *refs = refs
    dattn_ref, dq_ref, own_ref, send_ref, w_ref, do_ref, dk_ref, dv_ref, sems, r_sems = refs
    rows_there = fetch(pieces, dattn_ref, r_sems)
    weights_there = fetch_blocks(packs, place, packs[0].shape[1] - w_ref.shape[1], w_ref, sems)
    rows, width = q_ref.shape
    heads = width // HD
    steps = 2 * k_ref.shape[0] // KEYS_STEP
    rows_there()
    weights_there()
    do = nn(dattn_ref[...], w_ref[...])
    do_ref[...] = do.astype(BF16)
    both = (do_ref[...].astype(F32) * o_ref[...].astype(F32)).T
    deltas = [
        jnp.sum(both[h * HD : (h + 1) * HD, :], axis=0, keepdims=True) for h in range(heads)
    ]
    dq_t = [jnp.zeros((HD, rows), F32) for _ in range(heads)]
    for t in range(steps):
        at = pl.ds(t * KEYS_STEP, KEYS_STEP)
        part, cols = key_step(k_ref, t)
        k = k_ref[part, cols]
        v = v_ref[part, cols]
        k_t = k_ref[part, :].T[cols, :]
        bias = bias_ref[at, :]
        dk = jnp.zeros((KEYS_STEP, HD), F32)
        dv = jnp.zeros((KEYS_STEP, HD), F32)
        for h in range(heads):
            q_h = q_ref[:, h * HD : (h + 1) * HD]
            do_h = do_ref[:, h * HD : (h + 1) * HD]
            p = jnp.exp(nt(k, q_h) + bias - lse_ref[h : h + 1, :])
            ds = (p * (nt(v, do_h) - deltas[h])).astype(BF16)
            dv = dv + nn(p.astype(BF16), do_h)
            dk = dk + nn(ds, q_h)
            dq_t[h] = dq_t[h] + nn(k_t, ds)
        dk_ref[part, cols] = dk
        dv_ref[part, cols] = dv
    dq = jnp.concatenate(dq_t, axis=0).T * HD**-0.5
    dq_ref[...] = rope_back(dq, cos_ref[:, :width], sin_ref[:, :width]).astype(BF16)
    odd = place[CORE] == 1
    own_ref[...] = jnp.where(odd, dv_ref[...], dk_ref[...])
    send_ref[...] = jnp.where(odd, dk_ref[...], dv_ref[...]).astype(BF16)


def kv_add_kernel(own_ref, other_ref, out_ref):
    out_ref[...] = (own_ref[...] + other_ref[...].astype(F32)).astype(BF16)


def qkv_back_kernel(place, *refs, parts):
    packs, (x_hbm, dq_ref, kv_ref, cos_ref, sin_ref, *refs) = refs[:parts], refs[parts:]
    dqkv_ref, send_ref, mine_ref, gain_grad_ref, w_ref, x_ref, sems, x_sem = refs
    weights_there = fetch_blocks(packs, place, 0, w_ref, sems)
    rows_there = pltpu.make_async_copy(x_hbm, x_ref, x_sem)
    rows_there.start()
    width, odd = dq_ref.shape[1], place[CORE] == 1
    both = sum((kv_ref[i].astype(F32) for i in range(1, 8)), kv_ref[0].astype(F32))
    first, second = both[:, :HD], both[:, HD:]
    dk = jnp.concatenate([first, second], axis=0)
    dv = jnp.concatenate([second, first], axis=0)
    spare = jnp.zeros_like(dk)
    dkv = jnp.where(
        odd, jnp.concatenate([spare, dv], axis=1), jnp.concatenate([dk, spare], axis=1)
    )
    dkv = rope_back(dkv, cos_ref[:, width:], sin_ref[:, width:])
    dqkv_ref[:, :width] = dq_ref[...]
    dqkv_ref[:, width:] = dkv.astype(BF16)
    weights_there()
    da = nt(dqkv_ref[...], w_ref[...])
    halves_out(da, send_ref, mine_ref)
    rows_there.wait()
    x = x_ref[...].astype(F32)
    gain_grad_ref[...] = jnp.sum(da * (x * rms(x)), axis=0, keepdims=True)


def ffn_product_kernel(b_ref, dgu_ref, dff_ref, h_ref, out, whole, sems):
    n, steps = dgu_ref.shape[1], sems.shape[0]
    rows = whole.shape[0] // steps
    copies = []
    for i in range(steps):
        at = slice(i * rows, (i + 1) * rows)
        whole[at, :n] = tn(b_ref[:, at], dgu_ref[...]).astype(BF16)
        whole[at, n:] = tn(dff_ref[:, at], h_ref[...]).astype(BF16)
        here = pl.ds(i * rows, rows)
        copies.append(pltpu.make_async_copy(whole.at[here, :], out.at[here, :], sems.at[i]))
        copies[-1].start()
    for c in copies:
        c.wait()


def ffn_products(b, dgu, dff, hidden):
    dims = (b.shape[1], dgu.shape[1] + hidden.shape[1])
    return call(
        ffn_product_kernel,
        [pltpu.HBM(dims, BF16)],
        [(b, dgu, dff, hidden)],
        [pltpu.VMEM(dims, BF16), DMA((8,))],
        room=14,
        moved=20_000_000,
        out_spec=HBM,
    )[0]


def attn_product_kernel(dattn, a, gg_a, gg_f, ctx, dqkv, *refs, layer):
    *_, out, whole, sems = refs
    cols = pl.ds(layer * whole.shape[1], whole.shape[1])
    m, steps = ctx.shape[1], sems.shape[0]
    wide = m + dqkv.shape[1]
    rows = whole.shape[0] // steps
    row = lax.broadcasted_iota(jnp.int32, (whole.shape[1] - wide, rows), 0)
    copies = []
    for i in range(steps):
        at = slice(i * rows, (i + 1) * rows)
        whole[at, :m] = tn(dattn[:, at], ctx[...]).astype(BF16)
        whole[at, m:wide] = tn(a[:, at], dqkv[...]).astype(BF16)
        ga, gf = (jnp.broadcast_to(g[:, at], row.shape) for g in (gg_a, gg_f))
        gains = jnp.where(row == 0, ga, jnp.where(row == 1, gf, 0.0))
        whole[at, wide:] = gains.T.astype(BF16)
        here = pl.ds(i * rows, rows)
        copies.append(pltpu.make_async_copy(whole.at[here, :], out.at[here, cols], sems.at[i]))
        copies[-1].start()
    for c in copies:
        c.wait()


def attn_products(dattn, ctx, a, dqkv, gg_a, gg_f, layer, filled=None):
    d, wide = a.shape[1], ctx.shape[1] + dqkv.shape[1] + 128
    args = [(dattn, a, gg_a, gg_f, ctx, dqkv)]
    return call(
        functools.partial(attn_product_kernel, layer=layer),
        [pltpu.HBM((d, 2 * wide), BF16)],
        args if filled is None else args + [[filled]],
        [pltpu.VMEM((d, wide), BF16), DMA((4,))],
        room=14,
        out_spec=HBM,
        moved=12_000_000,
        aliases=None if filled is None else {6: 0},
    )[0]


def y_split_both_kernel(place, r_ref, keep_ref, near_ref, far_ref, straight_ref):
    n, c = keep_ref.shape
    here = pl.ds(pl.multiple_of(place[YLO] * n, n), n)
    there = pl.ds(pl.multiple_of((1 - place[YLO]) * n, n), n)

    def fill(mine, other):
        keep_ref[...] = r_ref[here, mine]
        near_ref[...] = r_ref[there, mine]
        straight_ref[...] = r_ref[here, other]
        far_ref[...] = r_ref[there, other]

    @pl.when(place[SECTION] == 0)
    def _():
        fill(slice(0, c), slice(c, 2 * c))

    @pl.when(place[SECTION] == 1)
    def _():
        fill(slice(c, 2 * c), slice(0, c))


def reduce_y_both(r, place):
    dims = (r.shape[0] // 2, r.shape[1] // 2)
    keep, near, far, straight = call(
        y_split_both_kernel, [held(dims)] * 4, [place, (r,)], room=16
    )
    return [keep, swap_ylo(near), swap_across(far), swap_section(straight)]


def y_split_kernel(place, r0_ref, r1_ref, keep_ref, near_ref, far_ref, straight_ref):
    n = keep_ref.shape[0]
    here = pl.ds(pl.multiple_of(place[YLO] * n, n), n)
    there = pl.ds(pl.multiple_of((1 - place[YLO]) * n, n), n)

    def fill(mine, other):
        keep_ref[...] = mine[here, :]
        near_ref[...] = mine[there, :]
        straight_ref[...] = other[here, :]
        far_ref[...] = other[there, :]

    @pl.when(place[SECTION] == 0)
    def _():
        fill(r0_ref, r1_ref)

    @pl.when(place[SECTION] == 1)
    def _():
        fill(r1_ref, r0_ref)


def by_core_kernel(place, *refs):
    *parts, own_ref, send_ref = refs
    n = own_ref.shape[0]
    here = pl.ds(pl.multiple_of(place[CORE] * n, n), n)
    there = pl.ds(pl.multiple_of((1 - place[CORE]) * n, n), n)
    own_ref[...] = sum(p[here, :].astype(F32) for p in parts)
    send_ref[...] = sum(p[there, :].astype(F32) for p in parts).astype(BF16)


def by_core(parts, place):
    n, c = parts[0].shape[0] // 2, parts[0].shape[1]
    own, send = call(
        by_core_kernel, [held((n, c), F32), shape((n, c))], [place, tuple(parts)], room=16
    )
    return own, swap_core(send)


def reduce_y(r0, r1, place):
    n, c = r0.shape[0] // 2, r0.shape[1]
    keep, near, far, straight = call(y_split_kernel, [held((n, c))] * 4, [place, (r0, r1)], room=16)
    return [keep, swap_ylo(near), swap_across(far), swap_section(straight)]


def ordered(odd, own, other):
    other = other.astype(F32)
    return jnp.concatenate(
        [jnp.where(odd, other, own), jnp.where(odd, own, other)], axis=1
    )


def attn_grads_kernel(place, own_ref, other_ref, o_ref, q_ref, k_ref, v_ref, *gain_refs):
    odd = place[CORE] == 1
    m = n = q_ref.shape[1] // 2
    own, other = own_ref[:, :m].T, other_ref[:, :m].astype(F32).T
    o_ref[:m, :] = jnp.where(odd, other, own)
    o_ref[m:, :] = jnp.where(odd, own, other)
    q_ref[...] = ordered(odd, own_ref[:, m : m + n], other_ref[:, m : m + n])
    both = own_ref[:, m + n :] + other_ref[:, m + n :].astype(F32)
    kv = both[:, : 2 * HD].T
    k_ref[...] = kv[:HD, :]
    v_ref[...] = kv[HD:, :]
    rows = gain_refs[0].shape[0]
    gain_refs[-1][...] = both[:, 2 * HD :]
    for k, ref in enumerate(gain_refs[:-1]):
        at = lax.rem(place[TP] + k, 4) * rows
        ref[...] = gain_refs[-1][pl.ds(pl.multiple_of(at, rows), rows), :]


def ffn_grads_kernel(place, own_ref, other_ref, gate_ref, up_ref, down_ref):
    odd = place[CORE] == 1
    n = gate_ref.shape[1] // 2
    gate_ref[...] = ordered(odd, own_ref[:, :n], other_ref[:, :n])
    up_ref[...] = ordered(odd, own_ref[:, n : 2 * n], other_ref[:, n : 2 * n])
    own, other = own_ref[:, 2 * n :].T[:n], other_ref[:, 2 * n :].astype(F32).T[:n]
    down_ref[:n, :] = jnp.where(odd, other, own)
    down_ref[n:, :] = jnp.where(odd, own, other)


def body(
    block_input,
    out_grad,
    seg_ids,
    attn_gain,
    w_query,
    w_key,
    w_value,
    w_out,
    ffn_gain,
    w_gate,
    w_up,
    w_down,
):
    at = {name: lax.axis_index(name) for name in AXES}
    section, core, tp = at["section"], at["core"], at["tp"]
    place = jnp.stack([at[name] for name in AXES]).astype(jnp.int32)
    d = block_input.shape[2]
    micro_rows = block_input.shape[1]
    group = 8 * micro_rows
    q_width = w_query.shape[2] // 2
    units = w_gate.shape[2] // 2
    own_rows = w_query.shape[1]

    padded = units + (-units) % 128
    attn_dims = (own_rows + GAIN_ROWS, 2 * q_width + 2 * HD)
    attn_own, attn_send = call(
        pack_attn_kernel,
        [shape(attn_dims)] * 2,
        [place, (w_query[0], w_key[0].T, w_value[0].T, w_out[0], attn_gain, ffn_gain)],
    )
    attn_shard = call(
        chip_attn_kernel,
        [held((2 * own_rows + GAIN_ROWS, attn_dims[1]))],
        [place, (attn_own, swap_core(attn_send))],
    )[0]
    ffn_own, ffn_send = call(
        pack_ffn_kernel,
        [shape((own_rows, 2 * units + padded))] * 2,
        [place, (w_down[0], w_gate[0], w_up[0])],
        room=16,
    )
    ffn_shard = chip_rows(place, ffn_own, swap_core(ffn_send))
    attn_y = y_exchange(after(attn_shard, ffn_shard))
    attn_pairs = pairs(place, attn_shard, attn_y)
    attn0 = [attn_pairs[0]] + [from_x(attn_pairs[0], k) for k in (1, 2, 3)]
    attn1 = [gather_x(attn_pairs[1])]
    ffn_y = y_exchange_on(after(ffn_shard, *attn_y))

    block = at["x"] * 2 + at["ylo"]
    seg_row = lax.dynamic_index_in_dim(seg_ids, section, 0, keepdims=False)
    def arranged(row):
        v = row.reshape(8, 2, 4, micro_rows)
        return lax.dynamic_slice_in_dim(jnp.concatenate([v, v], axis=2), tp, 4, 2)

    def keys_of(row):
        return arranged(row).transpose(1, 0, 2, 3).reshape(-1)

    def queries_of(row):
        v = lax.dynamic_index_in_dim(arranged(row), block, 0, keepdims=False)
        return jnp.where(core == 0, v, v[::-1]).reshape(-1)

    places = jnp.arange(seg_row.shape[0], dtype=jnp.int32)
    k_pos, k_seg = keys_of(places), keys_of(seg_row)
    q_pos, q_seg = queries_of(places), queries_of(seg_row)
    seen = (k_pos[:, None] <= q_pos[None, :]) & (k_seg[:, None] == q_seg[None, :])
    bias = jnp.where(seen, 0.0, MASKED).astype(F32)

    frequency = 10000.0 ** (-jnp.arange(0, HD, 2, dtype=F32) / HD)
    angles = q_pos.astype(F32)[:, None] * frequency[None, :]
    wide = q_width + 2 * HD
    plain = lax.broadcasted_iota(jnp.int32, (group, wide), 1) >= q_width + HD
    cos, sin = (jnp.concatenate([t] * 12, axis=1) for t in (jnp.cos(angles), jnp.sin(angles)))
    cos, sin = jnp.where(plain, 1.0, cos), jnp.where(plain, 0.0, sin)

    rows_low = shape((micro_rows, d))
    rows_f32 = shape((micro_rows, d), F32)
    mid_outs = [rows_f32, rows_low]
    partials = [shape((group // 2, d)), shape((group // 2, d), F32)]
    heads, keys = q_width // HD, seg_row.shape[0]
    gain_row = shape((1, d), F32)

    def project(x, packs):
        return call(
            functools.partial(qkv_kernel, parts=len(packs)),
            [held((group, d))] * 2
            + [shape((group, q_width)), shape((group // 2, 2 * HD))]
            + [gain_row, gain_row],
            [place, gather_rows(x) + packs, cos, sin],
            [
                pltpu.VMEM((d, wide), BF16),
                pltpu.VMEM((8, GAIN_ROWS, d // 8), BF16),
                DMA((8,)),
                DMA((8,)),
                DMA((8,)),
            ],
            room=18,
        )

    both_kv = held((keys // 2, 2 * HD))

    def attention(q, kv, packs):
        return call(
            functools.partial(attend_kernel, parts=len(packs)),
            [held((group, q_width)), held((heads, group), F32), both_kv, both_kv, *partials],
            [place, q, *kv, bias, packs],
            [
                pltpu.VMEM((heads, keys, group), F32),
                pltpu.VMEM((d, q_width), BF16),
                DMA((8,)),
            ],
            room=12,
        )

    def feed_forward(b, w_ffn):
        return call(
            ffn_kernel,
            [held((group, d)), held((group, 2 * units), F32), held((group, padded)), *partials],
            [[*gather_rows(b), w_ffn]],
            [
                pltpu.VMEM((d, 2 * units), BF16),
                pltpu.VMEM((d, padded), BF16),
                DMA((8,)),
                DMA((4,)),
                DMA,
            ],
            room=16,
        )

    def backward(dy, kept, layer, filled=None, pending=()):
        x, rows, a, q, k, v, ctx, lse, mid, b, gu, hidden, gain_a, gain_f, w_ffn, packs = kept
        dff, dgu, send, mine = call(
            ffn_back_kernel,
            [held((group, d)), held((group, 2 * units)), *partials],
            [[*gather_rows(dy), w_ffn, gu]],
            [
                pltpu.VMEM((d, 2 * units), BF16),
                pltpu.VMEM((d, padded), BF16),
                pltpu.VMEM((group, 2 * units), F32),
                DMA((8,)),
                DMA((3,)),
            ],
            room=16,
        )
        g_ffn = ffn_products(b, dgu, dff, hidden)
        dmid, dattn, gg_f = call(
            norm_back_kernel,
            [rows_f32, rows_low, held((1, d), F32)],
            [*reduce_rows(send, mine), dy, mid, gain_f],
        )
        dattn = after(dattn, g_ffn, *pending)
        dattn, dq, dkv, dkv_send = call(
            functools.partial(attend_back_kernel, parts=len(packs)),
            [
                held((group, d)),
                shape((group, q_width)),
                shape((keys // 2, 2 * HD), F32),
                shape((keys // 2, 2 * HD)),
            ],
            [place, gather_rows(dattn) + packs, (q, k, v), bias, (ctx, lse), cos, sin],
            [
                pltpu.VMEM((d, q_width), BF16),
                pltpu.VMEM((group, q_width), BF16),
                pltpu.VMEM((keys // 2, 2 * HD), F32),
                pltpu.VMEM((keys // 2, 2 * HD), F32),
                DMA((8,)),
                DMA((8,)),
            ],
            room=18,
        )
        dkv = call(kv_add_kernel, [shape(dkv.shape)], [dkv, swap_core(dkv_send)])[0]
        arrived = lax.all_to_all(
            dkv.reshape(8, group // 2, 2 * HD), ("x", "ylo"), 0, 0, tiled=True
        )
        dqkv, send, mine, gg_a = call(
            functools.partial(qkv_back_kernel, parts=len(packs)),
            [held((group, wide)), *partials, held((1, d), F32)],
            [place, packs + [rows], dq, arrived, cos, sin],
            [pltpu.VMEM((d, wide), BF16), pltpu.VMEM((group, d), BF16), DMA((8,)), DMA],
            room=16,
        )
        g_attn = attn_products(dattn, ctx, a, dqkv, gg_a, gg_f, layer, filled)
        dx, dx_low, _ = call(
            norm_back_kernel,
            [rows_f32, rows_low, held((1, d), F32)],
            [*reduce_rows(send, mine), dmid, x, gain_a],
        )
        return dx, dx_low, g_attn, g_ffn, dqkv

    x0 = lax.dynamic_index_in_dim(block_input, section, 0, keepdims=False)
    dy1 = lax.dynamic_index_in_dim(out_grad, section, 0, keepdims=False)

    rows0, a0, q0, kv0, ga0, gf0 = project(x0, attn0)
    ffn_pairs = pairs(place, ffn_shard, ffn_y)
    w_ffn0 = gather_x(after(ffn_pairs[0], *attn0[1:], *attn1))
    kv0 = gather_kv(kv0)
    ctx0, lse0, k0, v0, send, mine = attention(q0, kv0, attn0)
    mid0, b = call(add_norm_kernel, mid_outs, [*reduce_rows(send, mine), x0, gf0])
    w_ffn1 = gather_x(after(ffn_pairs[1], b))
    b0, up0, hidden0, send, mine = feed_forward(b, w_ffn0)
    y0 = call(add_kernel, [rows_low], [*reduce_rows(send, mine), mid0])[0]
    kept0 = (x0, rows0, a0, q0, k0, v0, ctx0, lse0, mid0, b0, up0, hidden0, ga0, gf0, w_ffn0, attn0)
    rows1, a1, q1, kv1, ga1, gf1 = project(y0, attn1)
    ctx1, lse1, k1, v1, send, mine = attention(q1, gather_kv(kv1), attn1)
    mid1, b = call(add_norm_kernel, mid_outs, [*reduce_rows(send, mine), y0, gf1])
    b1, up1, hidden1, send, mine = feed_forward(b, w_ffn1)
    last = (send, mine, mid1)
    kept1 = (y0, rows1, a1, q1, k1, v1, ctx1, lse1, mid1, b1, up1, hidden1, ga1, gf1, w_ffn1, attn1)

    early = section == 0

    def both_micros(layer0, layer1, dtype):
        mine = jnp.where(early, layer0, layer1).astype(dtype)
        other = jnp.where(early, layer1, layer0).astype(BF16)
        other = swap_section(other).astype(dtype)
        return jnp.stack([jnp.where(early, mine, other), jnp.where(early, other, mine)])[None]

    dx1, dx1_low, g_attn1, g_ffn1, _ = backward(dy1, kept1, 1)
    ffn1 = reduce_x(g_ffn1)
    dx0, dx0_low, g_attn, g_ffn0, dqkv0 = backward(dx1_low, kept0, 0, g_attn1, [ffn1])
    send, mine, mid1 = last
    y1 = call(add_kernel, [rows_low], [*reduce_rows(after(send, dqkv0), mine), mid1])[0]
    block_output = both_micros(y0, y1, BF16)
    input_grad = both_micros(dx0, dx1, F32)
    ffn_y = reduce_y(after(reduce_x(g_ffn0), input_grad, block_output), ffn1, place)

    attn_y = reduce_y_both(reduce_x(g_attn), place)
    ffn_parts = by_core([after(ffn_y[0], attn_y[0]), *ffn_y[1:]], place)

    def finish(kernel, dims, parts):
        return call(kernel, [held(s, F32) for s in dims], [place, parts], room=20)

    own = own_rows
    grad_gate, grad_up, grad_down = finish(
        ffn_grads_kernel, [(own, 2 * units)] * 2 + [(2 * units, own)], ffn_parts
    )
    attn_parts = by_core(attn_y, place)
    grad_out, grad_query, grad_key, grad_value, *gain_pieces, _ = finish(
        attn_grads_kernel,
        [(2 * q_width, own), (own, 2 * q_width), (HD, own), (HD, own)]
        + [(micro_rows, 128)] * 4
        + [(own, 128)],
        attn_parts,
    )
    gain_sums = gain_pieces[0]
    for k in (1, 2, 3):
        gain_sums = gain_sums + from_z(gain_pieces[k], -k)
    gain_sums = gain_sums[:, :2].T


    return (
        block_output,
        input_grad,
        gain_sums[0][None],
        grad_query[None],
        grad_key.T[None],
        grad_value.T[None],
        grad_out[None],
        gain_sums[1][None],
        grad_gate[None],
        grad_up[None],
        grad_down[None],
    )


def solution(mesh):
    fine = Mesh(mesh.devices.reshape(2, 4, 2, 2, 4), AXES)
    wide = ("x", "ylo", "core")
    rows = P(None, (*wide, "tp"), None)
    into = P("section", wide, "tp")
    out_of = P("section", "tp", wide)
    grown = P("section", None, (*wide, "tp"), None)
    gain_grad = P("section", (*wide, "tp"))
    return jax.shard_map(
        body,
        mesh=fine,
        in_specs=(
            rows, rows, P(), P("section", wide), into, into, into, out_of,
            P("section", wide), into, into, out_of,
        ),
        out_specs=(
            grown, grown, gain_grad, into, into, into, out_of, gain_grad, into, into, out_of,
        ),
        check_vma=False,
    )
```
